32 devices in a mesh: expert: 8 (over z, x), cuts: 4 (over y, core).
Axes of the slice: x: 2, y: 2, z: 4, core: 2. Of those that a mesh axis runs over, the one named last changes fastest.
Arguments:
- tokens: bfloat16 [8192, 768], P(('expert', 'cuts')), may hold values from -6 to 6
- cotangent: bfloat16 [8192, 768], P(('expert', 'cuts')), may hold values from -6 to 6
- expert_ids: int32 [8192, 2], P(('expert', 'cuts')), may hold values from 0 to 7, all different within a row; in each aligned block of 256 rows (0 to 255, 256 to 511, ...) at most 128 rows name the same one
- gate_units: int32 [8192, 2], P(('expert', 'cuts')), may hold values from 1024 to 4095
- capacity: int32 [8], replicated, may hold values from 64 to 128, as said below
- frozen: int32 [8], P('expert'), may hold values from 0 to 1, as said below
- attn_copy: bfloat16 [4, 768, 768], replicated
- attn_master: float32 [4, 768, 768], P('cuts'), may hold values from -0.21875 to 0.21875
- attn_momentum: float32 [4, 768, 768], P('cuts'), may hold values from -160 to 160
- norm_params: float32 [4, 768], replicated
- norm_first: float32 [4, 768], replicated, may hold values from -56 to 56
- norm_second: float32 [4, 768], replicated, may hold values from 8.192 to 32.768
- up_copy: bfloat16 [8, 768, 3072], P('expert', None, 'cuts'), may hold values from -0.21875 to 0.21875
- up_master: float32 [8, 768, 3072], P('expert', None, 'cuts'), may hold values from -0.21875 to 0.21875
- up_momentum: float32 [8, 768, 3072], P('expert', None, 'cuts'), may hold values from -80 to 80
- down_copy: bfloat16 [8, 3072, 768], P('expert', 'cuts'), may hold values from -0.21875 to 0.21875
- down_master: float32 [8, 3072, 768], P('expert', 'cuts'), may hold values from -0.109375 to 0.109375
- down_momentum: float32 [8, 3072, 768], P('expert', 'cuts'), may hold values from -64 to 64
Outputs:
- output: bfloat16 [8192, 768], P(('expert', 'cuts'))
- input_grad: float32 [8192, 768], P(('expert', 'cuts'))
- attn_new: float32 [4, 768, 768], P('cuts')
- attn_moment: float32 [4, 768, 768], P('cuts')
- attn_low: bfloat16 [4, 768, 768], P('cuts')
- up_new: float32 [8, 768, 3072], P('expert', None, 'cuts')
- up_moment: float32 [8, 768, 3072], P('expert', None, 'cuts')
- up_low: bfloat16 [8, 768, 3072], P('expert', None, 'cuts')
- down_new: float32 [8, 3072, 768], P('expert', 'cuts')
- down_moment: float32 [8, 3072, 768], P('expert', 'cuts')
- down_low: bfloat16 [8, 3072, 768], P('expert', 'cuts')
- norm_new: float32 [4, 768], replicated
- norm_first_new: float32 [4, 768], replicated
- norm_second_new: float32 [4, 768], replicated
The draws below stay inside these ranges and needn't reach their ends.
Inputs may be any that keep to these rules, and one draw needn't show every extreme that they name: `expert_ids`: each row names two different experts; among the 256 rows of one aligned block no expert is named more than 128 times. `capacity`: some expert has exactly 128. `frozen`: exactly 4 entries are 1.
All inputs are finite; a program needn't handle non-finite values.
Results may differ from the reference program's by a relative error of at most 0.02.
Values may be sent and summed in bfloat16 or wider, within the bound.
No kernel may reach another device: no remote copies, remote signals or barrier semaphores. Data moves between devices by JAX's collectives and lax.ppermute only.
A program may use at most 320 MiB of HBM per device.

```python
import math
import jax
import jax.numpy as jnp
import numpy as np
from jax import lax

D = 768
HEADS = 12
HEAD_DIM = 64
FF = 3072
SEQ = 256
ITERS = 5
STEP_COUNT = 10
EXPERTS = 8
TOKENS = 8192
CAP = 128


def draw_capacity(key, part):
    key = jax.random.fold_in(key, 11)
    pick_key, value_key = jax.random.split(key)
    values = jax.random.randint(value_key, (EXPERTS,), CAP // 2, CAP + 1)
    chosen = jax.random.randint(pick_key, (), 0, EXPERTS)
    return jnp.where(jnp.arange(EXPERTS) == chosen, CAP, values).astype(jnp.int32)


def draw_frozen(key, part):
    key = jax.random.fold_in(key, 12)
    order = jax.random.permutation(key, EXPERTS)
    return (order < EXPERTS // 2).astype(jnp.int32)


def draw_norm_params(key, part):
    key = jax.random.fold_in(key, 13)
    gain_key, shift_key = jax.random.split(key)
    gains = jnp.clip(1.0 + 0.15 * jax.random.normal(gain_key, (2, D), jnp.float32), 0.5, 1.5)
    shifts = 0.1 * jax.random.normal(shift_key, (2, D), jnp.float32)
    return jnp.stack([gains[0], shifts[0], gains[1], shifts[1]]).astype(jnp.float32)


def draw_attn_copy(key, part):
    key = jax.random.fold_in(key, 14)
    spread = jnp.array([1.0, 1.0, 1.0, 8.0 ** 0.5], jnp.float32) / D ** 0.5
    base = jax.random.normal(key, (4, D, D), jnp.float32)
    return (base * spread[:, None, None]).astype(jnp.bfloat16)


def touch_ends(drawn, rng, least, largest):
    dims = drawn.shape
    index_at = [jax.random.randint(jax.random.fold_in(rng, axis), (), 0, dims[axis]) for axis in range(len(dims))]
    drawn = drawn.at[tuple(index_at)].set(least)
    longest = dims.index(max(dims))
    index_at[longest] = (index_at[longest] + 1) % dims[longest]
    return drawn.at[tuple(index_at)].set(largest)


def levels(key, dims, cuts, smallest, high):
    level, own = 1.0, jax.random.fold_in(key, 6)
    for axis_at, blocks in cuts:
        draws = jnp.exp(jax.random.uniform(jax.random.fold_in(own, axis_at), (blocks,), jnp.float32, smallest / len(cuts), high / len(cuts)))
        level = level * jnp.repeat(draws, dims[axis_at] // blocks).reshape([-1 if axis == axis_at else 1 for axis in range(len(dims))])
    return level


def deal_out(own_key, own, number, rows, number_of, top, reach, slope):
    order = jax.random.permutation(own_key, number_of)
    packed, ordinary = load_shares(number_of, rows * top, reach, slope, True), load_shares(number_of, rows * top, reach, slope, False)
    places = jnp.arange(number_of)

    def named(lengths, turn):
        used = int((lengths > 0).sum())
        fixed = max(1, used // 4)
        moved = fixed + (places - fixed + turn * (used - fixed)) % max(1, number_of - fixed)
        return jnp.zeros((number_of,), jnp.int32).at[order[jnp.where(places < fixed, places, moved)]].set(jnp.asarray(lengths, jnp.int32))

    lengths = jnp.where(number % 4 == 0, named(packed, number // 4), named(ordinary, number - number // 4 - 1))
    mixed = jax.random.permutation(jax.random.fold_in(own, 3), number_of)
    source_of, receiver = mixed[0:number_of // 2 * 2:2], mixed[1:number_of // 2 * 2:2]
    room = jnp.minimum(lengths[source_of] - 1, reach - lengths[receiver]) // 2
    room = jnp.where((source_of == order[0]) | (receiver == order[0]) | (lengths[receiver] == 0), 0, jnp.maximum(room, 0))
    moved = jax.random.randint(jax.random.fold_in(own, 4), (number_of // 2,), 0, 1 << 20) % (room + 1)
    lengths = lengths.at[source_of].add(-moved).at[receiver].add(moved)
    labels = jnp.searchsorted(jnp.cumsum(lengths), jnp.arange(rows * top), side="right").astype(jnp.int32)
    table = labels.reshape(top, rows).T
    table = table[jax.random.permutation(jax.random.fold_in(own, 1), rows)]
    turn = jax.random.randint(jax.random.fold_in(own, 2), (rows, 1), 0, top)
    return jnp.take_along_axis(table, (jnp.arange(top)[None, :] + turn) % top, axis=1)


def load_shares(count, total, reach, lean, full):
    loads = [(1 << 20) // math.isqrt(grade ** lean) + 1 for grade in range(1, count + 1)]
    largest = reach if full else min(reach, max(-(-total // count), total * loads[0] // sum(loads)))
    least = 1 if total - largest >= count - 1 else 0
    given, spare = [largest] + [least] * (count - 1), total - largest - least * (count - 1)
    while spare > 0:
        free = [i for i in range(1, count) if given[i] < largest] or [i for i in range(1, count) if given[i] < reach]
        mass, remaining = sum([loads[i] for i in free]), spare
        for i in free:
            more = min(reach - given[i], max(1, remaining * loads[i] // mass), spare)
            given[i] = given[i] + more
            spare = spare - more
    return np.array(given)


def centred(stream_key, extent, scale, bound, cuts=(), kind=jnp.bfloat16):
    level = levels(stream_key, extent, cuts, -0.22, 0.18) if cuts else 1.0
    drawn = jax.random.normal(stream_key, extent, jnp.float32) * scale * level
    return jnp.minimum(jnp.maximum(drawn, -bound), bound).astype(kind)


def setup_inputs(seed: int = 0) -> dict:
    arg_keys = jax.random.split(jax.random.key(seed), 19)
    tokens = centred(arg_keys[0], (TOKENS, D), 1.0, 6.0, ((0, 32),))
    cotangent = centred(arg_keys[1], (TOKENS, D), 1.0, 6.0, ((0, 32),))
    expert_ids_keys = jax.random.split(jax.random.fold_in(arg_keys[2], 1), TOKENS // SEQ)
    expert_ids_turns = jax.random.permutation(jax.random.fold_in(arg_keys[2], 3), TOKENS // SEQ)
    expert_ids = jax.vmap(lambda own, number: deal_out(jax.random.fold_in(arg_keys[2], 2), own, number, SEQ, EXPERTS, 2, CAP, 2))(expert_ids_keys, expert_ids_turns).reshape((TOKENS, 2))
    gate_units = touch_ends(jax.random.randint(arg_keys[3], (TOKENS, 2), 1024, 4096), jax.random.fold_in(arg_keys[3], 1), 1024, 4095).astype(jnp.int32)
    capacity = draw_capacity(jax.random.fold_in(arg_keys[18], 71), 0)
    frozen = draw_frozen(jax.random.fold_in(arg_keys[18], 71), 0)
    attn_copy = draw_attn_copy(jax.random.fold_in(arg_keys[18], 71), 0)
    attn_master = centred(arg_keys[7], (4, D, D), D ** -0.5, 0.21875, ((0, 4),), jnp.float32)
    attn_momentum = centred(arg_keys[8], (4, D, D), (0.3 * TOKENS ** 0.5), 160.0, ((0, 4),), jnp.float32)
    norm_params = draw_norm_params(jax.random.fold_in(arg_keys[18], 71), 0)
    norm_first = centred(arg_keys[10], (4, D), (0.1 * TOKENS ** 0.5), 56.0, (), jnp.float32)
    norm_second = jnp.clip(jnp.exp(jax.random.uniform(arg_keys[11], (4, D), jnp.float32, math.log(8.192), math.log(32.768))), 8.192, 32.768)
    up_copy = centred(arg_keys[12], (EXPERTS, D, FF), D ** -0.5, 0.21875, ((0, 8), (2, 4)))
    up_master = centred(arg_keys[13], (EXPERTS, D, FF), D ** -0.5, 0.21875, ((0, 8), (2, 4)), jnp.float32)
    up_momentum = centred(arg_keys[14], (EXPERTS, D, FF), (0.3 * (2 * TOKENS // EXPERTS) ** 0.5), 80.0, ((0, 8), (2, 4)), jnp.float32)
    down_copy = centred(arg_keys[15], (EXPERTS, FF, D), (FF // 4) ** -0.5, 0.21875, ((0, 8), (1, 4)))
    down_master = centred(arg_keys[16], (EXPERTS, FF, D), FF ** -0.5, 0.109375, ((0, 8), (1, 4)), jnp.float32)
    down_momentum = centred(arg_keys[17], (EXPERTS, FF, D), (0.25 * (2 * TOKENS // EXPERTS) ** 0.5), 64.0, ((0, 8), (1, 4)), jnp.float32)
    return {"tokens": tokens, "cotangent": cotangent, "expert_ids": expert_ids, "gate_units": gate_units, "capacity": capacity, "frozen": frozen, "attn_copy": attn_copy, "attn_master": attn_master, "attn_momentum": attn_momentum, "norm_params": norm_params, "norm_first": norm_first, "norm_second": norm_second, "up_copy": up_copy, "up_master": up_master, "up_momentum": up_momentum, "down_copy": down_copy, "down_master": down_master, "down_momentum": down_momentum}


@jax.custom_vjp
def low(v):
    return lax.optimization_barrier(v.astype(jnp.bfloat16)).astype(jnp.float32)

@jax.custom_vjp
def low_back(v):
    return v

def low_keep(v):
    return (low(v), None)

def low_pass(kept, grad):
    return (grad,)

def back_keep(v):
    return (v, None)

def back_low(kept, grad):
    return (low(grad),)
low.defvjp(low_keep, low_pass)
low_back.defvjp(back_keep, back_low)
FULL_PRECISION = lax.Precision.HIGHEST
NORM_EPSILON = 1e-05
SCHULZ_LINEAR = 3.4445
SCHULZ_SQUARE = -4.775
SCHULZ_QUARTIC = 2.0315
MUON_RATE = 0.2
MUON_DECAY = 0.01
MOMENT_KEEP = 0.5
ADAM_RATE = 0.5
FIRST_DECAY = 0.9
SECOND_DECAY = 0.999
ADAM_EPSILON = 1e-08
ADAM_DECAY = 0.01
GATE_UNIT = 4096.0

def layer_norm(values, gain, shift):
    centre = values - lax.optimization_barrier(jnp.mean(values, axis=-1, keepdims=True))
    spread = lax.optimization_barrier(jnp.mean(centre * centre, axis=-1, keepdims=True))
    return centre * lax.rsqrt(spread + NORM_EPSILON) * gain + shift

def attend(inputs):
    query_rows, key_rows, value_rows = [member.reshape(SEQ, HEADS, HEAD_DIM) for member in inputs]
    scores = low_back(jnp.einsum('qhd,khd->hqk', query_rows, key_rows, precision=FULL_PRECISION) * HEAD_DIM ** (-0.5))
    positions = jnp.arange(SEQ)
    allowed = positions[None, :] <= positions[:, None]
    scores = jnp.where(allowed[None], scores, -1e+30)
    attn_prob = low(jax.nn.softmax(scores, axis=-1))
    mixed_heads = jnp.einsum('hqk,khd->qhd', attn_prob, value_rows, precision=FULL_PRECISION)
    return mixed_heads.reshape(SEQ, D)

def route_tables(expert_ids, gate_units, capacity):
    block_count = TOKENS // SEQ
    flat_ids = expert_ids.reshape(block_count, 2 * SEQ)
    one_hot = (flat_ids[:, :, None] == jnp.arange(EXPERTS, dtype=jnp.int32)[None, None, :]).astype(jnp.int32)
    placed = lax.optimization_barrier(jnp.sum((jnp.cumsum(one_hot, axis=1) - 1) * one_hot, axis=-1))
    limit = lax.optimization_barrier(jnp.sum(one_hot * capacity[None, None, :], axis=-1))
    kept = placed < limit
    slot_index = jnp.where(kept, flat_ids * CAP + placed, EXPERTS * CAP).astype(jnp.int32)
    token_index = (jnp.arange(block_count, dtype=jnp.int32)[:, None] * SEQ + jnp.arange(2 * SEQ, dtype=jnp.int32)[None, :] // 2).astype(jnp.int32)
    gate_value = gate_units.reshape(block_count, 2 * SEQ).astype(jnp.float32) / GATE_UNIT
    block_index = jnp.broadcast_to(jnp.arange(block_count, dtype=jnp.int32)[:, None], slot_index.shape)
    slot_token = jnp.full((block_count, EXPERTS * CAP + 1), -1, jnp.int32).at[block_index, slot_index].set(token_index)[:, :-1]
    slot_gate = jnp.zeros((block_count, EXPERTS * CAP + 1), jnp.float32).at[block_index, slot_index].set(gate_value)[:, :-1]
    slot_token = slot_token.reshape(block_count, EXPERTS, CAP).transpose(1, 0, 2).reshape(EXPERTS, block_count * CAP)
    slot_gate = slot_gate.reshape(block_count, EXPERTS, CAP).transpose(1, 0, 2).reshape(EXPERTS, block_count * CAP)
    return (slot_token, slot_gate)

def forward(inputs_f, attn_weights, norm_values, in_weights, out_weights, slot_token, slot_gate):
    normed_one = low(layer_norm(inputs_f, norm_values[0], norm_values[1]))
    projected = [low_back(low(jnp.dot(normed_one, attn_weights[which_one], precision=FULL_PRECISION))) for which_one in range(3)]
    block_count = TOKENS // SEQ
    attended = lax.map(jax.checkpoint(attend), tuple((member.reshape(block_count, SEQ, D) for member in projected)))
    attended = low_back(low(attended.reshape(TOKENS, D)))
    residual = inputs_f + low_back(jnp.dot(attended, attn_weights[3], precision=FULL_PRECISION))
    normed_two = low(layer_norm(residual, norm_values[2], norm_values[3]))

    def expert_step(totals, inputs):
        weight_in, weight_out, token_rows, gate_rows = inputs
        filled = (token_rows >= 0).astype(jnp.float32)
        safe_rows = jnp.maximum(token_rows, 0)
        slot_rows = low_back(jnp.take(normed_two, safe_rows, axis=0) * filled[:, None])
        hidden = low_back(jnp.dot(slot_rows, weight_in, precision=FULL_PRECISION))
        activated = low(jax.nn.gelu(hidden))
        expert_out = low_back(low(jnp.dot(activated, weight_out, precision=FULL_PRECISION)))
        return (totals.at[safe_rows].add(expert_out * (gate_rows * filled)[:, None]), None)
    mixture, unused = lax.scan(jax.checkpoint(expert_step), jnp.zeros_like(residual), (in_weights, out_weights, slot_token, slot_gate))
    return residual + mixture

def orthogonalize(moment):
    current = moment / (jnp.sqrt(jnp.sum(moment * moment)) + 1e-07)
    for repeat in range(ITERS):
        gram_matrix = jnp.dot(current, current.T, precision=FULL_PRECISION)
        polynomial = SCHULZ_SQUARE * gram_matrix + SCHULZ_QUARTIC * jnp.dot(gram_matrix, gram_matrix, precision=FULL_PRECISION)
        current = SCHULZ_LINEAR * current + jnp.dot(polynomial, current, precision=FULL_PRECISION)
    return current

def orthogonalize_tall(moment):
    return orthogonalize(moment.T).T

def reference(tokens, cotangent, expert_ids, gate_units, capacity, frozen, attn_copy, attn_master, attn_momentum, norm_params, norm_first, norm_second, up_copy, up_master, up_momentum, down_copy, down_master, down_momentum):
    slot_token, slot_gate = route_tables(expert_ids, gate_units, capacity)

    def closed(inputs_f, attn_weights, norm_values, in_weights, out_weights):
        return forward(inputs_f, attn_weights, norm_values, in_weights, out_weights, slot_token, slot_gate)
    result, pullback = jax.vjp(closed, tokens.astype(jnp.float32), attn_copy.astype(jnp.float32), norm_params, up_copy.astype(jnp.float32), down_copy.astype(jnp.float32))
    grad_input, grad_attn, grad_norm, grad_up, grad_down = pullback(cotangent.astype(jnp.float32))
    attn_moment = MOMENT_KEEP * attn_momentum + grad_attn
    attn_ortho = lax.map(orthogonalize, attn_moment)
    attn_new = attn_master * (1.0 - MUON_RATE * MUON_DECAY) - MUON_RATE * 0.2 * D ** 0.5 * attn_ortho
    frozen_mask = (frozen > 0)[:, None, None]
    wide_scale = 0.2 * max(D, FF) ** 0.5
    up_fresh = MOMENT_KEEP * up_momentum + grad_up
    up_ortho = lax.map(orthogonalize, up_fresh)
    up_new = jnp.where(frozen_mask, up_master, up_master * (1.0 - MUON_RATE * MUON_DECAY) - MUON_RATE * wide_scale * up_ortho)
    up_moment = jnp.where(frozen_mask, up_momentum, up_fresh)
    down_fresh = MOMENT_KEEP * down_momentum + grad_down
    down_ortho = lax.map(orthogonalize_tall, down_fresh)
    down_new = jnp.where(frozen_mask, down_master, down_master * (1.0 - MUON_RATE * MUON_DECAY) - MUON_RATE * wide_scale * down_ortho)
    down_moment = jnp.where(frozen_mask, down_momentum, down_fresh)
    first_new = FIRST_DECAY * norm_first + (1.0 - FIRST_DECAY) * grad_norm
    second_new = SECOND_DECAY * norm_second + (1.0 - SECOND_DECAY) * grad_norm * grad_norm
    first_hat = first_new / (1.0 - FIRST_DECAY ** STEP_COUNT)
    second_hat = second_new / (1.0 - SECOND_DECAY ** STEP_COUNT)
    norm_new = norm_params - ADAM_RATE * (first_hat / (jnp.sqrt(second_hat) + ADAM_EPSILON) + ADAM_DECAY * norm_params)
    return (result.astype(jnp.bfloat16), grad_input, attn_new, attn_moment, attn_new.astype(jnp.bfloat16), up_new, up_moment, up_new.astype(jnp.bfloat16), down_new, down_moment, down_new.astype(jnp.bfloat16), norm_new, first_new, second_new)
```

```python
import functools

import jax
import jax.numpy as jnp
from jax import lax
from jax.experimental import pallas as pl
from jax.experimental.pallas import tpu as pltpu
from jax.sharding import PartitionSpec as P

HEADS = 12
FF = 3072
ITERS = 5
STEP_COUNT = 10

NORM_EPSILON = 1e-05
SCHULZ_LINEAR = 3.4445
SCHULZ_SQUARE = -4.775
SCHULZ_QUARTIC = 2.0315
MUON_RATE = 0.2
MUON_DECAY = 0.01
MOMENT_KEEP = 0.5
ADAM_RATE = 0.5
FIRST_DECAY = 0.9
SECOND_DECAY = 0.999
ADAM_EPSILON = 1e-08
ADAM_DECAY = 0.01
GATE_UNIT = 4096.0

CENTRE = -SCHULZ_SQUARE / (2.0 * SCHULZ_QUARTIC)
REST = SCHULZ_LINEAR - SCHULZ_QUARTIC * CENTRE * CENTRE

GELU_SCALE = 0.7978845608028654
GELU_CUBIC = 0.044715

LOW = jnp.bfloat16
WIDE = jnp.float32
MIB = 1024 * 1024


def nn(left, right):
    return jnp.dot(left, right, preferred_element_type=WIDE)


def nt(left, right):
    return lax.dot_general(left, right, (((1,), (1,)), ((), ())), preferred_element_type=WIDE)


def tn(left, right):
    return lax.dot_general(left, right, (((0,), (0,)), ((), ())), preferred_element_type=WIDE)


def iota(shape, axis):
    return lax.broadcasted_iota(jnp.int32, shape, axis)


def shape_of(shape, dtype):
    return jax.ShapeDtypeStruct(shape, dtype)


def call(kernel, outs, args, flops, vmem=40, grid=None, in_specs=None, out_specs=None, scratch=()):
    moved = sum(a.size * a.dtype.itemsize for a in args)
    moved += sum(o.size * o.dtype.itemsize for o in outs)
    more = {}
    if grid is not None:
        more["grid"] = grid
    if in_specs is None:
        in_specs = [pl.BlockSpec(memory_space=pltpu.VMEM)] * len(args)
    if out_specs is None:
        out_specs = [pl.BlockSpec(memory_space=pltpu.VMEM)] * len(outs)
    return pl.pallas_call(
        kernel,
        out_shape=list(outs),
        in_specs=in_specs,
        out_specs=out_specs,
        scratch_shapes=list(scratch),
        compiler_params=pltpu.CompilerParams(vmem_limit_bytes=vmem * MIB),
        cost_estimate=pl.CostEstimate(flops=int(flops), bytes_accessed=int(moved), transcendentals=0),
        **more,
    )(*args)


def swap(value, axis, mask):
    count = lax.axis_size(axis)
    return lax.ppermute(value, axis, [(i, i ^ mask) for i in range(count)])


def dispatch_masks(meta, slots):
    lanes = iota((meta.shape[0], slots), 1).astype(WIDE)
    return lanes == meta[:, 0:1], lanes == meta[:, 1:2]


def gated_parts(meta, slots):
    first, second = dispatch_masks(meta, slots)
    gates = jnp.where(first, meta[:, 2:3], 0.0) + jnp.where(second, meta[:, 3:4], 0.0)
    high = gates.astype(LOW)
    return high, (gates - high.astype(WIDE)).astype(LOW)


def route_kernel(ids_ref, units_ref, capacity_ref, cotangent_ref, meta_ref, grads_ref, *, cap):
    rows = ids_ref.shape[0]
    lanes = iota((rows, 128), 1)
    ids = ids_ref[...]
    hots = [(lanes == ids[:, i : i + 1]).astype(WIDE) for i in range(2)]
    earlier = (iota((rows, rows), 0) > iota((rows, rows), 1)).astype(WIDE).astype(LOW)
    counts = nn(earlier, (hots[0] + hots[1]).astype(LOW))
    gates = units_ref[...].astype(WIDE) / GATE_UNIT
    meta = jnp.zeros((rows, 128), WIDE)
    for i in range(2):
        placed = jnp.sum(hots[i] * counts, axis=1, keepdims=True)
        limit = jnp.sum(hots[i] * capacity_ref[...], axis=1, keepdims=True)
        kept = placed < limit
        slot = jnp.where(kept, ids[:, i : i + 1].astype(WIDE) * cap + placed, -1.0)
        meta = jnp.where(lanes == i, slot, meta)
        meta = jnp.where(lanes == 2 + i, gates[:, i : i + 1], meta)
    meta_ref[...] = meta
    high, rest = gated_parts(meta, grads_ref.shape[0])
    cotangent = cotangent_ref[...]
    grads_ref[...] = (tn(high, cotangent) + tn(rest, cotangent)).astype(LOW)


def normalize(values):
    centre = values - jnp.mean(values, axis=-1, keepdims=True)
    spread = jnp.mean(centre * centre, axis=-1, keepdims=True)
    inverse = lax.rsqrt(spread + NORM_EPSILON)
    return centre * inverse, inverse


def head_probs(query, key, scale):
    rows = query.shape[0]
    scores = nt(query, key) * scale
    scores = jnp.where(iota((rows, rows), 1) <= iota((rows, rows), 0), scores, -1e30)
    exps = jnp.exp(scores - jnp.max(scores, axis=-1, keepdims=True))
    return exps / jnp.sum(exps, axis=-1, keepdims=True)


def front_kernel(
    tokens_ref, weights_ref, norm_ref, meta_ref,
    low_ref, query_ref, key_ref, value_ref, attended_ref, residual_ref, rows_ref, *, head,
):
    width = tokens_ref.shape[1]
    scale = head**-0.5
    inputs = tokens_ref[...].astype(WIDE)
    unit, _ = normalize(inputs)
    low = (unit * norm_ref[0:1, :] + norm_ref[1:2, :]).astype(LOW)
    low_ref[...] = low
    for which, ref in enumerate((query_ref, key_ref, value_ref)):
        ref[...] = nn(low, weights_ref[which]).astype(LOW)
    group = 128 // head
    lane = iota((1, 128), 1) // head
    for at in range(0, width, 128):
        query, key, value = (r[:, at : at + 128] for r in (query_ref, key_ref, value_ref))
        total = jnp.zeros(query.shape, WIDE)
        for h in range(group):
            mine = lane == h
            probs = head_probs(jnp.where(mine, query, jnp.zeros_like(query)), key, scale)
            total = jnp.where(mine, nn(probs.astype(LOW), value), total)
        attended_ref[:, at : at + 128] = total.astype(LOW)
    residual = inputs + nn(attended_ref[...], weights_ref[3])
    residual_ref[...] = residual
    unit, _ = normalize(residual)
    low = (unit * norm_ref[2:3, :] + norm_ref[3:4, :]).astype(LOW)
    first, second = dispatch_masks(meta_ref[...], rows_ref.shape[0])
    chosen = (first | second).astype(WIDE).astype(LOW)
    rows_ref[...] = tn(chosen, low).astype(LOW)


def expert_kernel(rows_ref, grads_ref, *refs, parts, step):
    ups, downs = refs[:parts], refs[parts : 2 * parts]
    act_refs, hid_refs = refs[2 * parts : 3 * parts], refs[3 * parts : 4 * parts]
    back_ref, out_ref = refs[4 * parts :]

    def block(i, carry):
        here = pl.ds(pl.multiple_of(i * step, step), step)
        rows, grads = rows_ref[here, :], grads_ref[here, :]
        back = jnp.zeros((step, rows.shape[1]), WIDE)
        out = jnp.zeros((step, rows.shape[1]), WIDE)
        for r in range(parts):
            hidden = nn(rows, ups[r][...])
            grad = nt(grads, downs[r][...])
            square = hidden * hidden
            bend = jnp.tanh(hidden * (GELU_SCALE + GELU_SCALE * GELU_CUBIC * square))
            half = 0.5 + 0.5 * bend
            act = (hidden * half).astype(LOW)
            slope = GELU_SCALE + 3.0 * GELU_SCALE * GELU_CUBIC * square
            curve = half + 0.5 * hidden * (1.0 - bend * bend) * slope
            hid = (grad * curve).astype(LOW)
            act_refs[r][here, :] = act
            hid_refs[r][here, :] = hid
            back = back + nt(hid, ups[r][...])
            out = out + nn(act, downs[r][...])
        back_ref[here, :] = back.astype(LOW)
        out_ref[here, :] = out.astype(LOW)
        return carry

    lax.fori_loop(0, rows_ref.shape[0] // step, block, 0)


def mix_kernel(returned_ref, residual_ref, meta_ref, output_ref):
    high, rest = gated_parts(meta_ref[...], returned_ref.shape[0])
    returned = returned_ref[...]
    output_ref[...] = (residual_ref[...] + nn(high, returned) + nn(rest, returned)).astype(LOW)


def norm_backward(grad, unit, inverse, gain):
    scaled = grad * gain
    mean = jnp.mean(scaled, axis=-1, keepdims=True)
    along = jnp.mean(scaled * unit, axis=-1, keepdims=True)
    return inverse * (scaled - mean - unit * along)


def back_kernel(
    returned_ref, meta_ref, tokens_ref, cotangent_ref, residual_ref, norm_ref, weights_ref,
    query_ref, key_ref, value_ref, right_ref, input_ref, sums_ref, *, head,
):
    width = tokens_ref.shape[1]
    scale = head**-0.5
    first, second = dispatch_masks(meta_ref[...], returned_ref.shape[0])
    chosen = (first | second).astype(WIDE).astype(LOW)
    grad = nn(chosen, returned_ref[...])
    unit, inverse = normalize(residual_ref[...])
    sums_ref[2:3, :] = jnp.sum(grad * unit, axis=0, keepdims=True)
    sums_ref[3:4, :] = jnp.sum(grad, axis=0, keepdims=True)
    through = cotangent_ref[...].astype(WIDE) + norm_backward(grad, unit, inverse, norm_ref[2:3, :])
    branch = through.astype(LOW)
    right_ref[3] = branch
    grad_heads = nt(branch, weights_ref[3]).astype(LOW)
    group = 128 // head
    lane = iota((1, 128), 1) // head
    for at in range(0, width, 128):
        query, key, value = (r[:, at : at + 128] for r in (query_ref, key_ref, value_ref))
        grad_out = grad_heads[:, at : at + 128]
        none = jnp.zeros_like(query)
        totals = [jnp.zeros(query.shape, WIDE) for _ in range(3)]
        for h in range(group):
            mine = lane == h
            probs = head_probs(jnp.where(mine, query, none), key, scale)
            dprob = nt(jnp.where(mine, grad_out, none), value)
            centre = jnp.sum(probs * dprob, axis=-1, keepdims=True)
            dscore = (probs * (dprob - centre)).astype(LOW)
            parts = (
                nn(dscore, key) * scale,
                tn(dscore, query) * scale,
                tn(probs.astype(LOW), grad_out),
            )
            totals = [jnp.where(mine, p, t) for p, t in zip(parts, totals)]
        for which in range(3):
            right_ref[which, :, at : at + 128] = totals[which].astype(LOW)
    grad = nt(right_ref[0], weights_ref[0])
    grad = grad + nt(right_ref[1], weights_ref[1])
    grad = grad + nt(right_ref[2], weights_ref[2])
    unit, inverse = normalize(tokens_ref[...].astype(WIDE))
    sums_ref[0:1, :] = jnp.sum(grad * unit, axis=0, keepdims=True)
    sums_ref[1:2, :] = jnp.sum(grad, axis=0, keepdims=True)
    input_ref[...] = through + norm_backward(grad, unit, inverse, norm_ref[0:1, :])


def products_kernel(*refs, parts):
    total = tn(refs[0][...], refs[parts][...])
    for r in range(1, parts):
        total = total + tn(refs[r][...], refs[parts + r][...])
    refs[2 * parts][...] = total.astype(LOW)


def diagonal(matrix):
    same = iota(matrix.shape, 0) == iota(matrix.shape, 1)
    return same, jnp.sum(jnp.where(same, matrix, 0.0), axis=1, keepdims=True)


def split_diagonal(matrix):
    same, line = diagonal(matrix)
    return line, jnp.where(same, 0.0, matrix).astype(LOW)


def quadratic(gram):
    same = iota(gram.shape, 0) == iota(gram.shape, 1)
    shifted = jnp.where(same, gram - CENTRE, gram)
    line, rest = split_diagonal(shifted)
    square = line * shifted + nn(rest, shifted.astype(LOW))
    line, rest = split_diagonal(square * SCHULZ_QUARTIC)
    return line + REST, rest


def attn_step_kernel(grad_ref, momentum_ref, master_ref, moment_ref, new_ref, low_ref, now_ref):
    width = grad_ref.shape[1]
    moment = MOMENT_KEEP * momentum_ref[...] + grad_ref[...].astype(WIDE)
    moment_ref[...] = moment
    length = jnp.sqrt(jnp.sum(moment * moment)) + 1e-07
    now_ref[...] = moment * (1.0 / length)

    def step(i, carry):
        now = now_ref[...]
        low = now.astype(LOW)
        line, rest = quadratic(nt(low, low))
        now_ref[...] = line * now + nn(rest, low)
        return carry

    lax.fori_loop(0, ITERS, step, 0)
    new = master_ref[...] * (1.0 - MUON_RATE * MUON_DECAY) - MUON_RATE * 0.2 * width**0.5 * now_ref[...]
    new_ref[...] = new
    low_ref[...] = new.astype(LOW)


BLOCK = 256


def packed_width(width):
    return sum(width - at for at in range(0, width, BLOCK))


def moments_kernel(
    flags_ref, up_a, up_b, down_a, down_b, up_mom, down_mom,
    up_moment, down_moment, keep_ref, send_ref,
):
    frozen = flags_ref[0] > 0
    up_fresh = MOMENT_KEEP * up_mom[...] + up_a[...] + up_b[...].astype(WIDE)
    down_fresh = MOMENT_KEEP * down_mom[...] + down_a[...] + down_b[...].astype(WIDE)
    up_moment[...] = jnp.where(frozen, up_mom[...], up_fresh)
    down_moment[...] = jnp.where(frozen, down_mom[...], down_fresh)
    up_low, down_low = up_fresh.astype(LOW), down_fresh.astype(LOW)
    width = up_fresh.shape[0]
    even = flags_ref[1] == 0
    column = 0
    for at in range(0, width, BLOCK):
        up_gram = nt(up_low[at : at + BLOCK, :], up_low[at:, :])
        down_gram = tn(down_low[:, at : at + BLOCK], down_low[:, at:])
        here = slice(column, column + width - at)
        keep_ref[:, here] = jnp.where(even, up_gram, down_gram)
        send_ref[:, here] = jnp.where(even, down_gram, up_gram)
        column += width - at


def polar_kernel(mine_ref, other_ref, result_ref, gram_ref, next_ref):
    width = gram_ref.shape[0]
    column = 0
    for at in range(0, width, BLOCK):
        here = slice(column, column + width - at)
        strip = mine_ref[:, here] + other_ref[:, here]
        gram_ref[at : at + BLOCK, at:] = strip
        for far in range(BLOCK, width - at, BLOCK):
            gram_ref[at + far : at + far + BLOCK, at : at + BLOCK] = strip[:, far : far + BLOCK].T
        column += width - at
    _, line = diagonal(gram_ref[...])
    length = jnp.sqrt(jnp.sum(line)) + 1e-07
    gram_ref[...] = gram_ref[...] * (1.0 / (length * length))
    product_ref = next_ref
    for k in range(ITERS):
        gram = gram_ref[...]
        line, rest = quadratic(gram)
        if k == 0:
            same = iota(gram.shape, 0) == iota(gram.shape, 1)
            product_ref[...] = jnp.where(same, line, rest.astype(WIDE))
        else:
            product = product_ref[...]
            product_ref[...] = line * product + nn(rest, product.astype(LOW))
        if k < ITERS - 1:
            half = line * gram + nn(rest, gram.astype(LOW))
            gram_ref[...] = line * half + nn(rest, half.astype(LOW))
    result_ref[...] = (product_ref[...] * (1.0 / length)).astype(LOW)


def apply_kernel(
    flags_ref, up_factor, down_factor, up_moment, down_moment, up_master, down_master,
    up_new, up_low, down_new, down_low, *, wide_scale,
):
    frozen = flags_ref[0] > 0
    for master, new_ref, low_ref, ortho in (
        (up_master, up_new, up_low, nn(up_factor[...], up_moment[...].astype(LOW))),
        (down_master, down_new, down_low, nn(down_moment[...].astype(LOW), down_factor[...])),
    ):
        old = master[...]
        new = old * (1.0 - MUON_RATE * MUON_DECAY) - MUON_RATE * wide_scale * ortho
        new = jnp.where(frozen, old, new)
        new_ref[...] = new
        low_ref[...] = new.astype(LOW)


def masks_of(axis):
    count = lax.axis_size(axis)
    return [1 << i for i in range(count.bit_length() - 1)]


def bit_of(axis, mask):
    return (lax.axis_index(axis) & mask) > 0


def sum_over(value, axis, masks):
    if len(masks) == 1:
        return (value.astype(WIDE) + swap(value, axis, masks[0]).astype(WIDE)).astype(value.dtype)
    half = value.shape[0] // 2
    upper = bit_of(axis, masks[0])
    low, high = value[:half], value[half:]
    came = swap(jnp.where(upper, low, high), axis, masks[0])
    mine = (jnp.where(upper, high, low).astype(WIDE) + came.astype(WIDE)).astype(value.dtype)
    mine = sum_over(mine, axis, masks[1:])
    came = swap(mine, axis, masks[0])
    return jnp.concatenate([jnp.where(upper, came, mine), jnp.where(upper, mine, came)], axis=0)


def total_over(value, axes):
    for axis in axes:
        for mask in masks_of(axis):
            value = value + swap(value, axis, mask)
    return value


def body(
    tokens,
    cotangent,
    expert_ids,
    gate_units,
    capacity,
    frozen,
    attn_copy,
    attn_master,
    attn_momentum,
    norm_params,
    norm_first,
    norm_second,
    up_copy,
    up_master,
    up_momentum,
    down_copy,
    down_master,
    down_momentum,
):
    rows, width = tokens.shape
    cuts = lax.axis_size("cuts")
    experts = capacity.shape[0]
    cap = 4 * rows // lax.axis_size("expert")
    slots = experts * cap
    head = width // HEADS
    hidden = up_copy.shape[2]
    cut = lax.axis_index("cuts")

    ups, downs = [up_copy[0]], [down_copy[0]]
    for mask in reversed(masks_of("cuts")):
        ups = ups + [swap(w, "cuts", mask) for w in ups]
        downs = downs + [swap(w, "cuts", mask) for w in downs]
    order = [0]
    for mask in reversed(masks_of("cuts")):
        order = order + [o ^ mask for o in order]
    place = [order.index(r) for r in range(cuts)]
    ups, downs = [ups[p] for p in place], [downs[p] for p in place]

    capacity_row = jnp.pad(capacity.astype(WIDE), (0, 128 - experts))[None]
    meta, send_grads = call(
        functools.partial(route_kernel, cap=cap),
        [shape_of((rows, 128), WIDE), shape_of((slots, width), LOW)],
        [expert_ids, gate_units, capacity_row, cotangent],
        4 * rows * slots * width,
    )

    def to_experts(value):
        return lax.all_to_all(value, "expert", split_axis=0, concat_axis=0, tiled=True)

    slot_grads = to_experts(send_grads)
    small = shape_of((rows, width), LOW)
    normed_low, query, key, value, attended, residual, send_rows = call(
        functools.partial(front_kernel, head=head),
        [small] * 5 + [shape_of((rows, width), WIDE), shape_of((slots, width), LOW)],
        [tokens, attn_copy, norm_params, meta],
        2 * rows * width * (4 * width + 4 * rows + slots),
    )
    slot_rows = to_experts(send_rows)

    def left_for(r):
        last = (cut ^ r) == cuts - 1
        return jnp.where(last, attended, normed_low)

    lefts = [left_for(0)] + [swap(left_for(r), "cuts", r) for r in range(1, cuts)]

    step = 256
    wide = shape_of((slots, hidden), LOW)
    outs = call(
        functools.partial(expert_kernel, parts=cuts, step=step),
        [wide] * (2 * cuts) + [shape_of((slots, width), LOW)] * 2,
        [slot_rows, slot_grads, *ups, *downs],
        8 * slots * width * hidden * cuts,
        vmem=56,
    )
    acts, hids = outs[:cuts], outs[cuts : 2 * cuts]
    slot_back, slot_out = outs[2 * cuts :]
    returned_grads = to_experts(slot_back)

    def weight_grads(r, dtype):
        return (
            tn(slot_rows, hids[r]).astype(dtype),
            tn(acts[r], slot_grads).astype(dtype),
        )

    sums = {r: weight_grads(r, LOW if r & 1 else WIDE) for r in range(cuts)}
    sums = {
        r: tuple(g + swap(h, "cuts", 1).astype(WIDE) for g, h in zip(sums[r], sums[r ^ 1]))
        for r in range(0, cuts, 2)
    }
    up_other, down_other = (swap(g.astype(LOW), "cuts", 2) for g in sums[2])
    up_own, down_own = sums[0]

    returned = to_experts(slot_out)

    rights, input_grad, norm_sums = call(
        functools.partial(back_kernel, head=head),
        [shape_of((4, rows, width), LOW), shape_of((rows, width), WIDE), shape_of((4, width), WIDE)],
        [
            returned_grads, meta, tokens, cotangent, residual, norm_params, attn_copy,
            query, key, value,
        ],
        2 * rows * width * (4 * width + 10 * rows + slots),
    )

    def right_for(r):
        return lax.dynamic_index_in_dim(rights, cut ^ r, 0, keepdims=False)

    rights = [right_for(0)] + [swap(right_for(r), "cuts", r) for r in range(1, cuts)]
    (attn_grad,) = call(
        functools.partial(products_kernel, parts=cuts),
        [shape_of((width, width), LOW)],
        [*lefts, *rights],
        2 * cuts * rows * width * width,
    )
    masks = masks_of("expert")
    half = width // 2
    attn_grad = jnp.concatenate(
        [
            sum_over(attn_grad[:half], "expert", masks),
            sum_over(attn_grad[half:], "expert", [masks[1], masks[0], *masks[2:]]),
        ],
        axis=0,
    )
    norm_total = total_over(norm_sums, ("cuts", "expert"))

    flags = jnp.stack([frozen[0], cut & 1])
    square = shape_of((width, width), WIDE)
    packed = shape_of((BLOCK, packed_width(width)), WIDE)
    whole = pl.BlockSpec(memory_space=pltpu.VMEM)
    scalars = pl.BlockSpec(memory_space=pltpu.SMEM)
    up_moment, down_moment, keep, send = call(
        moments_kernel,
        [square, square, packed, packed],
        [flags, up_own, up_other, down_own, down_other, up_momentum[0], down_momentum[0]],
        4 * width**3,
        in_specs=[scalars] + [whole] * 6,
    )
    keep = keep + swap(send, "cuts", 1)
    other = swap(keep, "cuts", 2)
    (factor,) = call(
        polar_kernel,
        [shape_of((width, width), LOW)],
        [keep, other],
        17 * 2 * width**3,
        scratch=[pltpu.VMEM((width, width), WIDE)] * 2,
    )
    other_factor = swap(factor, "cuts", 1)
    even = (cut & 1) == 0
    up_factor = jnp.where(even, factor, other_factor)
    down_factor = jnp.where(even, other_factor, factor)
    strips = pl.BlockSpec((BLOCK, width), lambda i: (i, 0))
    every = pl.BlockSpec((width, width), lambda i: (0, 0))
    low_square = shape_of((width, width), LOW)
    up_new, up_low, down_new, down_low = call(
        functools.partial(apply_kernel, wide_scale=0.2 * max(width, FF) ** 0.5),
        [square, low_square, square, low_square],
        [flags, up_factor, down_factor, up_moment, down_moment, up_master[0], down_master[0]],
        4 * width**3,
        grid=(width // BLOCK,),
        in_specs=[scalars, strips, every, every, strips, strips, strips],
        out_specs=[strips] * 4,
    )

    attn_moment, attn_new, attn_low = call(
        attn_step_kernel,
        [square, square, low_square],
        [attn_grad, attn_momentum[0], attn_master[0]],
        15 * 2 * width**3,
        scratch=[pltpu.VMEM((width, width), WIDE)],
    )

    (output,) = call(
        mix_kernel,
        [small],
        [returned, residual, meta],
        4 * rows * slots * width,
    )

    first_new = FIRST_DECAY * norm_first + (1.0 - FIRST_DECAY) * norm_total
    second_new = SECOND_DECAY * norm_second + (1.0 - SECOND_DECAY) * norm_total * norm_total
    first_hat = first_new / (1.0 - FIRST_DECAY**STEP_COUNT)
    second_hat = second_new / (1.0 - SECOND_DECAY**STEP_COUNT)
    norm_new = norm_params - ADAM_RATE * (
        first_hat / (jnp.sqrt(second_hat) + ADAM_EPSILON) + ADAM_DECAY * norm_params
    )
    return (
        output,
        input_grad,
        attn_new[None],
        attn_moment[None],
        attn_low[None],
        up_new[None],
        up_moment[None],
        up_low[None],
        down_new[None],
        down_moment[None],
        down_low[None],
        norm_new,
        first_new,
        second_new,
    )


def solution(mesh):
    rows = P(("expert", "cuts"), None)
    attn = P("cuts", None, None)
    ups = P("expert", None, "cuts")
    downs = P("expert", "cuts", None)
    return jax.shard_map(
        body,
        mesh=mesh,
        in_specs=(rows, rows, rows, rows, P(), P("expert"), P(), attn, attn, P(), P(), P())
        + (ups, ups, ups, downs, downs, downs),
        out_specs=(rows, rows, attn, attn, attn, ups, ups, ups, downs, downs, downs, P(), P(), P()),
        check_vma=False,
    )
```

```python
import functools

import jax
import jax.numpy as jnp
from jax import lax
from jax.experimental import pallas as pl
from jax.experimental.pallas import tpu as pltpu
from jax.sharding import PartitionSpec as P

HEADS = 12
FF = 3072
ITERS = 5
STEP_COUNT = 10

NORM_EPSILON = 1e-05
SCHULZ_LINEAR = 3.4445
SCHULZ_SQUARE = -4.775
SCHULZ_QUARTIC = 2.0315
MUON_RATE = 0.2
MUON_DECAY = 0.01
MOMENT_KEEP = 0.5
ADAM_RATE = 0.5
FIRST_DECAY = 0.9
SECOND_DECAY = 0.999
ADAM_EPSILON = 1e-08
ADAM_DECAY = 0.01
GATE_UNIT = 4096.0

CENTRE = -SCHULZ_SQUARE / (2.0 * SCHULZ_QUARTIC)
REST = SCHULZ_LINEAR - SCHULZ_QUARTIC * CENTRE * CENTRE

GELU_SCALE = 0.7978845608028654
GELU_CUBIC = 0.044715

LOW = jnp.bfloat16
WIDE = jnp.float32
MIB = 1024 * 1024


def nn(left, right):
    return jnp.dot(left, right, preferred_element_type=WIDE)


def nt(left, right):
    return lax.dot_general(left, right, (((1,), (1,)), ((), ())), preferred_element_type=WIDE)


def tn(left, right):
    return lax.dot_general(left, right, (((0,), (0,)), ((), ())), preferred_element_type=WIDE)


def iota(shape, axis):
    return lax.broadcasted_iota(jnp.int32, shape, axis)


def shape_of(shape, dtype):
    return jax.ShapeDtypeStruct(shape, dtype)


VMEM_BYTES = 63 * MIB


class Fetch:
    def __init__(self, source, held, semaphore):
        self.held, self.pending = held, pltpu.make_async_copy(source, held, semaphore)
        self.pending.start()

    def ref(self):
        if self.pending is not None:
            self.pending.wait()
            self.pending = None
        return self.held

    def get(self):
        return self.ref()[...]


class Put:
    def __init__(self, target, held, semaphore):
        self.ref, self.copy, self.started = held, pltpu.make_async_copy(held, target, semaphore), False

    def send(self):
        self.copy.start()
        self.started = True

    def set(self, value):
        self.ref[...] = value.astype(self.ref.dtype)
        self.send()

    def finish(self):
        if not self.started:
            self.send()
        self.copy.wait()


def views(ref, parts):
    if parts == 1:
        return [ref]
    size = ref.shape[0] // parts
    return [ref.at[pl.ds(i * size, size)] for i in range(parts)]


def staged_call(kernel, ins, outs, flops, smem=(), scratch=(), after=()):
    ins = [i if isinstance(i, tuple) else (i, 1) for i in ins]
    outs = [o if isinstance(o, tuple) else (o, 1) for o in outs]
    first, given, wanted, extra = len(smem), len(ins), len(outs), len(scratch)
    reads, writes = sum(n for _, n in ins), sum(n for _, n in outs)
    staged = sum(n > 0 for _, n in ins)

    def run(*refs):
        scalars, sources, refs = refs[:first], refs[first : first + given], refs[first + given + len(after) :]
        targets, work, refs = refs[:wanted], refs[wanted : wanted + extra], refs[wanted + extra :]
        held_in, held_out, (in_sem, out_sem) = refs[:staged], refs[staged : staged + wanted], refs[staged + wanted :]
        fetches, puts = [], []
        held_in, reads = list(held_in), 0
        for source, (_, n) in zip(sources, ins):
            if n == 0:
                fetches.append(source)
                continue
            for a, b in zip(views(source, n), views(held_in.pop(0), n)):
                fetches.append(Fetch(a, b, in_sem.at[reads]))
                reads += 1
        for target, held, (_, n) in zip(targets, held_out, outs):
            for a, b in zip(views(target, n), views(held, n)):
                puts.append(Put(a, b, out_sem.at[len(puts)]))
        kernel(*scalars, fetches, puts, *work)
        for put in puts:
            put.finish()

    shapes = [i for i, n in ins if n > 0] + [o for o, _ in outs]
    hbm = pl.BlockSpec(memory_space=pltpu.HBM)
    return pl.pallas_call(
        run,
        out_shape=[o for o, _ in outs],
        in_specs=[pl.BlockSpec(memory_space=pltpu.SMEM)] * first
        + [hbm] * given
        + [hbm] * len(after),
        out_specs=[hbm] * wanted,
        scratch_shapes=[
            *scratch,
            *[pltpu.VMEM(s.shape, s.dtype) for s in shapes],
            pltpu.SemaphoreType.DMA((max(reads, 1),)),
            pltpu.SemaphoreType.DMA((writes,)),
        ],
        compiler_params=pltpu.CompilerParams(vmem_limit_bytes=VMEM_BYTES),
        cost_estimate=pl.CostEstimate(flops=1, bytes_accessed=1, transcendentals=0),
    )(*smem, *[i for i, _ in ins], *after)


def swap(value, axis, mask):
    count = lax.axis_size(axis)
    return lax.ppermute(value, axis, [(i, i ^ mask) for i in range(count)])


def turned(meta):
    return meta.T


def chosen_slots(meta, slots):
    rows = iota((slots, meta.shape[1]), 0).astype(WIDE)
    return ((rows == meta[0:1, :]) | (rows == meta[1:2, :])).astype(WIDE).astype(LOW)


def split_gates(gates):
    high = gates.astype(LOW)
    return high, (gates - high.astype(WIDE)).astype(LOW)


def gated_rows(meta, values, slots):
    rows = iota((slots, meta.shape[1]), 0).astype(WIDE)
    gates = jnp.where(rows == meta[0:1, :], meta[2:3, :], 0.0) + jnp.where(rows == meta[1:2, :], meta[3:4, :], 0.0)
    high, rest = split_gates(gates)
    return (nn(high, values) + nn(rest, values)).astype(LOW)


def collect(meta, pieces, gated):
    meta = turned(meta)
    lanes = iota((meta.shape[0], pieces.shape[0]), 1).astype(WIDE)
    first, second = lanes == meta[:, 0:1], lanes == meta[:, 1:2]
    if not gated:
        return nn((first | second).astype(WIDE).astype(LOW), pieces)
    high, rest = split_gates(jnp.where(first, meta[:, 2:3], 0.0) + jnp.where(second, meta[:, 3:4], 0.0))
    return nn(high, pieces) + nn(rest, pieces)


SMALL = 64.0
SPARE = 16


def routed(ids, units, capacity_ref, me, cap):
    rows = ids.shape[1]
    experts = capacity_ref.shape[0]
    numbers = iota((experts, rows), 0)
    hots = [numbers == ids[i : i + 1, :] for i in range(2)]
    later = (iota((rows, rows), 0) < iota((rows, rows), 1)).astype(WIDE).astype(LOW)
    counts = nn((hots[0] | hots[1]).astype(WIDE).astype(LOW), later)
    slots = []
    for i in range(2):
        name = ids[i : i + 1, :]
        placed = jnp.sum(jnp.where(hots[i], counts, 0.0), axis=0, keepdims=True)
        limit = jnp.zeros_like(name)
        for e in range(experts):
            limit = jnp.where(name == e, capacity_ref[e], limit)
        near = (name ^ me).astype(WIDE)
        slots.append(jnp.where(placed < limit.astype(WIDE), near * cap + placed, -1.0))
    empty = jnp.zeros((1, rows), WIDE)
    meta = jnp.concatenate([*slots, units[0:1, :] / GATE_UNIT, units[1:2, :] / GATE_UNIT] + [empty] * 4, axis=0)
    return meta


def pack_kernel(flags_ref, capacity_ref, ins, outs, *, cap):
    ids_in, units_in, cotangent_in = ins
    meta_out, packed_out, *sends = outs
    rows, width = cotangent_in.held.shape
    ids, units = ids_in.get(), units_in.get().astype(WIDE)
    high = jnp.floor(units * (1.0 / SMALL))
    empty = jnp.zeros((SPARE - 6, rows), WIDE)
    lines = jnp.concatenate([ids.astype(WIDE), high, units - high * SMALL, empty], axis=0)
    packed_out.ref[rows:, :] = jnp.zeros((SPARE, width), LOW)
    packed_out.ref[rows:, 0:rows] = lines.astype(LOW)
    packed_out.ref[0:rows, :] = cotangent_in.get()
    packed_out.send()
    meta = routed(ids, units, capacity_ref, flags_ref[2], cap)
    meta_out.set(meta)
    put_slots(sends, [gated_rows(meta, cotangent_in.get(), len(sends) * cap)], cap)


def unpack(lines):
    lines = lines.astype(WIDE)
    return lines[0:2, :].astype(jnp.int32), lines[2:4, :] * SMALL + lines[4:6, :]


def far_kernel(ins, outs, *, cap):
    meta_in, low_in = ins
    low = nn(chosen_slots(meta_in.get(), len(outs) * cap), low_in.get()).astype(LOW)
    put_slots(outs, [low], cap)


def put_slots(sends, parts, cap):
    for r, put in enumerate(sends):
        for at, part in enumerate(parts):
            put.ref[at * cap : (at + 1) * cap, :] = part[r * cap : (r + 1) * cap, :]
        put.send()


def normalize(values):
    centre = values - jnp.mean(values, axis=-1, keepdims=True)
    spread = jnp.mean(centre * centre, axis=-1, keepdims=True)
    inverse = lax.rsqrt(spread + NORM_EPSILON)
    return centre * inverse, inverse


def head_probs(query, key, scale):
    rows = query.shape[0]
    scores = nt(query, key) * scale
    scores = jnp.where(iota((rows, rows), 1) <= iota((rows, rows), 0), scores, -1e30)
    exps = jnp.exp(scores - jnp.max(scores, axis=-1, keepdims=True))
    return exps / jnp.sum(exps, axis=-1, keepdims=True)


def front_kernel(ins, outs, weight_ref, semaphores, *, head):
    tokens_in, norm_in, all_weights = ins
    weights = [Fetch(all_weights.at[i], weight_ref.at[i], semaphores.at[i]) for i in range(3)]
    query_out, key_out, value_out, left_out = outs
    scale = head**-0.5
    inputs = tokens_in.get().astype(WIDE)
    norm_ref = norm_in.ref()
    rows, width = inputs.shape
    unit, _ = normalize(inputs)
    low = (unit * norm_ref[0:1, :] + norm_ref[1:2, :]).astype(LOW)
    left_out.ref[0:rows, :] = low
    for which, put in enumerate((query_out, key_out, value_out)):
        put.set(nn(low, weights[which].get()))
    group = 128 // head
    lane = iota((1, 128), 1) // head
    for at in range(0, width, 128):
        query, key, value = (p.ref[:, at : at + 128] for p in (query_out, key_out, value_out))
        total = jnp.zeros(query.shape, WIDE)
        for h in range(group):
            mine = lane == h
            probs = head_probs(jnp.where(mine, query, jnp.zeros_like(query)), key, scale)
            total = jnp.where(mine, nn(probs.astype(LOW), value), total)
        left_out.ref[rows:, at : at + 128] = total.astype(LOW)


def residual_kernel(flags_ref, capacity_ref, ins, outs, weight_ref, semaphores, *, cap):
    left_in, tokens_in, norm_in, meta_in, far_packed_in, all_weights = ins
    weight_in = Fetch(all_weights.at[3], weight_ref, semaphores.at[0])
    second_out, residual_out, far_meta_out, left_out, *sends = outs
    rows, width = tokens_in.held.shape
    slots = len(sends) * cap
    norm_ref = norm_in.ref()
    residual = tokens_in.get().astype(WIDE) + nn(left_in.ref()[rows:, :], weight_in.get())
    residual_out.set(residual)
    unit, _ = normalize(residual)
    second = (unit * norm_ref[2:3, :] + norm_ref[3:4, :]).astype(LOW)
    second_out.set(second)
    packed = far_packed_in.ref()
    far_meta = routed(*unpack(packed[rows:, 0:rows]), capacity_ref, flags_ref[2], cap)
    far_meta_out.set(far_meta)
    left_out.set(left_in.get())
    own = nn(chosen_slots(meta_in.get(), slots), second).astype(LOW)
    put_slots(sends, [gated_rows(far_meta, packed[0:rows, :], slots), own], cap)


class Loads:
    def __init__(self, in_sem, out_sem):
        self.in_sem, self.out_sem, self.loads, self.puts = in_sem, out_sem, [], []

    def load(self, source, target):
        self.loads.append(Fetch(source, target, self.in_sem.at[len(self.loads)]))
        return self.loads[-1]

    def put(self, source, target):
        self.puts.append(pltpu.make_async_copy(source, target, self.out_sem.at[len(self.puts)]))
        self.puts[-1].start()

    def finish(self):
        for copy in self.puts:
            copy.wait()


def slot_loads(moves, own, far, target, cap):
    for r in range(len(own)):
        for at, (piece, first) in enumerate((own[r], far[r])):
            moves.load(piece.at[pl.ds(first, cap)], target.at[pl.ds((2 * r + at) * cap, cap)])


def weight_loads(moves, weights, held, cut, parts):
    width = held.shape[1]
    return [
        moves.load(weights.at[pl.ds(pl.multiple_of((cut ^ r) * width, width), width)], held.at[r]) for r in parts
    ]


def forward_kernel(flags_ref, *refs, parts, count, cap, step):
    middle, last, weights = refs[:count], refs[count : 2 * count], refs[2 * count]
    refs = refs[2 * count + 1 :]
    rows_out, act_outs, slope_outs = refs[0], refs[1 : 1 + parts], refs[1 + parts : 1 + 2 * parts]
    rows_ref, act_ref, slope_ref, weight_ref, in_sem, out_sem = refs[1 + 2 * parts :]
    moves = Loads(in_sem, out_sem)
    slot_loads(moves, [(p, cap) for p in middle], [(p, 0) for p in last], rows_ref, cap)
    first = list(moves.loads)
    ups = weight_loads(moves, weights, weight_ref, flags_ref[3], range(parts))
    for fetch in first:
        fetch.ref()
    moves.put(rows_ref, rows_out)
    for r in range(parts):
        up = ups[r].ref()
        for b in range(2 * cap * count // step):
            here = pl.ds(b * step, step)
            hidden = nn(rows_ref[here, :], up[...])
            square = hidden * hidden
            bend = jnp.tanh(hidden * (GELU_SCALE + GELU_SCALE * GELU_CUBIC * square))
            half = 0.5 + 0.5 * bend
            curve = GELU_SCALE + 3.0 * GELU_SCALE * GELU_CUBIC * square
            act_ref[r, here, :] = (hidden * half).astype(LOW)
            slope_ref[r, here, :] = (half + 0.5 * hidden * (1.0 - bend * bend) * curve).astype(LOW)
        moves.put(act_ref.at[r], act_outs[r])
        moves.put(slope_ref.at[r], slope_outs[r])
    moves.finish()


def backward_kernel(flags_ref, *refs, parts, count, cap, step):
    first, middle, slopes = refs[:count], refs[count : 2 * count], refs[2 * count : 2 * count + parts]
    up_weights, down_weights = refs[2 * count + parts : 2 * count + parts + 2]
    refs = refs[2 * count + parts + 2 :]
    grads_out, hid_outs = refs[0], refs[1 : 1 + parts]
    back_own, back_far = refs[1 + parts : 1 + parts + count], refs[1 + parts + count : 1 + parts + 2 * count]
    grads_ref, slope_ref, hid_ref, back_ref, up_ref, down_ref, total_ref, in_sem, out_sem = refs[1 + parts + 2 * count :]
    moves = Loads(in_sem, out_sem)
    slot_loads(moves, [(p, 0) for p in first], [(p, 0) for p in middle], grads_ref, cap)
    slots = list(moves.loads)
    downs, curves, ups = [], [], []
    for r in range(parts):
        downs += weight_loads(moves, down_weights, down_ref, flags_ref[3], [r])
        curves.append(moves.load(slopes[r], slope_ref.at[r]))
        ups += weight_loads(moves, up_weights, up_ref, flags_ref[3], [r])
    for fetch in slots:
        fetch.ref()
    moves.put(grads_ref, grads_out)
    blocks = 2 * cap * count // step
    for r in range(parts):
        down, curve, up = downs[r].ref(), curves[r].ref(), ups[r].ref()
        for b in range(blocks):
            here = pl.ds(b * step, step)
            grad = nt(grads_ref[here, :], down[...])
            hid = (grad * curve[here, :].astype(WIDE)).astype(LOW)
            hid_ref[r, here, :] = hid
            more = nt(hid, up[...])
            if r > 0:
                more = more + total_ref[here, :]
            if r < parts - 1:
                total_ref[here, :] = more
                continue
            back_ref[here, :] = more.astype(LOW)
            for at in range(b * step, (b + 1) * step, 2 * cap):
                own = at // (2 * cap)
                moves.put(back_ref.at[pl.ds(at, cap), :], back_own[own])
                moves.put(back_ref.at[pl.ds(at + cap, cap), :], back_far[own])
        moves.put(hid_ref.at[r], hid_outs[r])
    moves.finish()


def other_halves(came, which, held, semaphores):
    size = held.shape[1]
    return [
        Fetch(came.at[pl.ds((2 * which + i) * size, size)], held.at[i], semaphores.at[i]) for i in range(2)
    ]


def odd_weight_kernel(ins, outs):
    rows, grads, *wides = ins
    for i in range(len(wides) // 2):
        hid, act = wides[2 * i : 2 * i + 2]
        outs[2 * i].set(tn(rows.get(), hid.get()))
        outs[2 * i + 1].set(tn(act.get(), grads.get()))


def far_weight_kernel(ins, outs, other_ref, semaphores):
    rows, hid, grads, act, came = ins
    up_other, down_other = other_halves(came, 0, other_ref, semaphores)
    outs[0].set(tn(rows.get(), hid.get()) + up_other.get().astype(WIDE))
    outs[1].set(tn(act.get(), grads.get()) + down_other.get().astype(WIDE))


def own_weight_kernel(flags_ref, ins, outs, other_ref, semaphores):
    rows, hid, grads, act, came, *momenta = ins
    others = other_halves(came, 1, other_ref, semaphores)
    frozen = flags_ref[0] > 0
    for left, right, put, at in ((rows, hid, outs[0], 0), (act, grads, outs[1], 1)):
        total = tn(left.get(), right.get()) + others[at].get().astype(WIDE)
        old = momenta[at].get()
        put.set(jnp.where(frozen, old, MOMENT_KEEP * old + total))


def out_kernel(flags_ref, *refs, parts, count, cap, step, extra):
    acts, weights, outs = refs[:parts], refs[parts], refs[parts + 1 + extra : parts + 1 + extra + count]
    act_ref, weight_ref, total_ref, in_sem, out_sem = refs[parts + 1 + extra + count :]
    width = weight_ref.shape[2]
    loads = []
    for r in range(parts):
        start = pl.multiple_of((flags_ref[3] ^ r) * width, width)
        loads.append(
            (
                Fetch(acts[r], act_ref.at[r], in_sem.at[2 * r]),
                Fetch(weights.at[pl.ds(start, width)], weight_ref.at[r], in_sem.at[2 * r + 1]),
            )
        )
    puts = []
    for b in range(2 * cap * count // step):
        here = slice(b * step, (b + 1) * step)
        total = None
        for act, down in loads:
            more = nn(act.ref()[here, :], down.ref()[...])
            total = more if total is None else total + more
        total_ref[here, :] = total.astype(LOW)
        for at in range(b * step, (b + 1) * step, 2 * cap):
            r = at // (2 * cap)
            puts.append(pltpu.make_async_copy(total_ref.at[pl.ds(at, 2 * cap)], outs[r], out_sem.at[r]))
            puts[-1].start()
    for copy in puts:
        copy.wait()


def gather_kernel(ins, outs, *, gated, cap, part):
    meta_in, *pieces = ins
    pieces = jnp.concatenate([p.ref()[part * cap : (part + 1) * cap, :] for p in pieces], axis=0)
    outs[0].set(collect(meta_in.get(), pieces, gated))


def mix_kernel(ins, outs, *, cap):
    meta_in, residual_in, came_in, *pieces = ins
    pieces = jnp.concatenate([p.ref()[:cap, :] for p in pieces], axis=0)
    total = collect(meta_in.get(), pieces, True) + came_in.get().astype(WIDE)
    outs[0].set(residual_in.get() + total)


def norm_backward(grad, unit, inverse, gain):
    scaled = grad * gain
    mean = jnp.mean(scaled, axis=-1, keepdims=True)
    along = jnp.mean(scaled * unit, axis=-1, keepdims=True)
    return inverse * (scaled - mean - unit * along)


def back_kernel(flags_ref, ins, outs, right_ref, weight_ref, small_ref, semaphores, *, head, parts):
    meta_in, came_in, *rest = ins
    pieces, (residual_in, cotangent_in, norm_in, all_weights, *smalls) = rest[:-8], rest[-8:]
    weights = [None] * 4
    weights[3] = Fetch(all_weights.at[3], weight_ref.at[3], semaphores.at[3])
    smalls = [Fetch(s, small_ref.at[i], semaphores.at[4 + i]) for i, s in enumerate(smalls)]
    query_in, key_in, value_in, tokens_in = smalls
    for i in range(3):
        weights[i] = Fetch(all_weights.at[i], weight_ref.at[i], semaphores.at[i])
    input_out, *rights = outs
    scale = head**-0.5
    pieces = jnp.concatenate([p.get() for p in pieces], axis=0)
    grad = collect(meta_in.get(), pieces, False) + came_in.get().astype(WIDE)
    unit, inverse = normalize(residual_in.get())
    norm_ref = norm_in.ref()
    rows, width = unit.shape
    second = [jnp.sum(grad * unit, axis=0, keepdims=True), jnp.sum(grad, axis=0, keepdims=True)]
    through = cotangent_in.get().astype(WIDE) + norm_backward(grad, unit, inverse, norm_ref[2:3, :])
    branch = through.astype(LOW)
    right_ref[3] = branch
    grad_heads = nt(branch, weights[3].get()).astype(LOW)
    group = 128 // head
    lane = iota((1, 128), 1) // head
    held = [r.ref() for r in (query_in, key_in, value_in)]
    for at in range(0, width, 128):
        query, key, value = (r[:, at : at + 128] for r in held)
        grad_out = grad_heads[:, at : at + 128]
        none = jnp.zeros_like(query)
        totals = [jnp.zeros(query.shape, WIDE) for _ in range(3)]
        for h in range(group):
            mine = lane == h
            probs = head_probs(jnp.where(mine, query, none), key, scale)
            dprob = nt(jnp.where(mine, grad_out, none), value)
            centre = jnp.sum(probs * dprob, axis=-1, keepdims=True)
            dscore = (probs * (dprob - centre)).astype(LOW)
            news = (
                nn(dscore, key) * scale,
                tn(dscore, query) * scale,
                tn(probs.astype(LOW), grad_out),
            )
            totals = [jnp.where(mine, p, t) for p, t in zip(news, totals)]
        for which in range(3):
            right_ref[which, :, at : at + 128] = totals[which].astype(LOW)
    grad = nt(right_ref[0], weights[0].get())
    grad = grad + nt(right_ref[1], weights[1].get())
    grad = grad + nt(right_ref[2], weights[2].get())
    unit, inverse = normalize(tokens_in.get().astype(WIDE))
    first = [jnp.sum(grad * unit, axis=0, keepdims=True), jnp.sum(grad, axis=0, keepdims=True)]
    sums = jnp.concatenate([*first, *second, jnp.zeros((SPARE - 4, width), WIDE)], axis=0).astype(LOW)
    for r, put in enumerate(rights):
        put.ref[0:rows, :] = right_ref[flags_ref[3] ^ r]
        put.ref[rows:, :] = sums
        put.send()
    input_out.set(through + norm_backward(grad, unit, inverse, norm_ref[0:1, :]))


def products_kernel(flags_ref, lefts, *refs, parts, extra):
    rights, refs = refs[:parts], refs[parts + extra :]
    outs, (left_ref, right_ref, out_ref, sums_ref, in_sem, out_sem) = refs[:3], refs[3:]
    rows = left_ref.shape[1]
    moves = Loads(in_sem, out_sem)
    mine = (flags_ref[3] == parts - 1).astype(jnp.int32) * rows
    loads = []
    for r in range(parts):
        start = pl.multiple_of((flags_ref[3] ^ r) * (2 * rows) + mine, rows)
        loads.append((moves.load(lefts.at[pl.ds(start, rows)], left_ref.at[r]), moves.load(rights[r], right_ref.at[r])))
    total = None
    for left, right in loads:
        more = tn(left.ref()[...], right.ref()[0:rows, :])
        total = more if total is None else total + more
    out_ref[...] = total.astype(LOW)
    half = out_ref.shape[0] // 2
    moves.put(out_ref.at[pl.ds(0, half)], outs[0])
    moves.put(out_ref.at[pl.ds(half, half)], outs[1])
    sums = [right_ref[r, rows:, :].astype(WIDE) for r in range(parts)]
    while len(sums) > 1:
        sums = [a + b for a, b in zip(sums[::2], sums[1::2])]
    sums_ref[...] = sums[0]
    moves.put(sums_ref, outs[2])
    moves.finish()


BLOCK = 256


def packed_width(width):
    return sum(width - at for at in range(0, width, BLOCK))


def moments_kernel(flags_ref, ins, outs):
    up_own, down_own, up_other, down_other = ins
    up_out, down_out, keep_out, send_out = outs
    frozen = flags_ref[0] > 0
    even = flags_ref[1] == 0
    lows = []
    for own, other, out in ((up_own, up_other, up_out), (down_own, down_other, down_out)):
        own = own.get()
        moment = jnp.where(frozen, own, own + other.get().astype(WIDE))
        out.set(moment)
        lows.append(moment.astype(LOW))
    up_low, down_low = lows
    width = up_low.shape[0]
    column = 0
    for at in range(0, width, BLOCK):
        up_gram = nt(up_low[at : at + BLOCK, :], up_low[at:, :])
        down_gram = tn(down_low[:, at : at + BLOCK], down_low[:, at:])
        here = slice(column, column + width - at)
        send_out.ref[:, here] = jnp.where(even, down_gram, up_gram)
        keep_out.ref[:, here] = jnp.where(even, up_gram, down_gram)
        column += width - at


class Square:
    SHAPES = (WIDE, LOW, LOW, LOW)

    def __init__(self, refs, lines):
        self.shifted, self.shifted_low, self.shifted_rest, self.factor_rest = refs
        self.shifted_line, self.factor_line = lines
        width = self.shifted.shape[0]
        self.strips = [slice(at, at + BLOCK) for at in range(0, width, BLOCK)]

    def diagonal(self, here, strip):
        same = iota(strip.shape, 0) + here.start == iota(strip.shape, 1)
        return same, jnp.sum(jnp.where(same, strip, 0.0), axis=1, keepdims=True)

    def take(self, here, gram):
        same, line = self.diagonal(here, gram)
        line = line - CENTRE
        strip = jnp.where(same, line, gram)
        self.shifted[here, :] = strip
        self.shifted_low[here, :] = strip.astype(LOW)
        self.shifted_rest[here, :] = jnp.where(same, 0.0, strip).astype(LOW)
        self.shifted_line[here, :] = jnp.broadcast_to(line, (BLOCK, 128))

    def square(self):
        for here in self.strips:
            product = nn(self.shifted_rest[here, :], self.shifted_low[...])
            strip = SCHULZ_QUARTIC * (self.shifted_line[here, 0:1] * self.shifted[here, :] + product)
            same, line = self.diagonal(here, strip)
            self.factor_rest[here, :] = jnp.where(same, 0.0, strip).astype(LOW)
            self.factor_line[here, :] = jnp.broadcast_to(line + REST, (BLOCK, 128))

    def times(self, here, strip, low):
        return self.factor_line[here, 0:1] * strip + nn(self.factor_rest[here, :], low)


def square_scratch(width):
    return [pltpu.VMEM((width, width), t) for t in Square.SHAPES] + [pltpu.VMEM((width, 128), WIDE)] * 2


def attn_step_kernel(ins, outs, now_ref, low_a, low_b, *refs):
    top, bottom, momentum, master = ins
    moment_out, new_out, low_out = outs
    square = Square(refs[:4], refs[4:])
    width = now_ref.shape[1]
    half = width // 2
    old = momentum.ref()
    moment_out.ref[0:half, :] = MOMENT_KEEP * old[0:half, :] + top.get().astype(WIDE)
    moment_out.ref[half:, :] = MOMENT_KEEP * old[half:, :] + bottom.get().astype(WIDE)
    moment_out.send()
    moment = moment_out.ref[...]
    now = moment * (1.0 / (jnp.sqrt(jnp.sum(moment * moment)) + 1e-07))
    now_ref[...] = now
    low_a[...] = now.astype(LOW)
    low, later = low_a, low_b
    for k in range(ITERS):
        for here in square.strips:
            square.take(here, nt(low[here, :], low[...]))
        square.square()
        for here in square.strips:
            strip = square.times(here, now_ref[here, :], low[...])
            if k < ITERS - 1:
                now_ref[here, :] = strip
                later[here, :] = strip.astype(LOW)
                continue
            new = master.ref()[here, :] * (1.0 - MUON_RATE * MUON_DECAY) - MUON_RATE * 0.2 * width**0.5 * strip
            new_out.ref[here, :] = new
            low_out.ref[here, :] = new.astype(LOW)
        low, later = later, low


def polar_kernel(ins, outs, gram_ref, gram_low, half_ref, half_low, product_ref, low_a, low_b, *refs):
    square = Square(refs[:4], refs[4:])
    mine_ref, other_ref = (i.ref() for i in ins)
    width = gram_ref.shape[0]
    column = 0
    for at in range(0, width, BLOCK):
        here = slice(column, column + width - at)
        strip = mine_ref[:, here] + other_ref[:, here]
        gram_ref[at : at + BLOCK, at:] = strip
        for far in range(BLOCK, width - at, BLOCK):
            gram_ref[at + far : at + far + BLOCK, at : at + BLOCK] = strip[:, far : far + BLOCK].T
        column += width - at
    total = 0.0
    for here in square.strips:
        total = total + jnp.sum(square.diagonal(here, gram_ref[here, :])[1])
    length = jnp.sqrt(total) + 1e-07

    def take(here, strip):
        gram_ref[here, :] = strip
        gram_low[here, :] = strip.astype(LOW)
        square.take(here, strip)

    for here in square.strips:
        take(here, gram_ref[here, :] * (1.0 / (length * length)))
    low, later = low_a, low_b
    for k in range(ITERS):
        square.square()
        for here in square.strips:
            if k == 0:
                same = iota((BLOCK, width), 0) + here.start == iota((BLOCK, width), 1)
                strip = jnp.where(same, square.factor_line[here, 0:1], square.factor_rest[here, :].astype(WIDE))
            else:
                strip = square.times(here, product_ref[here, :], low[...])
            if k < ITERS - 1:
                product_ref[here, :] = strip
                later[here, :] = strip.astype(LOW)
                half = square.times(here, gram_ref[here, :], gram_low[...])
                half_ref[here, :] = half
                half_low[here, :] = half.astype(LOW)
            else:
                outs[0].ref[here, :] = (strip * (1.0 / length)).astype(LOW)
        if k < ITERS - 1:
            for here in square.strips:
                take(here, square.times(here, half_ref[here, :], half_low[...]))
        low, later = later, low


def apply_kernel(flags_ref, ins, outs, *, wide_scale, strips):
    mine, came, up_moment, down_moment = ins[:4]
    up_masters, down_masters = ins[4 : 4 + strips], ins[4 + strips :]
    up_new, up_low, down_new, down_low = (outs[i * strips : (i + 1) * strips] for i in range(4))
    frozen = flags_ref[0] > 0
    even = flags_ref[1] == 0
    factors = mine.get(), came.get()
    up_factor = jnp.where(even, factors[0], factors[1])
    down_factor = jnp.where(even, factors[1], factors[0])

    def update(master, new_put, low_put, ortho):
        old = master.get()
        new = old * (1.0 - MUON_RATE * MUON_DECAY) - MUON_RATE * wide_scale * ortho
        new = jnp.where(frozen, old, new)
        new_put.set(new)
        low_put.set(new)

    up_matrix, down_matrix = up_moment.get().astype(LOW), down_moment.get().astype(LOW)
    size = up_factor.shape[0] // strips
    for i in range(strips):
        here = slice(i * size, (i + 1) * size)
        update(up_masters[i], up_new[i], up_low[i], nn(up_factor[here, :], up_matrix))
        update(down_masters[i], down_new[i], down_low[i], nn(down_matrix[here, :], down_factor))


def masks_of(axis):
    count = lax.axis_size(axis)
    return [1 << i for i in range(count.bit_length() - 1)]


def bit_of(axis, mask):
    return (lax.axis_index(axis) & mask) > 0


def add_low(left, right):
    return left.astype(LOW).astype(WIDE) + right.astype(LOW).astype(WIDE)


def sum_over(value, axis, masks, extra):
    def trade(part, mask, extra):
        if extra is None:
            return swap(part, axis, mask), None
        came = swap(jnp.concatenate([part, extra.astype(LOW)], axis=0), axis, mask)
        return came[: part.shape[0]], add_low(extra, came[part.shape[0] :])

    if len(masks) == 1:
        came, extra = trade(value, masks[0], extra)
        return add_low(value, came).astype(LOW), extra
    half = value.shape[0] // 2
    upper = bit_of(axis, masks[0])
    low, high = value[:half], value[half:]
    came, extra = trade(jnp.where(upper, low, high), masks[0], extra)
    mine = add_low(jnp.where(upper, high, low), came).astype(LOW)
    mine, extra = sum_over(mine, axis, masks[1:], extra)
    came = swap(mine, axis, masks[0])
    whole = jnp.concatenate([jnp.where(upper, came, mine), jnp.where(upper, mine, came)], axis=0)
    return whole, extra


def body(
    tokens,
    cotangent,
    expert_ids,
    gate_units,
    capacity,
    frozen,
    attn_copy,
    attn_master,
    attn_momentum,
    norm_params,
    norm_first,
    norm_second,
    up_copy,
    up_master,
    up_momentum,
    down_copy,
    down_master,
    down_momentum,
):
    rows, width = tokens.shape
    cuts = lax.axis_size("cuts")
    experts = capacity.shape[0]
    members = lax.axis_size("expert")
    cap = 4 * rows // members
    slots = experts * cap
    head = width // HEADS
    hidden = up_copy.shape[2]
    cut = lax.axis_index("cuts")
    me = lax.axis_index("expert")
    count = members // 2
    flags = jnp.stack([frozen[0], cut & 1, me, cut])
    small = shape_of((rows, width), LOW)
    square = shape_of((width, width), WIDE)
    square_low = shape_of((width, width), LOW)

    def cross(value):
        return swap(value, "expert", count)

    def spread(values):
        return [values[0]] + [swap(values[r], "expert", r) for r in range(1, count)]

    ups = lax.all_gather(up_copy[0], "cuts", tiled=True)
    downs = lax.all_gather(down_copy[0], "cuts", tiled=True)
    meta_shape = shape_of((8, rows), WIDE)
    piece = shape_of((cap, width), LOW)
    pair = shape_of((2 * cap, width), LOW)
    meta, packed, *sends = staged_call(
        functools.partial(pack_kernel, cap=cap),
        [expert_ids.T, gate_units.T, cotangent],
        [meta_shape, shape_of((rows + SPARE, width), LOW)] + [piece] * count,
        1,
        smem=[flags, capacity],
    )
    far_packed = cross(packed)
    first = spread(sends)
    query, key, value, left = staged_call(
        functools.partial(front_kernel, head=head),
        [tokens, norm_params, (attn_copy, 0)],
        [small] * 3 + [shape_of((2 * rows, width), LOW)],
        1,
        scratch=[pltpu.VMEM((3, width, width), LOW), pltpu.SemaphoreType.DMA((3,))],
        after=[packed],
    )
    normed_two, residual, far_meta, left, *sends = staged_call(
        functools.partial(residual_kernel, cap=cap),
        [left, tokens, norm_params, meta, far_packed, (attn_copy, 0)],
        [small, shape_of((rows, width), WIDE), meta_shape, shape_of((2 * rows, width), LOW)]
        + [pair] * count,
        1,
        scratch=[pltpu.VMEM((width, width), LOW), pltpu.SemaphoreType.DMA((1,))],
        after=first[1:],
        smem=[flags, capacity],
    )
    far_normed = cross(normed_two)
    lefts = lax.all_gather(left, "cuts", tiled=True)
    middle = spread(sends)
    last = spread(
        staged_call(functools.partial(far_kernel, cap=cap), [far_meta, far_normed], [piece] * count, 1)
    )

    step = 256
    wide = shape_of((slots, hidden), LOW)
    slot_shape = shape_of((slots, width), LOW)
    anywhere = pl.BlockSpec(memory_space=pltpu.HBM)
    scalars = pl.BlockSpec(memory_space=pltpu.SMEM)
    all_slots = pltpu.VMEM((slots, width), LOW)
    all_wide = pltpu.VMEM((cuts, slots, hidden), LOW)
    all_weights = pltpu.VMEM((cuts, width, hidden), LOW)

    def placed_call(kernel, outs, args, held, loads, puts, flops, moved):
        return pl.pallas_call(
            kernel,
            out_shape=outs,
            in_specs=[scalars] + [anywhere] * len(args),
            out_specs=[anywhere] * len(outs),
            scratch_shapes=[*held, pltpu.SemaphoreType.DMA((loads,)), pltpu.SemaphoreType.DMA((puts,))],
            compiler_params=pltpu.CompilerParams(vmem_limit_bytes=VMEM_BYTES),
            cost_estimate=pl.CostEstimate(flops=1, bytes_accessed=1, transcendentals=0),
        )(flags, *args)

    one = 2 * slots * width * hidden * cuts
    sizes = dict(parts=cuts, count=count, cap=cap, step=step)
    slot_rows, *outs = placed_call(
        functools.partial(forward_kernel, **sizes),
        [slot_shape] + [wide] * (2 * cuts),
        [*middle, *last, ups],
        [all_slots, all_wide, all_wide, all_weights],
        cuts + 2 * count,
        1 + 2 * cuts,
        one,
        20,
    )
    acts, slopes = outs[:cuts], outs[cuts:]
    slot_grads, *outs = placed_call(
        functools.partial(backward_kernel, **sizes),
        [slot_shape] + [wide] * cuts + [piece] * (2 * count),
        [*first, *middle, *slopes, ups, downs],
        [all_slots, all_wide, all_wide, all_slots, all_weights, all_weights, pltpu.VMEM((slots, width), WIDE)],
        3 * cuts + 2 * count,
        1 + cuts + 2 * count,
        2 * one,
        26,
    )
    hids, back_own, back_far = outs[:cuts], outs[cuts : cuts + count], outs[cuts + count :]
    back_far = spread(back_far)

    pair_shape = shape_of((2 * width, hidden), LOW)
    odd = staged_call(
        odd_weight_kernel,
        [slot_rows, slot_grads, hids[3], acts[3], hids[1], acts[1]],
        [(shape_of((4 * width, hidden), LOW), 4)],
        1,
    )[0]
    odd_came = swap(odd, "cuts", 1)

    def gather(meta_of, pieces, gated, part, after=()):
        (total,) = staged_call(
            functools.partial(gather_kernel, gated=gated, cap=cap, part=part),
            [meta_of, *pieces],
            [small],
            2 * rows * width * cap * count,
            after=after,
        )
        return total

    gathered = gather(far_meta, back_far, False, 0, after=[odd, lefts])
    came = cross(gathered)
    back_own = spread(back_own)
    other_scratch = [pltpu.VMEM((2, width, hidden), LOW), pltpu.SemaphoreType.DMA((2,))]
    (second,) = staged_call(
        far_weight_kernel,
        [slot_rows, hids[2], slot_grads, acts[2], (odd_came, 0)],
        [(pair_shape, 2)],
        1,
        scratch=other_scratch,
        after=[gathered],
    )
    second_came = swap(second, "cuts", 2)
    pieces = placed_call(
        functools.partial(out_kernel, extra=1, **sizes),
        [pair] * count,
        [*acts, downs, second],
        [all_wide, all_weights, all_slots],
        2 * cuts,
        count,
        one,
        13,
    )
    own_shape = shape_of((2 * width, hidden), WIDE)
    (zeroth,) = staged_call(
        own_weight_kernel,
        [slot_rows, hids[0], slot_grads, acts[0], (odd_came, 0), up_momentum[0], down_momentum[0]],
        [(own_shape, 2)],
        1,
        scratch=other_scratch,
        smem=[flags],
    )
    input_grad, *rights = staged_call(
        functools.partial(back_kernel, head=head, parts=cuts),
        [meta, came, *back_own, residual, cotangent, norm_params]
        + [(a, 0) for a in (attn_copy, query, key, value, tokens)],
        [shape_of((rows, width), WIDE)] + [shape_of((rows + SPARE, width), LOW)] * cuts,
        2 * rows * width * (4 * width + 10 * rows + slots),
        scratch=[
            pltpu.VMEM((4, rows, width), LOW),
            pltpu.VMEM((4, width, width), LOW),
            pltpu.VMEM((4, rows, width), LOW),
            pltpu.SemaphoreType.DMA((8,)),
        ],
        smem=[flags],
        after=[pieces[0]],
    )
    rights_came = [rights[0]] + [swap(rights[r], "cuts", r) for r in range(1, cuts)]

    strips = shape_of((BLOCK, packed_width(width)), WIDE)
    up_moment, down_moment, keep, send = staged_call(
        moments_kernel,
        [(zeroth, 2), (second_came, 2)],
        [square, square, strips, strips],
        4 * width**3,
        smem=[flags],
    )
    half = shape_of((width // 2, width), LOW)
    top, bottom, norm_sums = placed_call(
        functools.partial(products_kernel, parts=cuts, extra=1),
        [half, half, shape_of((SPARE, width), WIDE)],
        [lefts, *rights_came, keep],
        [
            pltpu.VMEM((cuts, rows, width), LOW),
            pltpu.VMEM((cuts, rows + SPARE, width), LOW),
            pltpu.VMEM((width, width), LOW),
            pltpu.VMEM((SPARE, width), WIDE),
        ],
        2 * cuts,
        3,
        2 * cuts * rows * width * width,
        5,
    )
    masks = masks_of("expert")
    top, norm_sums = sum_over(top, "expert", masks, norm_sums)
    bottom, _ = sum_over(bottom, "expert", [masks[1], masks[0], *masks[2:]], None)
    norm_total = norm_sums[:4]

    keep = keep + swap(send, "cuts", 1)
    other = swap(keep, "cuts", 2)
    attn_moment, attn_new, attn_low = staged_call(
        attn_step_kernel,
        [top, bottom, attn_momentum[0], attn_master[0]],
        [square, square, square_low],
        15 * 2 * width**3,
        scratch=[*[pltpu.VMEM((width, width), t) for t in (WIDE, LOW, LOW)], *square_scratch(width)],
    )
    pieces = spread(pieces)
    gathered_out = gather(far_meta, pieces, True, 1, after=[attn_low])
    came_out = cross(gathered_out)
    (factor,) = staged_call(
        polar_kernel,
        [keep, other],
        [square_low],
        17 * 2 * width**3,
        scratch=[
            *[pltpu.VMEM((width, width), t) for t in (WIDE, LOW, WIDE, LOW, WIDE, LOW, LOW)],
            *square_scratch(width),
        ],
        after=[gathered_out],
    )
    (output,) = staged_call(
        functools.partial(mix_kernel, cap=cap),
        [meta, residual, came_out, *pieces],
        [small],
        4 * rows * slots * width,
        after=[factor],
    )

    thirds = width // BLOCK
    up_new, up_low, down_new, down_low = staged_call(
        functools.partial(apply_kernel, wide_scale=0.2 * max(width, FF) ** 0.5, strips=thirds),
        [factor, swap(factor, "cuts", 1), up_moment, down_moment, (up_master[0], thirds), (down_master[0], thirds)],
        [(square, thirds), (square_low, thirds)] * 2,
        4 * width**3,
        smem=[flags],
        after=[output],
    )
    first_new = FIRST_DECAY * norm_first + (1.0 - FIRST_DECAY) * norm_total
    second_new = SECOND_DECAY * norm_second + (1.0 - SECOND_DECAY) * norm_total * norm_total
    first_hat = first_new / (1.0 - FIRST_DECAY**STEP_COUNT)
    second_hat = second_new / (1.0 - SECOND_DECAY**STEP_COUNT)
    norm_new = norm_params - ADAM_RATE * (
        first_hat / (jnp.sqrt(second_hat) + ADAM_EPSILON) + ADAM_DECAY * norm_params
    )
    return (
        output,
        input_grad,
        attn_new[None],
        attn_moment[None],
        attn_low[None],
        up_new[None],
        up_moment[None],
        up_low[None],
        down_new[None],
        down_moment[None],
        down_low[None],
        norm_new,
        first_new,
        second_new,
    )


def solution(mesh):
    rows = P(("expert", "cuts"), None)
    attn = P("cuts", None, None)
    ups = P("expert", None, "cuts")
    downs = P("expert", "cuts", None)
    return jax.shard_map(
        body,
        mesh=mesh,
        in_specs=(rows, rows, rows, rows, P(), P("expert"), P(), attn, attn, P(), P(), P())
        + (ups, ups, ups, downs, downs, downs),
        out_specs=(rows, rows, attn, attn, attn, ups, ups, ups, downs, downs, downs, P(), P(), P()),
        check_vma=False,
    )
```

```python
import functools

import jax
import jax.numpy as jnp
from jax import lax
from jax.experimental import pallas as pl
from jax.experimental.pallas import tpu as pltpu
from jax.sharding import PartitionSpec as P

HEADS = 12
FF = 3072
ITERS = 5
STEP_COUNT = 10

NORM_EPSILON = 1e-05
SCHULZ_LINEAR = 3.4445
SCHULZ_SQUARE = -4.775
SCHULZ_QUARTIC = 2.0315
MUON_RATE = 0.2
MUON_DECAY = 0.01
MOMENT_KEEP = 0.5
ADAM_RATE = 0.5
FIRST_DECAY = 0.9
SECOND_DECAY = 0.999
ADAM_EPSILON = 1e-08
ADAM_DECAY = 0.01
GATE_UNIT = 4096.0

CENTRE = -SCHULZ_SQUARE / (2.0 * SCHULZ_QUARTIC)
REST = SCHULZ_LINEAR - SCHULZ_QUARTIC * CENTRE * CENTRE

GELU_SCALE = 0.7978845608028654
GELU_CUBIC = 0.044715

LOW = jnp.bfloat16
WIDE = jnp.float32
MIB = 1024 * 1024


def nn(left, right):
    return jnp.dot(left, right, preferred_element_type=WIDE)


def nt(left, right):
    return lax.dot_general(left, right, (((1,), (1,)), ((), ())), preferred_element_type=WIDE)


def tn(left, right):
    return lax.dot_general(left, right, (((0,), (0,)), ((), ())), preferred_element_type=WIDE)


def iota(shape, axis):
    return lax.broadcasted_iota(jnp.int32, shape, axis)


def shape_of(shape, dtype):
    return jax.ShapeDtypeStruct(shape, dtype)


VMEM_BYTES = 63 * MIB


def cost_of(microseconds):
    return pl.CostEstimate(flops=int(1 + microseconds * 1e9), bytes_accessed=1, transcendentals=0)


class Fetch:
    def __init__(self, source, held, semaphore):
        self.held, self.pending = held, pltpu.make_async_copy(source, held, semaphore)
        self.pending.start()

    def ref(self):
        if self.pending is not None:
            self.pending.wait()
            self.pending = None
        return self.held

    def get(self):
        return self.ref()[...]


class Put:
    def __init__(self, target, held, semaphore):
        self.ref, self.copy, self.started = held, pltpu.make_async_copy(held, target, semaphore), False

    def send(self):
        self.copy.start()
        self.started = True

    def set(self, value):
        self.ref[...] = value.astype(self.ref.dtype)
        self.send()

    def finish(self):
        if not self.started:
            self.send()
        self.copy.wait()


def views(ref, parts):
    if parts == 1:
        return [ref]
    size = ref.shape[0] // parts
    return [ref.at[pl.ds(i * size, size)] for i in range(parts)]


def staged_call(kernel, ins, outs, cost=0, smem=(), scratch=(), after=()):
    ins = [i if isinstance(i, tuple) else (i, 1) for i in ins]
    outs = [o if isinstance(o, tuple) else (o, 1) for o in outs]
    first, given, wanted, extra = len(smem), len(ins), len(outs), len(scratch)
    reads, writes = sum(n for _, n in ins), sum(n for _, n in outs)
    staged = sum(n > 0 for _, n in ins)

    def run(*refs):
        scalars, sources, refs = refs[:first], refs[first : first + given], refs[first + given + len(after) :]
        targets, work, refs = refs[:wanted], refs[wanted : wanted + extra], refs[wanted + extra :]
        held_in, held_out, (in_sem, out_sem) = refs[:staged], refs[staged : staged + wanted], refs[staged + wanted :]
        fetches, puts = [], []
        held_in, reads = list(held_in), 0
        for source, (_, n) in zip(sources, ins):
            if n == 0:
                fetches.append(source)
                continue
            for a, b in zip(views(source, n), views(held_in.pop(0), n)):
                fetches.append(Fetch(a, b, in_sem.at[reads]))
                reads += 1
        for target, held, (_, n) in zip(targets, held_out, outs):
            for a, b in zip(views(target, n), views(held, n)):
                puts.append(Put(a, b, out_sem.at[len(puts)]))
        kernel(*scalars, fetches, puts, *work)
        for put in puts:
            put.finish()

    shapes = [i for i, n in ins if n > 0] + [o for o, _ in outs]
    hbm = pl.BlockSpec(memory_space=pltpu.HBM)
    return pl.pallas_call(
        run,
        out_shape=[o for o, _ in outs],
        in_specs=[pl.BlockSpec(memory_space=pltpu.SMEM)] * first
        + [hbm] * given
        + [hbm] * len(after),
        out_specs=[hbm] * wanted,
        scratch_shapes=[
            *scratch,
            *[pltpu.VMEM(s.shape, s.dtype) for s in shapes],
            pltpu.SemaphoreType.DMA((max(reads, 1),)),
            pltpu.SemaphoreType.DMA((writes,)),
        ],
        compiler_params=pltpu.CompilerParams(vmem_limit_bytes=VMEM_BYTES),
        cost_estimate=cost_of(cost),
    )(*smem, *[i for i, _ in ins], *after)


def swap(value, axis, mask):
    count = lax.axis_size(axis)
    return lax.ppermute(value, axis, [(i, i ^ mask) for i in range(count)])


def turned(meta):
    return meta.T


def chosen_slots(meta, slots):
    rows = iota((slots, meta.shape[1]), 0).astype(WIDE)
    return ((rows == meta[0:1, :]) | (rows == meta[1:2, :])).astype(WIDE).astype(LOW)


def split_gates(gates):
    high = gates.astype(LOW)
    return high, (gates - high.astype(WIDE)).astype(LOW)


def gated_rows(meta, values, slots):
    rows = iota((slots, meta.shape[1]), 0).astype(WIDE)
    gates = jnp.where(rows == meta[0:1, :], meta[2:3, :], 0.0) + jnp.where(rows == meta[1:2, :], meta[3:4, :], 0.0)
    high, rest = split_gates(gates)
    return (nn(high, values) + nn(rest, values)).astype(LOW)


def collect(meta, pieces, gated):
    meta = turned(meta)
    lanes = iota((meta.shape[0], pieces.shape[0]), 1).astype(WIDE)
    first, second = lanes == meta[:, 0:1], lanes == meta[:, 1:2]
    if not gated:
        return nn((first | second).astype(WIDE).astype(LOW), pieces)
    high, rest = split_gates(jnp.where(first, meta[:, 2:3], 0.0) + jnp.where(second, meta[:, 3:4], 0.0))
    return nn(high, pieces) + nn(rest, pieces)


SMALL = 64.0
SPARE = 16


def routed(ids, units, capacity_ref, me, cap):
    rows = ids.shape[1]
    experts = capacity_ref.shape[0]
    numbers = iota((experts, rows), 0)
    hots = [numbers == ids[i : i + 1, :] for i in range(2)]
    later = (iota((rows, rows), 0) < iota((rows, rows), 1)).astype(WIDE).astype(LOW)
    counts = nn((hots[0] | hots[1]).astype(WIDE).astype(LOW), later)
    slots = []
    for i in range(2):
        name = ids[i : i + 1, :]
        placed = jnp.sum(jnp.where(hots[i], counts, 0.0), axis=0, keepdims=True)
        limit = jnp.zeros_like(name)
        for e in range(experts):
            limit = jnp.where(name == e, capacity_ref[e], limit)
        near = (name ^ me).astype(WIDE)
        slots.append(jnp.where(placed < limit.astype(WIDE), near * cap + placed, -1.0))
    empty = jnp.zeros((1, rows), WIDE)
    meta = jnp.concatenate([*slots, units[0:1, :] / GATE_UNIT, units[1:2, :] / GATE_UNIT] + [empty] * 4, axis=0)
    return meta


def pack_kernel(flags_ref, capacity_ref, ins, outs, *, cap):
    ids_in, units_in, cotangent_in, up_in, down_in = ins
    meta_out, packed_out, up_out, down_out, *sends = outs
    rows, width = cotangent_in.held.shape
    ids, units = ids_in.get(), units_in.get().astype(WIDE)
    high = jnp.floor(units * (1.0 / SMALL))
    empty = jnp.zeros((SPARE - 6, rows), WIDE)
    lines = jnp.concatenate([ids.astype(WIDE), high, units - high * SMALL, empty], axis=0)
    packed_out.ref[rows:, :] = jnp.zeros((SPARE, width), LOW)
    packed_out.ref[rows:, 0:rows] = lines.astype(LOW)
    packed_out.ref[0:rows, :] = cotangent_in.get()
    packed_out.send()
    up_out.set(up_in.get())
    down_out.set(down_in.get())
    meta = routed(ids, units, capacity_ref, flags_ref[2], cap)
    meta_out.set(meta)
    put_slots(sends, [gated_rows(meta, cotangent_in.get(), len(sends) * cap)], cap)


def stack_kernel(ins, outs):
    blocks = iter(outs)
    for fetch in ins:
        value = fetch.ref()
        for at in range(0, value.shape[0], BLOCK):
            next(blocks).set(value[at : at + BLOCK, :])


def unpack(lines):
    lines = lines.astype(WIDE)
    return lines[0:2, :].astype(jnp.int32), lines[2:4, :] * SMALL + lines[4:6, :]


def far_kernel(ins, outs, *, cap):
    meta_in, low_in = ins
    low = nn(chosen_slots(meta_in.get(), len(outs) * cap), low_in.get()).astype(LOW)
    put_slots(outs, [low], cap)


def put_slots(sends, parts, cap):
    for r, put in enumerate(sends):
        for at, part in enumerate(parts):
            put.ref[at * cap : (at + 1) * cap, :] = part[r * cap : (r + 1) * cap, :]
        put.send()


def normalize(values):
    centre = values - jnp.mean(values, axis=-1, keepdims=True)
    spread = jnp.mean(centre * centre, axis=-1, keepdims=True)
    inverse = lax.rsqrt(spread + NORM_EPSILON)
    return centre * inverse, inverse


def head_probs(query, key, scale):
    rows = query.shape[0]
    scores = nt(query, key) * scale
    scores = jnp.where(iota((rows, rows), 1) <= iota((rows, rows), 0), scores, -1e30)
    exps = jnp.exp(scores - jnp.max(scores, axis=-1, keepdims=True))
    return exps / jnp.sum(exps, axis=-1, keepdims=True)


def front_kernel(flags_ref, ins, outs, weight_ref, semaphores, *, head):
    tokens_in, norm_in, all_weights = ins
    weights = [Fetch(all_weights.at[i], weight_ref.at[i], semaphores.at[i]) for i in range(3)]
    query_out, key_out, value_out, left_out, *lefts = outs
    scale = head**-0.5
    inputs = tokens_in.get().astype(WIDE)
    norm_ref = norm_in.ref()
    rows, width = inputs.shape
    unit, _ = normalize(inputs)
    low = (unit * norm_ref[0:1, :] + norm_ref[1:2, :]).astype(LOW)
    left_out.ref[0:rows, :] = low
    for which, put in enumerate((query_out, key_out, value_out)):
        put.set(nn(low, weights[which].get()))
    group = 128 // head
    lane = iota((1, 128), 1) // head
    for at in range(0, width, 128):
        query, key, value = (p.ref[:, at : at + 128] for p in (query_out, key_out, value_out))
        total = jnp.zeros(query.shape, WIDE)
        for h in range(group):
            mine = lane == h
            probs = head_probs(jnp.where(mine, query, jnp.zeros_like(query)), key, scale)
            total = jnp.where(mine, nn(probs.astype(LOW), value), total)
        left_out.ref[rows:, at : at + 128] = total.astype(LOW)
    left_out.send()
    for r in range(4):
        last = ((flags_ref[3] ^ r) == 3).astype(jnp.int32) * rows
        here = max(r - 2, 0) * rows
        lefts[min(r, 2)].ref[here : here + rows, :] = left_out.ref[pl.ds(pl.multiple_of(last, rows), rows), :]


def residual_kernel(flags_ref, capacity_ref, ins, outs, weight_ref, semaphores, *, cap):
    left_in, tokens_in, norm_in, meta_in, far_packed_in, all_weights = ins
    weight_in = Fetch(all_weights.at[3], weight_ref, semaphores.at[0])
    second_out, residual_out, far_meta_out, *sends = outs
    rows, width = tokens_in.held.shape
    slots = len(sends) * cap
    norm_ref = norm_in.ref()
    residual = tokens_in.get().astype(WIDE) + nn(left_in.ref()[rows:, :], weight_in.get())
    residual_out.set(residual)
    unit, _ = normalize(residual)
    second = (unit * norm_ref[2:3, :] + norm_ref[3:4, :]).astype(LOW)
    second_out.set(second)
    packed = far_packed_in.ref()
    far_meta = routed(*unpack(packed[rows:, 0:rows]), capacity_ref, flags_ref[2], cap)
    far_meta_out.set(far_meta)
    own = nn(chosen_slots(meta_in.get(), slots), second).astype(LOW)
    put_slots(sends, [gated_rows(far_meta, packed[0:rows, :], slots), own], cap)


class Loads:
    def __init__(self, in_sem, out_sem):
        self.in_sem, self.out_sem, self.loads, self.puts = in_sem, out_sem, [], []

    def load(self, source, target):
        self.loads.append(Fetch(source, target, self.in_sem.at[len(self.loads)]))
        return self.loads[-1]

    def put(self, source, target):
        self.puts.append(pltpu.make_async_copy(source, target, self.out_sem.at[len(self.puts)]))
        self.puts[-1].start()

    def finish(self):
        for copy in self.puts:
            copy.wait()


def slot_loads(moves, own, far, target, cap):
    for r in range(len(own)):
        for at, (piece, start) in enumerate((own[r], far[r])):
            moves.load(piece.at[pl.ds(start, cap)], target.at[pl.ds((2 * r + at) * cap, cap)])


def expert_kernel(*refs, parts, count, cap, step, starts, extra):
    first, middle, last = (refs[i * count : (i + 1) * count] for i in range(3))
    weights, refs = refs[3 * count : 3 * count + parts], refs[3 * count + parts + extra :]
    rows_out, grads_out, act_outs, hid_outs = refs[0], refs[1], refs[2 : 2 + parts], refs[2 + parts : 2 + 2 * parts]
    refs = refs[2 + 2 * parts :]
    back_own, back_far = refs[:count], refs[count : 2 * count]
    rows_ref, grads_ref, act_ref, hid_ref, back_ref, weight_ref, total_ref, in_sem, out_sem = refs[2 * count :]
    width = rows_ref.shape[1]
    moves = Loads(in_sem, out_sem)
    slot_loads(moves, [(p, cap) for p in middle], [(p, 0) for p in last], rows_ref, cap)
    rows_loads = list(moves.loads)
    ups, downs = [], []

    def load_weights(r):
        ups.append(moves.load(weights[r].at[pl.ds(starts[r], width)], weight_ref.at[2 * r]))
        downs.append(moves.load(weights[r].at[pl.ds(starts[r] + width, width)], weight_ref.at[2 * r + 1]))

    load_weights(0)
    slot_loads(moves, [(p, 0) for p in first], [(p, 0) for p in middle], grads_ref, cap)
    grads_loads = moves.loads[len(rows_loads) + 2 :]
    for r in range(1, parts):
        load_weights(r)
    for fetch in rows_loads:
        fetch.ref()
    moves.put(rows_ref, rows_out)
    blocks = 2 * cap * count // step
    for r in range(parts):
        for b in range(blocks):
            here = pl.ds(b * step, step)
            hidden = nn(rows_ref[here, :], ups[r].ref()[...])
            if r == 0 and b == 0:
                for fetch in grads_loads:
                    fetch.ref()
                moves.put(grads_ref, grads_out)
            grad = nt(grads_ref[here, :], downs[r].ref()[...])
            inner = hidden * (GELU_SCALE + GELU_SCALE * GELU_CUBIC * (hidden * hidden))
            half = 0.5 + 0.5 * jnp.tanh(inner)
            act_ref[r, here, :] = (hidden * half).astype(LOW)
            bend = 6.0 * inner - (4.0 * GELU_SCALE) * hidden
            hid = (grad * (half + half * (1.0 - half) * bend)).astype(LOW)
            hid_ref[r, here, :] = hid
            more = nt(hid, ups[r].ref()[...])
            if r > 0:
                more = more + total_ref[here, :]
            if r < parts - 1:
                total_ref[here, :] = more
                continue
            back_ref[here, :] = more.astype(LOW)
            for at in range(b * step, (b + 1) * step, 2 * cap):
                own = at // (2 * cap)
                moves.put(back_ref.at[pl.ds(at, cap), :], back_own[own])
                moves.put(back_ref.at[pl.ds(at + cap, cap), :], back_far[own])
        moves.put(act_ref.at[r], act_outs[r])
        moves.put(hid_ref.at[r], hid_outs[r])
    moves.finish()


def other_halves(came, held, semaphores):
    size = held.shape[1]
    return [Fetch(came.at[pl.ds(i * size, size)], held.at[i], semaphores.at[i]) for i in range(2)]


def weights_kernel(ins, outs, *, products):
    blocks = iter(outs)
    for left, right in products:
        total = tn(ins[left].get(), ins[right].get())
        for at in range(0, total.shape[0], BLOCK):
            next(blocks).set(total[at : at + BLOCK, :])
    for put, fetch in zip(blocks, ins[4:]):
        put.set(fetch.ref()[put.ref.shape[0] :, :])


def far_weight_kernel(ins, outs, other_ref, semaphores):
    rows, hid, grads, act, came = ins
    up_other, down_other = other_halves(came, other_ref, semaphores)
    outs[0].set(tn(rows.get(), hid.get()) + up_other.get().astype(WIDE))
    outs[1].set(tn(act.get(), grads.get()) + down_other.get().astype(WIDE))


def own_weight_kernel(flags_ref, ins, outs, other_ref, semaphores):
    rows, hid, grads, act, came, *momenta = ins
    others = other_halves(came, other_ref, semaphores)
    frozen = flags_ref[0] > 0
    for left, right, put, at in ((rows, hid, outs[0], 0), (act, grads, outs[1], 1)):
        total = tn(left.get(), right.get()) + others[at].get().astype(WIDE)
        old = momenta[at].get()
        put.set(jnp.where(frozen, old, MOMENT_KEEP * old + total))


def out_kernel(*refs, parts, count, cap, step, starts, extra):
    acts, weights, outs = refs[:parts], refs[parts : 2 * parts], refs[2 * parts + extra : 2 * parts + extra + count]
    act_ref, weight_ref, total_ref, in_sem, out_sem = refs[2 * parts + extra + count :]
    width = weight_ref.shape[2]
    moves = Loads(in_sem, out_sem)
    loads = []
    for r in range(parts):
        act = moves.load(acts[r], act_ref.at[r])
        loads.append((act, moves.load(weights[r].at[pl.ds(starts[r] + width, width)], weight_ref.at[r])))
    for b in range(2 * cap * count // step):
        here = slice(b * step, (b + 1) * step)
        total = None
        for act, down in loads:
            more = nn(act.ref()[here, :], down.ref()[...])
            total = more if total is None else total + more
        total_ref[here, :] = total.astype(LOW)
        for at in range(b * step, (b + 1) * step, 2 * cap):
            moves.put(total_ref.at[pl.ds(at, 2 * cap)], outs[at // (2 * cap)])
    moves.finish()


def gather_kernel(ins, outs, *, gated, cap, part):
    meta_in, *pieces = ins
    pieces = jnp.concatenate([p.ref()[part * cap : (part + 1) * cap, :] for p in pieces], axis=0)
    outs[0].set(collect(meta_in.get(), pieces, gated))


def mix_kernel(ins, outs, *, cap):
    meta_in, residual_in, came_in, *pieces = ins
    pieces = jnp.concatenate([p.ref()[:cap, :] for p in pieces], axis=0)
    total = collect(meta_in.get(), pieces, True) + came_in.get().astype(WIDE)
    outs[0].set(residual_in.get() + total)


def norm_backward(grad, unit, inverse, gain):
    scaled = grad * gain
    mean = jnp.mean(scaled, axis=-1, keepdims=True)
    along = jnp.mean(scaled * unit, axis=-1, keepdims=True)
    return inverse * (scaled - mean - unit * along)


def back_kernel(flags_ref, ins, outs, right_ref, weight_ref, small_ref, semaphores, *, head, parts):
    meta_in, came_in, *rest = ins
    pieces, (residual_in, cotangent_in, norm_in, all_weights, *smalls) = rest[:-8], rest[-8:]
    weights = [None] * 4
    weights[3] = Fetch(all_weights.at[3], weight_ref.at[3], semaphores.at[3])
    smalls = [Fetch(s, small_ref.at[i], semaphores.at[4 + i]) for i, s in enumerate(smalls)]
    query_in, key_in, value_in, tokens_in = smalls
    for i in range(3):
        weights[i] = Fetch(all_weights.at[i], weight_ref.at[i], semaphores.at[i])
    input_out, *rights = outs
    scale = head**-0.5
    pieces = jnp.concatenate([p.get() for p in pieces], axis=0)
    grad = collect(meta_in.get(), pieces, False) + came_in.get().astype(WIDE)
    unit, inverse = normalize(residual_in.get())
    norm_ref = norm_in.ref()
    rows, width = unit.shape
    second = [jnp.sum(grad * unit, axis=0, keepdims=True), jnp.sum(grad, axis=0, keepdims=True)]
    through = cotangent_in.get().astype(WIDE) + norm_backward(grad, unit, inverse, norm_ref[2:3, :])
    branch = through.astype(LOW)
    right_ref[3] = branch
    grad_heads = nt(branch, weights[3].get()).astype(LOW)
    group = 128 // head
    lane = iota((1, 128), 1) // head
    held = [r.ref() for r in (query_in, key_in, value_in)]
    for at in range(0, width, 128):
        query, key, value = (r[:, at : at + 128] for r in held)
        grad_out = grad_heads[:, at : at + 128]
        none = jnp.zeros_like(query)
        totals = [jnp.zeros(query.shape, WIDE) for _ in range(3)]
        for h in range(group):
            mine = lane == h
            probs = head_probs(jnp.where(mine, query, none), key, scale)
            dprob = nt(jnp.where(mine, grad_out, none), value)
            centre = jnp.sum(probs * dprob, axis=-1, keepdims=True)
            dscore = (probs * (dprob - centre)).astype(LOW)
            news = (
                nn(dscore, key) * scale,
                tn(dscore, query) * scale,
                tn(probs.astype(LOW), grad_out),
            )
            totals = [jnp.where(mine, p, t) for p, t in zip(news, totals)]
        for which in range(3):
            right_ref[which, :, at : at + 128] = totals[which].astype(LOW)
    grad = nt(right_ref[0], weights[0].get())
    grad = grad + nt(right_ref[1], weights[1].get())
    grad = grad + nt(right_ref[2], weights[2].get())
    unit, inverse = normalize(tokens_in.get().astype(WIDE))
    first = [jnp.sum(grad * unit, axis=0, keepdims=True), jnp.sum(grad, axis=0, keepdims=True)]
    sums = jnp.concatenate([*first, *second, jnp.zeros((SPARE - 4, width), WIDE)], axis=0).astype(LOW)
    for r, put in enumerate(rights):
        put.ref[0:rows, :] = right_ref[flags_ref[3] ^ r]
        put.ref[rows:, :] = sums
        put.send()
    input_out.set(through + norm_backward(grad, unit, inverse, norm_ref[0:1, :]))


def products_kernel(flags_ref, ins, outs, left_ref, semaphores, *, starts, masks):
    parts = len(starts)
    rights, lefts = ins[:parts], ins[parts:]
    rows = left_ref.shape[1]
    lefts = [
        Fetch(left.at[pl.ds(start, rows)], left_ref.at[r], semaphores.at[r])
        for r, (left, start) in enumerate(zip(lefts, starts))
    ]
    total = None
    for left, right in zip(lefts, rights):
        more = tn(left.get(), right.ref()[0:rows, :])
        total = more if total is None else total + more
    sums = [right.ref()[rows:, :].astype(WIDE) for right in rights]
    while len(sums) > 1:
        sums = [a + b for a, b in zip(sums[::2], sums[1::2])]
    total, half = total.astype(LOW), total.shape[0] // 2
    divide(flags_ref[2], [total[:half], total[half:]], sums[0].astype(LOW), outs, masks)


def divide(me, totals, sums, outs, masks):
    for i, (total, mask) in enumerate(zip(totals, masks)):
        size = total.shape[0] // 2
        upper = (me & mask) > 0
        send = jnp.where(upper, total[:size], total[size:])
        keep = jnp.where(upper, total[size:], total[:size])
        for put, part in ((outs[2 * i], send), (outs[2 * i + 1], keep)):
            put.ref[0:size, :] = part
            if i == 0:
                put.ref[size:, :] = sums
            put.send()


def added(keep, came):
    return (keep.get().astype(WIDE) + came.get().astype(WIDE)).astype(LOW)


def divide_kernel(flags_ref, ins, outs, *, masks):
    totals = [added(*ins[0:2]), added(*ins[2:4])]
    size = totals[1].shape[0]
    divide(flags_ref[2], [totals[0][:size], totals[1]], totals[0][size:], outs, masks)


def whole_kernel(ins, outs):
    outs[0].set(jnp.concatenate([added(*ins[0:2]), added(*ins[2:4])], axis=0))


def add_kernel(ins, outs):
    outs[0].set(added(*ins))


def part_kernel(ins, outs):
    total = added(*ins)
    size = outs[0].ref.shape[0]
    outs[0].set(total[:size])
    outs[1].set(total[size + SPARE :])
    outs[2].set(total[size : size + SPARE])


def joined(me, mine, came, mask):
    upper = (me & mask) > 0
    mine, came = mine.get(), came.get()
    return jnp.concatenate([jnp.where(upper, came, mine), jnp.where(upper, mine, came)], axis=0)


def join_kernel(flags_ref, ins, outs, *, masks):
    for i, mask in enumerate(masks):
        outs[i].set(joined(flags_ref[2], *ins[2 * i : 2 * i + 2], mask))


BLOCK = 256


def packed_width(width):
    return sum(width - at for at in range(0, width, BLOCK))


def moments_kernel(flags_ref, ins, outs):
    up_own, down_own, up_other, down_other = ins
    up_out, down_out, keep_out, send_out = outs
    frozen = flags_ref[0] > 0
    even = flags_ref[1] == 0
    lows = []
    for own, other, out in ((up_own, up_other, up_out), (down_own, down_other, down_out)):
        own = own.get()
        moment = jnp.where(frozen, own, own + other.get().astype(WIDE))
        out.set(moment)
        lows.append(moment.astype(LOW))
    up_low, down_low = lows
    width = up_low.shape[0]
    column = 0
    for at in range(0, width, BLOCK):
        up_gram = nt(up_low[at : at + BLOCK, :], up_low[at:, :])
        down_gram = tn(down_low[:, at : at + BLOCK], down_low[:, at:])
        here = slice(column, column + width - at)
        send_out.ref[:, here] = jnp.where(even, down_gram, up_gram)
        keep_out.ref[:, here] = jnp.where(even, up_gram, down_gram)
        column += width - at


class Square:
    SHAPES = (WIDE, LOW, LOW, LOW)

    def __init__(self, refs, lines):
        self.shifted, self.shifted_low, self.shifted_rest, self.factor_rest = refs
        self.shifted_line, self.factor_line = lines
        width = self.shifted.shape[0]
        self.strips = [slice(at, at + BLOCK) for at in range(0, width, BLOCK)]

    def diagonal(self, here, strip):
        same = iota(strip.shape, 0) + here.start == iota(strip.shape, 1)
        return same, jnp.sum(jnp.where(same, strip, 0.0), axis=1, keepdims=True)

    def take(self, here, gram):
        same, line = self.diagonal(here, gram)
        line = line - CENTRE
        strip = jnp.where(same, line, gram)
        self.shifted[here, :] = strip
        self.shifted_low[here, :] = strip.astype(LOW)
        self.shifted_rest[here, :] = jnp.where(same, 0.0, strip).astype(LOW)
        self.shifted_line[here, :] = jnp.broadcast_to(line, (BLOCK, 128))

    def square(self):
        for here in self.strips:
            product = nn(self.shifted_rest[here, :], self.shifted_low[...])
            strip = SCHULZ_QUARTIC * (self.shifted_line[here, 0:1] * self.shifted[here, :] + product)
            same, line = self.diagonal(here, strip)
            self.factor_rest[here, :] = jnp.where(same, 0.0, strip).astype(LOW)
            self.factor_line[here, :] = jnp.broadcast_to(line + REST, (BLOCK, 128))

    def times(self, here, strip, low):
        return self.factor_line[here, 0:1] * strip + nn(self.factor_rest[here, :], low)


def square_scratch(width):
    return [pltpu.VMEM((width, width), t) for t in Square.SHAPES] + [pltpu.VMEM((width, 128), WIDE)] * 2


def attn_step_kernel(flags_ref, ins, outs, now_ref, low_a, low_b, *refs, masks):
    momentum, master = ins[4:]
    moment_out, new_out, low_out = outs
    square = Square(refs[:4], refs[4:])
    width = now_ref.shape[1]
    half = width // 2
    old = momentum.ref()
    for i, mask in enumerate(masks):
        here = slice(i * half, (i + 1) * half)
        grad = joined(flags_ref[2], *ins[2 * i : 2 * i + 2], mask)
        moment_out.ref[here, :] = MOMENT_KEEP * old[here, :] + grad.astype(WIDE)
    moment_out.send()
    moment = moment_out.ref[...]
    now = moment * (1.0 / (jnp.sqrt(jnp.sum(moment * moment)) + 1e-07))
    now_ref[...] = now
    low_a[...] = now.astype(LOW)
    low, later = low_a, low_b
    for k in range(ITERS):
        for here in square.strips:
            square.take(here, nt(low[here, :], low[...]))
        square.square()
        for here in square.strips:
            strip = square.times(here, now_ref[here, :], low[...])
            if k < ITERS - 1:
                now_ref[here, :] = strip
                later[here, :] = strip.astype(LOW)
                continue
            new = master.ref()[here, :] * (1.0 - MUON_RATE * MUON_DECAY) - MUON_RATE * 0.2 * width**0.5 * strip
            new_out.ref[here, :] = new
            low_out.ref[here, :] = new.astype(LOW)
        low, later = later, low


def gram_kernel(ins, outs):
    outs[0].set(ins[0].get() + ins[1].get())


def polar_kernel(ins, outs, gram_ref, gram_low, half_ref, half_low, product_ref, low_a, low_b, *refs):
    square = Square(refs[:4], refs[4:])
    mine_ref, other_ref = (i.ref() for i in ins)
    width = gram_ref.shape[0]
    column = 0
    for at in range(0, width, BLOCK):
        here = slice(column, column + width - at)
        strip = mine_ref[:, here] + other_ref[:, here]
        gram_ref[at : at + BLOCK, at:] = strip
        for far in range(BLOCK, width - at, BLOCK):
            gram_ref[at + far : at + far + BLOCK, at : at + BLOCK] = strip[:, far : far + BLOCK].T
        column += width - at
    total = 0.0
    for here in square.strips:
        total = total + jnp.sum(square.diagonal(here, gram_ref[here, :])[1])
    length = jnp.sqrt(total) + 1e-07

    def take(here, strip):
        gram_ref[here, :] = strip
        gram_low[here, :] = strip.astype(LOW)
        square.take(here, strip)

    for here in square.strips:
        take(here, gram_ref[here, :] * (1.0 / (length * length)))
    low, later = low_a, low_b
    for k in range(ITERS):
        square.square()
        for here in square.strips:
            if k == 0:
                same = iota((BLOCK, width), 0) + here.start == iota((BLOCK, width), 1)
                strip = jnp.where(same, square.factor_line[here, 0:1], square.factor_rest[here, :].astype(WIDE))
            else:
                strip = square.times(here, product_ref[here, :], low[...])
            if k < ITERS - 1:
                product_ref[here, :] = strip
                later[here, :] = strip.astype(LOW)
                half = square.times(here, gram_ref[here, :], gram_low[...])
                half_ref[here, :] = half
                half_low[here, :] = half.astype(LOW)
            else:
                product_ref[here, :] = strip * (1.0 / length)
        if k < ITERS - 1:
            for here in square.strips:
                take(here, square.times(here, half_ref[here, :], half_low[...]))
        low, later = later, low
    size = width // len(outs)
    for i, put in enumerate(outs):
        put.set(product_ref[i * size : (i + 1) * size, :])


def apply_kernel(flags_ref, ins, outs, *, wide_scale, strips):
    quarters, ins = ins[:8], ins[8:]
    up_moment, down_moment = ins[:2]
    up_masters, down_masters = ins[2 : 2 + strips], ins[2 + strips :]
    up_new, up_low, down_new, down_low = (outs[i * strips : (i + 1) * strips] for i in range(4))
    frozen = flags_ref[0] > 0
    even = flags_ref[1] == 0
    factors = [jnp.concatenate([q.get() for q in part], axis=0) for part in (quarters[:4], quarters[4:])]
    up_factor = jnp.where(even, factors[0], factors[1])
    down_factor = jnp.where(even, factors[1], factors[0])

    def update(master, new_put, low_put, ortho):
        old = master.get()
        new = old * (1.0 - MUON_RATE * MUON_DECAY) - MUON_RATE * wide_scale * ortho
        new = jnp.where(frozen, old, new)
        new_put.set(new)
        low_put.set(new)

    up_matrix, down_matrix = up_moment.get().astype(LOW), down_moment.get().astype(LOW)
    size = up_factor.shape[0] // strips
    for i in range(strips):
        here = slice(i * size, (i + 1) * size)
        update(up_masters[i], up_new[i], up_low[i], nn(up_factor[here, :], up_matrix))
        update(down_masters[i], down_new[i], down_low[i], nn(down_matrix[here, :], down_factor))


def masks_of(axis):
    count = lax.axis_size(axis)
    return [1 << i for i in range(count.bit_length() - 1)]


def body(
    tokens,
    cotangent,
    expert_ids,
    gate_units,
    capacity,
    frozen,
    attn_copy,
    attn_master,
    attn_momentum,
    norm_params,
    norm_first,
    norm_second,
    up_copy,
    up_master,
    up_momentum,
    down_copy,
    down_master,
    down_momentum,
):
    rows, width = tokens.shape
    cuts = lax.axis_size("cuts")
    experts = capacity.shape[0]
    members = lax.axis_size("expert")
    cap = 4 * rows // members
    slots = experts * cap
    head = width // HEADS
    hidden = up_copy.shape[2]
    cut = lax.axis_index("cuts")
    me = lax.axis_index("expert")
    count = members // 2
    flags = jnp.stack([frozen[0], cut & 1, me, cut])
    small = shape_of((rows, width), LOW)
    square = shape_of((width, width), WIDE)
    square_low = shape_of((width, width), LOW)

    def cross(value):
        return swap(value, "expert", count)

    def spread(values):
        return [values[0]] + [swap(values[r], "expert", r) for r in range(1, count)]

    pair_shape = shape_of((2 * width, hidden), LOW)
    meta_shape = shape_of((8, rows), WIDE)
    piece = shape_of((cap, width), LOW)
    pair = shape_of((2 * cap, width), LOW)
    meta, packed, weights, *sends = staged_call(
        functools.partial(pack_kernel, cap=cap),
        [expert_ids.T, gate_units.T, cotangent, up_copy[0], down_copy[0]],
        [meta_shape, shape_of((rows + SPARE, width), LOW), (pair_shape, 2)] + [piece] * count,
        smem=[flags, capacity],
    )
    far_packed = cross(packed)
    weights = {0: weights, 2: swap(weights, "cuts", 2)}
    first = spread(sends)
    query, key, value, both_lefts, left, core_left, far_lefts = staged_call(
        functools.partial(front_kernel, head=head),
        [tokens, norm_params, (attn_copy, 0)],
        [small] * 3 + [shape_of((2 * rows, width), LOW), small, small, shape_of((2 * rows, width), LOW)],
        scratch=[pltpu.VMEM((3, width, width), LOW), pltpu.SemaphoreType.DMA((3,))],
        smem=[flags],
        after=[packed],
    )
    normed_two, residual, far_meta, *sends = staged_call(
        functools.partial(residual_kernel, cap=cap),
        [both_lefts, tokens, norm_params, meta, far_packed, (attn_copy, 0)],
        [small, shape_of((rows, width), WIDE), meta_shape] + [pair] * count,
        scratch=[pltpu.VMEM((width, width), LOW), pltpu.SemaphoreType.DMA((1,))],
        after=first[1:],
        smem=[flags, capacity],
    )
    far_normed = cross(normed_two)
    middle = spread(sends)
    sends = staged_call(functools.partial(far_kernel, cap=cap), [far_meta, far_normed], [piece] * count)
    last = spread(sends)
    (both,) = staged_call(
        stack_kernel,
        [weights[0], weights[2], core_left],
        [(shape_of((4 * width + rows, hidden), LOW), (4 * width + rows) // BLOCK)],
        after=[sends[0], *middle[1:]],
    )
    both = swap(both, "cuts", 1)
    places = ((weights[0], 0), (both, 0), (weights[2], 0), (both, 2 * width))

    step = 256
    wide = shape_of((slots, hidden), LOW)
    slot_shape = shape_of((slots, width), LOW)
    anywhere = pl.BlockSpec(memory_space=pltpu.HBM)
    scalars = pl.BlockSpec(memory_space=pltpu.SMEM)
    all_slots = pltpu.VMEM((slots, width), LOW)
    all_wide = pltpu.VMEM((cuts, slots, hidden), LOW)
    all_weights = pltpu.VMEM((cuts, width, hidden), LOW)

    def placed_call(kernel, outs, args, held, loads, puts, cost=0):
        return pl.pallas_call(
            kernel,
            out_shape=outs,
            in_specs=[anywhere] * len(args),
            out_specs=[anywhere] * len(outs),
            scratch_shapes=[*held, pltpu.SemaphoreType.DMA((loads,)), pltpu.SemaphoreType.DMA((puts,))],
            compiler_params=pltpu.CompilerParams(vmem_limit_bytes=VMEM_BYTES),
            cost_estimate=cost_of(cost),
        )(*args)

    sizes = dict(parts=cuts, count=count, cap=cap, step=step, starts=[at for _, at in places])
    slot_rows, slot_grads, *outs = placed_call(
        functools.partial(expert_kernel, extra=0, **sizes),
        [slot_shape] * 2 + [wide] * (2 * cuts) + [piece] * (2 * count),
        [*first, *middle, *last, *[w for w, _ in places]],
        [
            *[all_slots, all_slots, all_wide, all_wide, all_slots],
            pltpu.VMEM((2 * cuts, width, hidden), LOW),
            pltpu.VMEM((slots, width), WIDE),
        ],
        2 * cuts + 4 * count,
        2 + 2 * cuts + 2 * count,
    )
    acts, hids = outs[:cuts], outs[cuts : 2 * cuts]
    back_own, back_far = outs[2 * cuts : 2 * cuts + count], outs[2 * cuts + count :]
    back_far = spread(back_far)

    strip_count = width // BLOCK

    def weight_grads(products, ins, after, extra=0, cost=0):
        size = len(products) * width + extra
        (total,) = staged_call(
            functools.partial(weights_kernel, products=products),
            ins,
            [(shape_of((size, hidden), LOW), size // BLOCK)],
            cost=cost,
            after=after,
        )
        return total

    far_lefts = swap(far_lefts, "cuts", 2)
    def gather(meta_of, pieces, gated, part, after=()):
        (total,) = staged_call(
            functools.partial(gather_kernel, gated=gated, cap=cap, part=part),
            [meta_of, *pieces],
            [small],
            after=after,
        )
        return total

    gathered = gather(far_meta, back_far, False, 0)
    came = cross(gathered)
    back_own = spread(back_own)
    third = weight_grads(
        [(0, 1), (2, 3)], [slot_rows, hids[3], acts[3], slot_grads], [gathered, far_lefts]
    )
    third_came = swap(third, "cuts", 1)
    odd = weight_grads(
        [(0, 1), (2, 3)], [slot_rows, hids[1], acts[1], slot_grads, far_lefts], [third], extra=rows, cost=60
    )
    odd_came = swap(odd, "cuts", 1)
    other_scratch = [pltpu.VMEM((2, width, hidden), LOW), pltpu.SemaphoreType.DMA((2,))]
    (second,) = staged_call(
        far_weight_kernel,
        [slot_rows, hids[2], slot_grads, acts[2], (third_came, 0)],
        [(pair_shape, 2)],
        scratch=other_scratch,
        after=[odd],
    )
    second_came = swap(second, "cuts", 2)
    input_grad, *rights = staged_call(
        functools.partial(back_kernel, head=head, parts=cuts),
        [meta, came, *back_own, residual, cotangent, norm_params]
        + [(a, 0) for a in (attn_copy, query, key, value, tokens)],
        [shape_of((rows, width), WIDE)] + [shape_of((rows + SPARE, width), LOW)] * cuts,
        scratch=[
            pltpu.VMEM((4, rows, width), LOW),
            pltpu.VMEM((4, width, width), LOW),
            pltpu.VMEM((4, rows, width), LOW),
            pltpu.SemaphoreType.DMA((8,)),
        ],
        smem=[flags],
        after=[second],
        cost=40,
    )
    rights_came = [rights[0]] + [swap(rights[r], "cuts", r) for r in range(1, cuts)]
    pieces = placed_call(
        functools.partial(out_kernel, extra=1, **sizes),
        [pair] * count,
        [*acts, *[w for w, _ in places], rights_came[1]],
        [all_wide, all_weights, all_slots],
        2 * cuts,
        count,
    )
    own_shape = shape_of((2 * width, hidden), WIDE)
    (zeroth,) = staged_call(
        own_weight_kernel,
        [slot_rows, hids[0], slot_grads, acts[0], (odd_came, 0), up_momentum[0], down_momentum[0]],
        [(own_shape, 2)],
        scratch=[pltpu.VMEM((2, width, hidden), LOW), pltpu.SemaphoreType.DMA((2,))],
        smem=[flags],
        after=[pieces[0]],
    )

    pieces = spread(pieces)
    gathered_out = gather(far_meta, pieces, True, 1, after=[zeroth])
    came_out = cross(gathered_out)
    strips = shape_of((BLOCK, packed_width(width)), WIDE)
    up_moment, down_moment, keep, send = staged_call(
        moments_kernel,
        [(zeroth, 2), (second_came, 2)],
        [square, square, strips, strips],
        smem=[flags],
        after=[gathered_out],
    )
    masks = masks_of("expert")
    order = (masks[0:2], [masks[1], masks[0]])

    def part_shape(share, extra):
        return shape_of((width // share + extra * SPARE, width), LOW)

    def trade(sends, step):
        return [swap(v, "expert", order[i][step]) for i, v in enumerate(sends)]

    send_a, keep_a, send_b, keep_b = staged_call(
        functools.partial(
            products_kernel, starts=(0, 4 * width, 0, 2 * width), masks=(order[0][0], order[1][0])
        ),
        [*rights_came, (left, 0), (both, 0), (far_lefts, 0), (odd_came, 0)],
        [part_shape(4, 1)] * 2 + [part_shape(4, 0)] * 2,
        scratch=[pltpu.VMEM((cuts, rows, width), LOW), pltpu.SemaphoreType.DMA((cuts,))],
        smem=[flags],
        cost=60,
    )
    (keep,) = staged_call(gram_kernel, [keep, swap(send, "cuts", 1)], [strips], after=[send_a])
    other = swap(keep, "cuts", 2)
    (output,) = staged_call(
        functools.partial(mix_kernel, cap=cap),
        [meta, residual, came_out, *pieces],
        [small],
        after=[send_a],
    )
    came_a, came_b = trade([send_a, send_b], 0)
    send_a, keep_a, send_b, keep_b = staged_call(
        functools.partial(divide_kernel, masks=(order[0][1], order[1][1])),
        [keep_a, came_a, keep_b, came_b],
        [part_shape(8, 1)] * 2 + [part_shape(8, 0)] * 2,
        smem=[flags],
        after=[output],
    )
    came_a, came_b = trade([send_a, send_b], 1)
    (total,) = staged_call(whole_kernel, [keep_a, came_a, keep_b, came_b], [part_shape(4, 1)])
    for mask in masks[2:-1]:
        (total,) = staged_call(add_kernel, [total, swap(total, "expert", mask)], [part_shape(4, 1)])
    came = swap(total, "expert", masks[-1])
    factor = staged_call(
        polar_kernel,
        [keep, other],
        [shape_of((width // 4, width), LOW)] * 4,
        scratch=[
            *[pltpu.VMEM((width, width), t) for t in (WIDE, LOW, WIDE, LOW, WIDE, LOW, LOW)],
            *square_scratch(width),
        ],
        after=[total],
    )
    part_a, part_b, norm_sums = staged_call(
        part_kernel,
        [total, came],
        [part_shape(8, 0)] * 2 + [shape_of((SPARE, width), LOW)],
        after=[factor[0]],
    )
    came_a, came_b = trade([part_a, part_b], 1)
    half_a, half_b = staged_call(
        functools.partial(join_kernel, masks=(order[0][1], order[1][1])),
        [part_a, came_a, part_b, came_b],
        [part_shape(4, 0)] * 2,
        smem=[flags],
    )
    came_a, came_b = trade([half_a, half_b], 0)
    norm_total = norm_sums[:4].astype(WIDE)
    attn_moment, attn_new, attn_low = staged_call(
        functools.partial(attn_step_kernel, masks=(order[0][0], order[1][0])),
        [half_a, came_a, half_b, came_b, attn_momentum[0], attn_master[0]],
        [square, square, square_low],
        scratch=[*[pltpu.VMEM((width, width), t) for t in (WIDE, LOW, LOW)], *square_scratch(width)],
        smem=[flags],
        cost=40,
    )
    thirds = width // BLOCK
    up_new, up_low, down_new, down_low = staged_call(
        functools.partial(apply_kernel, wide_scale=0.2 * max(width, FF) ** 0.5, strips=thirds),
        [*factor, *[swap(f, "cuts", 1) for f in factor], up_moment, down_moment, (up_master[0], thirds), (down_master[0], thirds)],
        [(square, thirds), (square_low, thirds)] * 2,
        smem=[flags],
    )
    first_new = FIRST_DECAY * norm_first + (1.0 - FIRST_DECAY) * norm_total
    second_new = SECOND_DECAY * norm_second + (1.0 - SECOND_DECAY) * norm_total * norm_total
    first_hat = first_new / (1.0 - FIRST_DECAY**STEP_COUNT)
    second_hat = second_new / (1.0 - SECOND_DECAY**STEP_COUNT)
    norm_new = norm_params - ADAM_RATE * (
        first_hat / (jnp.sqrt(second_hat) + ADAM_EPSILON) + ADAM_DECAY * norm_params
    )
    return (
        output,
        input_grad,
        attn_new[None],
        attn_moment[None],
        attn_low[None],
        up_new[None],
        up_moment[None],
        up_low[None],
        down_new[None],
        down_moment[None],
        down_low[None],
        norm_new,
        first_new,
        second_new,
    )


def solution(mesh):
    rows = P(("expert", "cuts"), None)
    attn = P("cuts", None, None)
    ups = P("expert", None, "cuts")
    downs = P("expert", "cuts", None)
    return jax.shard_map(
        body,
        mesh=mesh,
        in_specs=(rows, rows, rows, rows, P(), P("expert"), P(), attn, attn, P(), P(), P())
        + (ups, ups, ups, downs, downs, downs),
        out_specs=(rows, rows, attn, attn, attn, ups, ups, ups, downs, downs, downs, P(), P(), P()),
        check_vma=False,
    )
```

```python
import functools

import jax
import jax.numpy as jnp
from jax import lax
from jax.experimental import pallas as pl
from jax.experimental.pallas import tpu as pltpu
from jax.sharding import PartitionSpec as P

HEADS = 12
FF = 3072
ITERS = 5
STEP_COUNT = 10

NORM_EPSILON = 1e-05
SCHULZ_LINEAR = 3.4445
SCHULZ_SQUARE = -4.775
SCHULZ_QUARTIC = 2.0315
MUON_RATE = 0.2
MUON_DECAY = 0.01
MOMENT_KEEP = 0.5
ADAM_RATE = 0.5
FIRST_DECAY = 0.9
SECOND_DECAY = 0.999
ADAM_EPSILON = 1e-08
ADAM_DECAY = 0.01
GATE_UNIT = 4096.0

CENTRE = -SCHULZ_SQUARE / (2.0 * SCHULZ_QUARTIC)
REST = SCHULZ_LINEAR - SCHULZ_QUARTIC * CENTRE * CENTRE

GELU_SCALE = 0.7978845608028654
GELU_CUBIC = 0.044715

LOW = jnp.bfloat16
BLOCK = 256
WIDE = jnp.float32
MIB = 1024 * 1024


def nn(left, right):
    return jnp.dot(left, right, preferred_element_type=WIDE)


def nt(left, right):
    return lax.dot_general(left, right, (((1,), (1,)), ((), ())), preferred_element_type=WIDE)


def tn(left, right):
    return lax.dot_general(left, right, (((0,), (0,)), ((), ())), preferred_element_type=WIDE)


def iota(shape, axis):
    return lax.broadcasted_iota(jnp.int32, shape, axis)


def shape_of(shape, dtype):
    return jax.ShapeDtypeStruct(shape, dtype)


VMEM_BYTES = 63 * MIB


def cost_of(microseconds):
    return pl.CostEstimate(flops=int(1 + microseconds * 1e9), bytes_accessed=1, transcendentals=0)


class Fetch:
    def __init__(self, source, held, semaphore):
        self.held, self.pending = held, pltpu.make_async_copy(source, held, semaphore)
        self.pending.start()

    def ref(self):
        if self.pending is not None:
            self.pending.wait()
            self.pending = None
        return self.held

    def get(self):
        return self.ref()[...]


class Put:
    def __init__(self, target, held, semaphore):
        self.ref, self.copy, self.started = held, pltpu.make_async_copy(held, target, semaphore), False

    def send(self):
        self.copy.start()
        self.started = True

    def set(self, value):
        self.ref[...] = value.astype(self.ref.dtype)
        self.send()

    def finish(self):
        if not self.started:
            self.send()
        self.copy.wait()


def views(ref, parts):
    if parts == 1:
        return [ref]
    size = ref.shape[0] // parts
    return [ref.at[pl.ds(i * size, size)] for i in range(parts)]


def staged_call(kernel, ins, outs, cost=0, smem=(), scratch=(), after=()):
    ins = [i if isinstance(i, tuple) else (i, 1) for i in ins]
    outs = [o if isinstance(o, tuple) else (o, 1) for o in outs]
    first, given, wanted, extra = len(smem), len(ins), len(outs), len(scratch)
    reads, writes = sum(n for _, n in ins), sum(n for _, n in outs)
    staged = sum(n > 0 for _, n in ins)

    def run(*refs):
        scalars, sources, refs = refs[:first], refs[first : first + given], refs[first + given + len(after) :]
        targets, work, refs = refs[:wanted], refs[wanted : wanted + extra], refs[wanted + extra :]
        held_in, held_out, (in_sem, out_sem) = refs[:staged], refs[staged : staged + wanted], refs[staged + wanted :]
        fetches, puts = [], []
        held_in, reads = list(held_in), 0
        for source, (_, n) in zip(sources, ins):
            if n == 0:
                fetches.append(source)
                continue
            for a, b in zip(views(source, n), views(held_in.pop(0), n)):
                fetches.append(Fetch(a, b, in_sem.at[reads]))
                reads += 1
        for target, held, (_, n) in zip(targets, held_out, outs):
            for a, b in zip(views(target, n), views(held, n)):
                puts.append(Put(a, b, out_sem.at[len(puts)]))
        kernel(*scalars, fetches, puts, *work)
        for put in puts:
            put.finish()

    shapes = [i for i, n in ins if n > 0] + [o for o, _ in outs]
    hbm = pl.BlockSpec(memory_space=pltpu.HBM)
    return pl.pallas_call(
        run,
        out_shape=[o for o, _ in outs],
        in_specs=[pl.BlockSpec(memory_space=pltpu.SMEM)] * first
        + [hbm] * given
        + [hbm] * len(after),
        out_specs=[hbm] * wanted,
        scratch_shapes=[
            *scratch,
            *[pltpu.VMEM(s.shape, s.dtype) for s in shapes],
            pltpu.SemaphoreType.DMA((max(reads, 1),)),
            pltpu.SemaphoreType.DMA((writes,)),
        ],
        compiler_params=pltpu.CompilerParams(vmem_limit_bytes=VMEM_BYTES),
        cost_estimate=cost_of(cost),
    )(*smem, *[i for i, _ in ins], *after)


def swap(value, axis, mask):
    count = lax.axis_size(axis)
    return lax.ppermute(value, axis, [(i, i ^ mask) for i in range(count)])


def turned(meta):
    return meta.T


def chosen_slots(meta, slots):
    rows = iota((slots, meta.shape[1]), 0).astype(WIDE)
    return ((rows == meta[0:1, :]) | (rows == meta[1:2, :])).astype(WIDE).astype(LOW)


def split_gates(gates):
    high = gates.astype(LOW)
    return high, (gates - high.astype(WIDE)).astype(LOW)


def gated_rows(meta, values, slots):
    rows = iota((slots, meta.shape[1]), 0).astype(WIDE)
    gates = jnp.where(rows == meta[0:1, :], meta[2:3, :], 0.0) + jnp.where(rows == meta[1:2, :], meta[3:4, :], 0.0)
    high, rest = split_gates(gates)
    return (nn(high, values) + nn(rest, values)).astype(LOW)


def collect(meta, pieces, gated):
    meta = turned(meta)
    lanes = iota((meta.shape[0], pieces.shape[0]), 1).astype(WIDE)
    first, second = lanes == meta[:, 0:1], lanes == meta[:, 1:2]
    if not gated:
        return nn((first | second).astype(WIDE).astype(LOW), pieces)
    high, rest = split_gates(jnp.where(first, meta[:, 2:3], 0.0) + jnp.where(second, meta[:, 3:4], 0.0))
    return nn(high, pieces) + nn(rest, pieces)


SMALL = 64.0
SPARE = 16


def routed(ids, units, capacity_ref, me, cap):
    rows = ids.shape[1]
    experts = capacity_ref.shape[0]
    numbers = iota((experts, rows), 0)
    hots = [numbers == ids[i : i + 1, :] for i in range(2)]
    later = (iota((rows, rows), 0) < iota((rows, rows), 1)).astype(WIDE).astype(LOW)
    counts = nn((hots[0] | hots[1]).astype(WIDE).astype(LOW), later)
    slots = []
    for i in range(2):
        name = ids[i : i + 1, :]
        placed = jnp.sum(jnp.where(hots[i], counts, 0.0), axis=0, keepdims=True)
        limit = jnp.zeros_like(name)
        for e in range(experts):
            limit = jnp.where(name == e, capacity_ref[e], limit)
        near = (name ^ me).astype(WIDE)
        slots.append(jnp.where(placed < limit.astype(WIDE), near * cap + placed, -1.0))
    empty = jnp.zeros((1, rows), WIDE)
    meta = jnp.concatenate([*slots, units[0:1, :] / GATE_UNIT, units[1:2, :] / GATE_UNIT] + [empty] * 4, axis=0)
    return meta


def pack_kernel(flags_ref, capacity_ref, ins, outs, *, cap):
    ids_in, units_in, cotangent_in, up_in, down_in = ins
    meta_out, packed_out, up_out, down_out, *sends = outs
    rows, width = cotangent_in.held.shape
    ids, units = ids_in.get(), units_in.get().astype(WIDE)
    high = jnp.floor(units * (1.0 / SMALL))
    empty = jnp.zeros((SPARE - 6, rows), WIDE)
    lines = jnp.concatenate([ids.astype(WIDE), high, units - high * SMALL, empty], axis=0)
    packed_out.ref[rows:, :] = jnp.zeros((SPARE, width), LOW)
    packed_out.ref[rows:, 0:rows] = lines.astype(LOW)
    packed_out.ref[0:rows, :] = cotangent_in.get()
    packed_out.send()
    up_out.set(up_in.get())
    down_out.set(down_in.get())
    meta = routed(ids, units, capacity_ref, flags_ref[2], cap)
    meta_out.set(meta)
    put_slots(sends, [gated_rows(meta, cotangent_in.get(), len(sends) * cap)], cap)


def stack_kernel(ins, outs):
    blocks = iter(outs)
    for fetch in ins:
        value = fetch.ref()
        for at in range(0, value.shape[0], BLOCK):
            next(blocks).set(value[at : at + BLOCK, :])


def unpack(lines):
    lines = lines.astype(WIDE)
    return lines[0:2, :].astype(jnp.int32), lines[2:4, :] * SMALL + lines[4:6, :]


def copy_kernel(ins, outs):
    outs[0].set(ins[0].get())


def far_kernel(ins, outs, *, cap):
    meta_in, low_in = ins
    low = nn(chosen_slots(meta_in.get(), len(outs) * cap), low_in.get()).astype(LOW)
    put_slots(outs, [low], cap)


def put_slots(sends, parts, cap):
    for r, put in enumerate(sends):
        for at, part in enumerate(parts):
            put.ref[at * cap : (at + 1) * cap, :] = part[r * cap : (r + 1) * cap, :]
        put.send()


def normalize(values):
    centre = values - jnp.mean(values, axis=-1, keepdims=True)
    spread = jnp.mean(centre * centre, axis=-1, keepdims=True)
    inverse = lax.rsqrt(spread + NORM_EPSILON)
    return centre * inverse, inverse


def head_probs(query, key, scale):
    rows = query.shape[0]
    scores = nt(query, key) * scale
    scores = jnp.where(iota((rows, rows), 1) <= iota((rows, rows), 0), scores, -1e30)
    exps = jnp.exp(scores - jnp.max(scores, axis=-1, keepdims=True))
    return exps / jnp.sum(exps, axis=-1, keepdims=True)


def front_kernel(flags_ref, ins, outs, weight_ref, semaphores, *, head):
    tokens_in, norm_in, all_weights = ins
    weights = [Fetch(all_weights.at[i], weight_ref.at[i], semaphores.at[i]) for i in range(3)]
    query_out, key_out, value_out, left_out, *lefts = outs
    scale = head**-0.5
    inputs = tokens_in.get().astype(WIDE)
    norm_ref = norm_in.ref()
    rows, width = inputs.shape
    unit, _ = normalize(inputs)
    low = (unit * norm_ref[0:1, :] + norm_ref[1:2, :]).astype(LOW)
    left_out.ref[0:rows, :] = low
    for which, put in enumerate((query_out, key_out, value_out)):
        put.set(nn(low, weights[which].get()))
    group = 128 // head
    lane = iota((1, 128), 1) // head
    for at in range(0, width, 128):
        query, key, value = (p.ref[:, at : at + 128] for p in (query_out, key_out, value_out))
        total = jnp.zeros(query.shape, WIDE)
        for h in range(group):
            mine = lane == h
            probs = head_probs(jnp.where(mine, query, jnp.zeros_like(query)), key, scale)
            total = jnp.where(mine, nn(probs.astype(LOW), value), total)
        left_out.ref[rows:, at : at + 128] = total.astype(LOW)
    left_out.send()
    for r in range(4):
        last = ((flags_ref[3] ^ r) == 3).astype(jnp.int32) * rows
        here = max(r - 2, 0) * rows
        lefts[min(r, 2)].ref[here : here + rows, :] = left_out.ref[pl.ds(pl.multiple_of(last, rows), rows), :]


def residual_kernel(flags_ref, capacity_ref, ins, outs, weight_ref, semaphores, *, cap):
    left_in, tokens_in, norm_in, meta_in, far_packed_in, all_weights = ins
    weight_in = Fetch(all_weights.at[3], weight_ref, semaphores.at[0])
    second_out, residual_out, far_meta_out, *sends = outs
    rows, width = tokens_in.held.shape
    slots = len(sends) * cap
    norm_ref = norm_in.ref()
    residual = tokens_in.get().astype(WIDE) + nn(left_in.ref()[rows:, :], weight_in.get())
    residual_out.set(residual)
    unit, _ = normalize(residual)
    second = (unit * norm_ref[2:3, :] + norm_ref[3:4, :]).astype(LOW)
    second_out.set(second)
    packed = far_packed_in.ref()
    far_meta = routed(*unpack(packed[rows:, 0:rows]), capacity_ref, flags_ref[2], cap)
    far_meta_out.set(far_meta)
    own = nn(chosen_slots(meta_in.get(), slots), second).astype(LOW)
    put_slots(sends, [gated_rows(far_meta, packed[0:rows, :], slots), own], cap)


class Loads:
    def __init__(self, in_sem, out_sem):
        self.in_sem, self.out_sem, self.loads, self.puts = in_sem, out_sem, [], []

    def load(self, source, target):
        self.loads.append(Fetch(source, target, self.in_sem.at[len(self.loads)]))
        return self.loads[-1]

    def put(self, source, target):
        self.puts.append(pltpu.make_async_copy(source, target, self.out_sem.at[len(self.puts)]))
        self.puts[-1].start()

    def finish(self):
        for copy in self.puts:
            copy.wait()


def slot_loads(moves, own, far, target, cap):
    for r in range(len(own)):
        for at, (piece, start) in enumerate((own[r], far[r])):
            moves.load(piece.at[pl.ds(start, cap)], target.at[pl.ds((2 * r + at) * cap, cap)])


def expert_kernel(*refs, parts, count, cap, step, starts, extra):
    first, middle, last = (refs[i * count : (i + 1) * count] for i in range(3))
    weights, refs = refs[3 * count : 3 * count + parts], refs[3 * count + parts + extra :]
    rows_out, grads_out, act_outs, hid_outs = refs[0], refs[1], refs[2 : 2 + parts], refs[2 + parts : 2 + 2 * parts]
    third_out, second_out, refs = refs[2 + 2 * parts], refs[3 + 2 * parts], refs[4 + 2 * parts :]
    back_own, back_far = refs[:count], refs[count : 2 * count]
    refs = refs[2 * count :]
    rows_ref, grads_ref, act_ref, hid_ref, back_ref, weight_ref, total_ref, product_ref, in_sem, out_sem = refs
    width = rows_ref.shape[1]
    moves = Loads(in_sem, out_sem)
    slot_loads(moves, [(p, cap) for p in middle], [(p, 0) for p in last], rows_ref, cap)
    rows_loads = list(moves.loads)
    ups, downs, order = {}, {}, (3, 1, 2, 0)

    def load_weights(r):
        ups[r] = moves.load(weights[r].at[pl.ds(starts[r], width)], weight_ref.at[2 * r])
        downs[r] = moves.load(weights[r].at[pl.ds(starts[r] + width, width)], weight_ref.at[2 * r + 1])

    load_weights(order[0])
    slot_loads(moves, [(p, 0) for p in first], [(p, 0) for p in middle], grads_ref, cap)
    grads_loads = moves.loads[len(rows_loads) + 2 :]
    for r in order[1:]:
        load_weights(r)
    for fetch in rows_loads:
        fetch.ref()
    moves.put(rows_ref, rows_out)
    blocks = 2 * cap * count // step
    for r in order:
        for b in range(blocks):
            here = pl.ds(b * step, step)
            hidden = nn(rows_ref[here, :], ups[r].ref()[...])
            if r == order[0] and b == 0:
                for fetch in grads_loads:
                    fetch.ref()
                moves.put(grads_ref, grads_out)
            grad = nt(grads_ref[here, :], downs[r].ref()[...])
            inner = hidden * (GELU_SCALE + GELU_SCALE * GELU_CUBIC * (hidden * hidden))
            half = 0.5 + 0.5 * jnp.tanh(inner)
            act_ref[r, here, :] = (hidden * half).astype(LOW)
            bend = 6.0 * inner - (4.0 * GELU_SCALE) * hidden
            hid = (grad * (half + half * (1.0 - half) * bend)).astype(LOW)
            hid_ref[r, here, :] = hid
            more = nt(hid, ups[r].ref()[...])
            if r != order[0]:
                more = more + total_ref[here, :]
            if r != order[-1]:
                total_ref[here, :] = more
                continue
            back_ref[here, :] = more.astype(LOW)
            for at in range(b * step, (b + 1) * step, 2 * cap):
                own = at // (2 * cap)
                moves.put(back_ref.at[pl.ds(at, cap), :], back_own[own])
                moves.put(back_ref.at[pl.ds(at + cap, cap), :], back_far[own])
        moves.put(act_ref.at[r], act_outs[r])
        moves.put(hid_ref.at[r], hid_outs[r])
        if r > 0:
            target, start, at = {3: (third_out, 0, 0), 1: (third_out, 2 * width, 2), 2: (second_out, 0, 4)}[r]
            product_ref[at] = tn(rows_ref[...], hid_ref[r]).astype(LOW)
            moves.put(product_ref.at[at], target.at[pl.ds(start, width)])
            product_ref[at + 1] = tn(act_ref[r], grads_ref[...]).astype(LOW)
            moves.put(product_ref.at[at + 1], target.at[pl.ds(start + width, width)])
    moves.finish()


def other_halves(came, start, held, semaphores):
    size = held.shape[1]
    return [Fetch(came.at[pl.ds(start + i * size, size)], held.at[i], semaphores.at[i]) for i in range(2)]


def sum_kernel(ins, outs, held, semaphores, *, start):
    *blocks, came = ins
    size = held.shape[0] // len(outs)
    others = [
        Fetch(came.at[pl.ds(start + i * size, size)], held.at[pl.ds(i * size, size)], semaphores.at[i])
        for i in range(len(outs))
    ]
    for put, block, other in zip(outs, blocks, others):
        put.set(block.get().astype(WIDE) + other.get().astype(WIDE))


def own_weight_kernel(flags_ref, ins, outs, other_ref, semaphores, *, start):
    rows, hid, grads, act, came, *momenta = ins
    others = other_halves(came, start, other_ref, semaphores)
    frozen = flags_ref[0] > 0
    for left, right, put, at in ((rows, hid, outs[0], 0), (act, grads, outs[1], 1)):
        total = tn(left.get(), right.get()) + others[at].get().astype(WIDE)
        old = momenta[at].get()
        put.set(jnp.where(frozen, old, MOMENT_KEEP * old + total))


def out_kernel(*refs, parts, count, cap, step, starts, extra):
    acts, weights, outs = refs[:parts], refs[parts : 2 * parts], refs[2 * parts + extra : 2 * parts + extra + count]
    act_ref, weight_ref, total_ref, in_sem, out_sem = refs[2 * parts + extra + count :]
    width = weight_ref.shape[2]
    moves = Loads(in_sem, out_sem)
    loads = []
    for r in range(parts):
        act = moves.load(acts[r], act_ref.at[r])
        loads.append((act, moves.load(weights[r].at[pl.ds(starts[r] + width, width)], weight_ref.at[r])))
    for b in range(2 * cap * count // step):
        here = slice(b * step, (b + 1) * step)
        total = None
        for act, down in loads:
            more = nn(act.ref()[here, :], down.ref()[...])
            total = more if total is None else total + more
        total_ref[here, :] = total.astype(LOW)
        for at in range(b * step, (b + 1) * step, 2 * cap):
            moves.put(total_ref.at[pl.ds(at, 2 * cap)], outs[at // (2 * cap)])
    moves.finish()


def gather_kernel(ins, outs, *, gated, cap, part):
    meta_in, *pieces = ins
    pieces = jnp.concatenate([p.ref()[part * cap : (part + 1) * cap, :] for p in pieces], axis=0)
    outs[0].set(collect(meta_in.get(), pieces, gated))


def mix_kernel(ins, outs, *, cap):
    meta_in, residual_in, came_in, *pieces = ins
    pieces = jnp.concatenate([p.ref()[:cap, :] for p in pieces], axis=0)
    total = collect(meta_in.get(), pieces, True) + came_in.get().astype(WIDE)
    outs[0].set(residual_in.get() + total)


def norm_backward(grad, unit, inverse, gain):
    scaled = grad * gain
    mean = jnp.mean(scaled, axis=-1, keepdims=True)
    along = jnp.mean(scaled * unit, axis=-1, keepdims=True)
    return inverse * (scaled - mean - unit * along)


def back_kernel(flags_ref, ins, outs, right_ref, weight_ref, small_ref, semaphores, *, head, parts):
    meta_in, came_in, *rest = ins
    pieces, (residual_in, cotangent_in, norm_in, all_weights, *smalls) = rest[:-8], rest[-8:]
    weights = [None] * 4
    weights[3] = Fetch(all_weights.at[3], weight_ref.at[3], semaphores.at[3])
    smalls = [Fetch(s, small_ref.at[i], semaphores.at[4 + i]) for i, s in enumerate(smalls)]
    query_in, key_in, value_in, tokens_in = smalls
    for i in range(3):
        weights[i] = Fetch(all_weights.at[i], weight_ref.at[i], semaphores.at[i])
    input_out, *rights = outs
    scale = head**-0.5
    pieces = jnp.concatenate([p.get() for p in pieces], axis=0)
    grad = collect(meta_in.get(), pieces, False) + came_in.get().astype(WIDE)
    unit, inverse = normalize(residual_in.get())
    norm_ref = norm_in.ref()
    rows, width = unit.shape
    second = [jnp.sum(grad * unit, axis=0, keepdims=True), jnp.sum(grad, axis=0, keepdims=True)]
    through = cotangent_in.get().astype(WIDE) + norm_backward(grad, unit, inverse, norm_ref[2:3, :])
    branch = through.astype(LOW)
    right_ref[3] = branch
    grad_heads = nt(branch, weights[3].get()).astype(LOW)
    group = 128 // head
    lane = iota((1, 128), 1) // head
    held = [r.ref() for r in (query_in, key_in, value_in)]
    for at in range(0, width, 128):
        query, key, value = (r[:, at : at + 128] for r in held)
        grad_out = grad_heads[:, at : at + 128]
        none = jnp.zeros_like(query)
        totals = [jnp.zeros(query.shape, WIDE) for _ in range(3)]
        for h in range(group):
            mine = lane == h
            probs = head_probs(jnp.where(mine, query, none), key, scale)
            dprob = nt(jnp.where(mine, grad_out, none), value)
            centre = jnp.sum(probs * dprob, axis=-1, keepdims=True)
            dscore = (probs * (dprob - centre)).astype(LOW)
            news = (
                nn(dscore, key) * scale,
                tn(dscore, query) * scale,
                tn(probs.astype(LOW), grad_out),
            )
            totals = [jnp.where(mine, p, t) for p, t in zip(news, totals)]
        for which in range(3):
            right_ref[which, :, at : at + 128] = totals[which].astype(LOW)
    grad = nt(right_ref[0], weights[0].get())
    grad = grad + nt(right_ref[1], weights[1].get())
    grad = grad + nt(right_ref[2], weights[2].get())
    unit, inverse = normalize(tokens_in.get().astype(WIDE))
    first = [jnp.sum(grad * unit, axis=0, keepdims=True), jnp.sum(grad, axis=0, keepdims=True)]
    sums = jnp.concatenate([*first, *second, jnp.zeros((SPARE - 4, width), WIDE)], axis=0).astype(LOW)
    for r, put in enumerate(rights):
        put.ref[0:rows, :] = right_ref[flags_ref[3] ^ r]
        put.ref[rows:, :] = sums
        put.send()
    input_out.set(through + norm_backward(grad, unit, inverse, norm_ref[0:1, :]))


def products_kernel(flags_ref, ins, outs, left_ref, semaphores, *, starts, masks):
    parts = len(starts)
    rights, lefts = ins[:parts], ins[parts:]
    rows = left_ref.shape[1]
    lefts = [
        Fetch(left.at[pl.ds(start, rows)], left_ref.at[r], semaphores.at[r])
        for r, (left, start) in enumerate(zip(lefts, starts))
    ]
    total = None
    for left, right in zip(lefts, rights):
        more = tn(left.get(), right.ref()[0:rows, :])
        total = more if total is None else total + more
    sums = [right.ref()[rows:, :].astype(WIDE) for right in rights]
    while len(sums) > 1:
        sums = [a + b for a, b in zip(sums[::2], sums[1::2])]
    total, half = total.astype(LOW), total.shape[0] // 2
    divide(flags_ref[2], [total[:half], total[half:]], sums[0].astype(LOW), outs, masks)


def divide(me, totals, sums, outs, masks):
    for i, (total, mask) in enumerate(zip(totals, masks)):
        size = total.shape[0] // 2
        upper = (me & mask) > 0
        send = jnp.where(upper, total[:size], total[size:])
        keep = jnp.where(upper, total[size:], total[:size])
        for put, part in ((outs[2 * i], send), (outs[2 * i + 1], keep)):
            put.ref[0:size, :] = part
            if i == 0:
                put.ref[size:, :] = sums
            put.send()


def added(keep, came):
    return (keep.get().astype(WIDE) + came.get().astype(WIDE)).astype(LOW)


def divide_kernel(flags_ref, ins, outs, *, masks):
    totals = [added(*ins[0:2]), added(*ins[2:4])]
    size = totals[1].shape[0]
    divide(flags_ref[2], [totals[0][:size], totals[1]], totals[0][size:], outs, masks)


def whole_kernel(ins, outs):
    outs[0].set(jnp.concatenate([added(*ins[0:2]), added(*ins[2:4])], axis=0))


def add_kernel(ins, outs):
    outs[0].set(added(*ins))


def part_kernel(ins, outs):
    total = added(*ins)
    size = outs[0].ref.shape[0]
    outs[0].set(total[:size])
    outs[1].set(total[size + SPARE :])
    outs[2].set(total[size : size + SPARE])


def joined(me, mine, came, mask):
    upper = (me & mask) > 0
    mine, came = mine.get(), came.get()
    return jnp.concatenate([jnp.where(upper, came, mine), jnp.where(upper, mine, came)], axis=0)


def join_kernel(flags_ref, ins, outs, *, masks):
    for i, mask in enumerate(masks):
        outs[i].set(joined(flags_ref[2], *ins[2 * i : 2 * i + 2], mask))


def packed_width(width):
    return sum(width - at for at in range(0, width, BLOCK))


def moments_kernel(flags_ref, ins, outs):
    up_own, down_own, up_other, down_other = ins
    up_out, down_out, up_low_out, down_low_out, keep_out, send_out = outs
    frozen = flags_ref[0] > 0
    even = flags_ref[1] == 0
    lows = []
    for own, other, out, low_out in ((up_own, up_other, up_out, up_low_out), (down_own, down_other, down_out, down_low_out)):
        own = own.get()
        moment = jnp.where(frozen, own, own + other.get().astype(WIDE))
        out.set(moment)
        lows.append(moment.astype(LOW))
        low_out.set(lows[-1])
    up_low, down_low = lows
    width = up_low.shape[0]
    column = 0
    for at in range(0, width, BLOCK):
        up_gram = nt(up_low[at : at + BLOCK, :], up_low[at:, :])
        down_gram = tn(down_low[:, at : at + BLOCK], down_low[:, at:])
        here = slice(column, column + width - at)
        send_out.ref[:, here] = jnp.where(even, down_gram, up_gram)
        keep_out.ref[:, here] = jnp.where(even, up_gram, down_gram)
        column += width - at


class Square:
    SHAPES = (WIDE, LOW, LOW, LOW)

    def __init__(self, refs, lines):
        self.shifted, self.shifted_low, self.shifted_rest, self.factor_rest = refs
        self.shifted_line, self.factor_line = lines
        width = self.shifted.shape[0]
        self.strips = [slice(at, at + BLOCK) for at in range(0, width, BLOCK)]

    def diagonal(self, here, strip):
        same = iota(strip.shape, 0) + here.start == iota(strip.shape, 1)
        return same, jnp.sum(jnp.where(same, strip, 0.0), axis=1, keepdims=True)

    def take(self, here, gram):
        same, line = self.diagonal(here, gram)
        line = line - CENTRE
        strip = jnp.where(same, line, gram)
        self.shifted[here, :] = strip
        self.shifted_low[here, :] = strip.astype(LOW)
        self.shifted_rest[here, :] = jnp.where(same, 0.0, strip).astype(LOW)
        self.shifted_line[here, :] = jnp.broadcast_to(line, (BLOCK, 128))

    def square(self):
        for here in self.strips:
            product = nn(self.shifted_rest[here, :], self.shifted_low[...])
            strip = SCHULZ_QUARTIC * (self.shifted_line[here, 0:1] * self.shifted[here, :] + product)
            same, line = self.diagonal(here, strip)
            self.factor_rest[here, :] = jnp.where(same, 0.0, strip).astype(LOW)
            self.factor_line[here, :] = jnp.broadcast_to(line + REST, (BLOCK, 128))

    def times(self, here, strip, low):
        return self.factor_line[here, 0:1] * strip + nn(self.factor_rest[here, :], low)


def square_scratch(width):
    return [pltpu.VMEM((width, width), t) for t in Square.SHAPES] + [pltpu.VMEM((width, 128), WIDE)] * 2


def attn_step_kernel(flags_ref, ins, outs, now_ref, low_a, low_b, *refs, masks):
    momentum, master = ins[4:]
    moment_out, new_out, low_out = outs
    square = Square(refs[:4], refs[4:])
    width = now_ref.shape[1]
    half = width // 2
    old = momentum.ref()
    for i, mask in enumerate(masks):
        here = slice(i * half, (i + 1) * half)
        grad = joined(flags_ref[2], *ins[2 * i : 2 * i + 2], mask)
        moment_out.ref[here, :] = MOMENT_KEEP * old[here, :] + grad.astype(WIDE)
    moment_out.send()
    moment = moment_out.ref[...]
    now = moment * (1.0 / (jnp.sqrt(jnp.sum(moment * moment)) + 1e-07))
    now_ref[...] = now
    low_a[...] = now.astype(LOW)
    low, later = low_a, low_b
    for k in range(ITERS):
        for here in square.strips:
            square.take(here, nt(low[here, :], low[...]))
        square.square()
        for here in square.strips:
            strip = square.times(here, now_ref[here, :], low[...])
            if k < ITERS - 1:
                now_ref[here, :] = strip
                later[here, :] = strip.astype(LOW)
                continue
            new = master.ref()[here, :] * (1.0 - MUON_RATE * MUON_DECAY) - MUON_RATE * 0.2 * width**0.5 * strip
            new_out.ref[here, :] = new
            low_out.ref[here, :] = new.astype(LOW)
        low, later = later, low


def gram_kernel(ins, outs):
    outs[0].set(ins[0].get() + ins[1].get())


def polar_kernel(ins, outs, gram_ref, gram_low, half_ref, half_low, product_ref, low_a, low_b, *refs):
    square = Square(refs[:4], refs[4:])
    mine_ref, other_ref = (i.ref() for i in ins)
    width = gram_ref.shape[0]
    column = 0
    for at in range(0, width, BLOCK):
        here = slice(column, column + width - at)
        strip = mine_ref[:, here] + other_ref[:, here]
        gram_ref[at : at + BLOCK, at:] = strip
        for far in range(BLOCK, width - at, BLOCK):
            gram_ref[at + far : at + far + BLOCK, at : at + BLOCK] = strip[:, far : far + BLOCK].T
        column += width - at
    total = 0.0
    for here in square.strips:
        total = total + jnp.sum(square.diagonal(here, gram_ref[here, :])[1])
    length = jnp.sqrt(total) + 1e-07

    def take(here, strip):
        gram_ref[here, :] = strip
        gram_low[here, :] = strip.astype(LOW)
        square.take(here, strip)

    for here in square.strips:
        take(here, gram_ref[here, :] * (1.0 / (length * length)))
    low, later = low_a, low_b
    for k in range(ITERS):
        square.square()
        for here in square.strips:
            if k == 0:
                same = iota((BLOCK, width), 0) + here.start == iota((BLOCK, width), 1)
                strip = jnp.where(same, square.factor_line[here, 0:1], square.factor_rest[here, :].astype(WIDE))
            else:
                strip = square.times(here, product_ref[here, :], low[...])
            if k < ITERS - 1:
                product_ref[here, :] = strip
                later[here, :] = strip.astype(LOW)
                half = square.times(here, gram_ref[here, :], gram_low[...])
                half_ref[here, :] = half
                half_low[here, :] = half.astype(LOW)
            else:
                product_ref[here, :] = strip * (1.0 / length)
        if k < ITERS - 1:
            for here in square.strips:
                take(here, square.times(here, half_ref[here, :], half_low[...]))
        low, later = later, low
    size = width // len(outs)
    for i, put in enumerate(outs):
        put.set(product_ref[i * size : (i + 1) * size, :])


def apply_kernel(flags_ref, ins, outs, *, wide_scale, strips):
    quarters, ins = ins[:8], ins[8:]
    up_moment, down_moment = ins[:2]
    up_masters, down_masters = ins[2 : 2 + strips], ins[2 + strips :]
    up_new, up_low, down_new, down_low = (outs[i * strips : (i + 1) * strips] for i in range(4))
    frozen = flags_ref[0] > 0
    even = flags_ref[1] == 0
    factors = [jnp.concatenate([q.get() for q in part], axis=0) for part in (quarters[:4], quarters[4:])]
    up_factor = jnp.where(even, factors[0], factors[1])
    down_factor = jnp.where(even, factors[1], factors[0])

    def update(master, new_put, low_put, ortho):
        old = master.get()
        new = old * (1.0 - MUON_RATE * MUON_DECAY) - MUON_RATE * wide_scale * ortho
        new = jnp.where(frozen, old, new)
        new_put.set(new)
        low_put.set(new)

    up_matrix, down_matrix = up_moment.get(), down_moment.get()
    size = up_factor.shape[0] // strips
    for i in range(strips):
        here = slice(i * size, (i + 1) * size)
        update(up_masters[i], up_new[i], up_low[i], nn(up_factor[here, :], up_matrix))
        update(down_masters[i], down_new[i], down_low[i], nn(down_matrix[here, :], down_factor))


def masks_of(axis):
    count = lax.axis_size(axis)
    return [1 << i for i in range(count.bit_length() - 1)]


def body(
    tokens,
    cotangent,
    expert_ids,
    gate_units,
    capacity,
    frozen,
    attn_copy,
    attn_master,
    attn_momentum,
    norm_params,
    norm_first,
    norm_second,
    up_copy,
    up_master,
    up_momentum,
    down_copy,
    down_master,
    down_momentum,
):
    rows, width = tokens.shape
    cuts = lax.axis_size("cuts")
    experts = capacity.shape[0]
    members = lax.axis_size("expert")
    cap = 4 * rows // members
    slots = experts * cap
    head = width // HEADS
    hidden = up_copy.shape[2]
    cut = lax.axis_index("cuts")
    me = lax.axis_index("expert")
    count = members // 2
    flags = jnp.stack([frozen[0], cut & 1, me, cut])
    small = shape_of((rows, width), LOW)
    square = shape_of((width, width), WIDE)
    square_low = shape_of((width, width), LOW)

    def cross(value):
        return swap(value, "expert", count)

    def spread(values):
        return [values[0]] + [swap(values[r], "expert", r) for r in range(1, count)]

    pair_shape = shape_of((2 * width, hidden), LOW)
    meta_shape = shape_of((8, rows), WIDE)
    piece = shape_of((cap, width), LOW)
    pair = shape_of((2 * cap, width), LOW)
    meta, packed, weights, *sends = staged_call(
        functools.partial(pack_kernel, cap=cap),
        [expert_ids.T, gate_units.T, cotangent, up_copy[0], down_copy[0]],
        [meta_shape, shape_of((rows + SPARE, width), LOW), (pair_shape, 2)] + [piece] * count,
        smem=[flags, capacity],
    )
    far_packed = cross(packed)
    weights = {0: weights, 2: swap(weights, "cuts", 2)}
    first = spread(sends)
    query, key, value, both_lefts, left, core_left, far_lefts = staged_call(
        functools.partial(front_kernel, head=head),
        [tokens, norm_params, (attn_copy, 0)],
        [small] * 3 + [shape_of((2 * rows, width), LOW), small, small, shape_of((2 * rows, width), LOW)],
        scratch=[pltpu.VMEM((3, width, width), LOW), pltpu.SemaphoreType.DMA((3,))],
        smem=[flags],
        after=[packed],
    )
    normed_two, residual, far_meta, *sends = staged_call(
        functools.partial(residual_kernel, cap=cap),
        [both_lefts, tokens, norm_params, meta, far_packed, (attn_copy, 0)],
        [small, shape_of((rows, width), WIDE), meta_shape] + [pair] * count,
        scratch=[pltpu.VMEM((width, width), LOW), pltpu.SemaphoreType.DMA((1,))],
        after=first[1:],
        smem=[flags, capacity],
    )
    far_normed = cross(normed_two)
    middle = spread(sends)
    sends = staged_call(functools.partial(far_kernel, cap=cap), [far_meta, far_normed], [piece] * count)
    last = spread(sends)
    (both,) = staged_call(
        stack_kernel,
        [weights[0], weights[2], core_left],
        [(shape_of((4 * width + rows, hidden), LOW), (4 * width + rows) // BLOCK)],
        after=[sends[0], *middle[1:]],
    )
    both = swap(both, "cuts", 1)
    places = ((weights[0], 0), (both, 0), (weights[2], 0), (both, 2 * width))

    step = 256
    wide = shape_of((slots, hidden), LOW)
    slot_shape = shape_of((slots, width), LOW)
    anywhere = pl.BlockSpec(memory_space=pltpu.HBM)
    scalars = pl.BlockSpec(memory_space=pltpu.SMEM)
    all_slots = pltpu.VMEM((slots, width), LOW)
    all_wide = pltpu.VMEM((cuts, slots, hidden), LOW)
    all_weights = pltpu.VMEM((cuts, width, hidden), LOW)

    def placed_call(kernel, outs, args, held, loads, puts, cost=0):
        return pl.pallas_call(
            kernel,
            out_shape=outs,
            in_specs=[anywhere] * len(args),
            out_specs=[anywhere] * len(outs),
            scratch_shapes=[*held, pltpu.SemaphoreType.DMA((loads,)), pltpu.SemaphoreType.DMA((puts,))],
            compiler_params=pltpu.CompilerParams(vmem_limit_bytes=VMEM_BYTES),
            cost_estimate=cost_of(cost),
        )(*args)

    sizes = dict(parts=cuts, count=count, cap=cap, step=step, starts=[at for _, at in places])
    slot_rows, slot_grads, *outs = placed_call(
        functools.partial(expert_kernel, extra=0, **sizes),
        [slot_shape] * 2 + [wide] * (2 * cuts)
        + [shape_of((4 * width, hidden), LOW), pair_shape]
        + [piece] * (2 * count),
        [*first, *middle, *last, *[w for w, _ in places]],
        [
            *[all_slots, all_slots, all_wide, all_wide, all_slots],
            pltpu.VMEM((2 * cuts, width, hidden), LOW),
            pltpu.VMEM((slots, width), WIDE),
            pltpu.VMEM((6, width, hidden), LOW),
        ],
        2 * cuts + 4 * count,
        8 + 2 * cuts + 2 * count,
    )
    acts, hids = outs[:cuts], outs[cuts : 2 * cuts]
    odd, second = outs[2 * cuts : 2 * cuts + 2]
    back_own, back_far = outs[2 * cuts + 2 : 2 * cuts + 2 + count], outs[2 * cuts + 2 + count :]
    back_far = spread(back_far)

    far_lefts = swap(far_lefts, "cuts", 2)
    (ready,) = staged_call(copy_kernel, [meta], [meta_shape], cost=60, after=[far_lefts, slot_rows])
    def gather(meta_of, pieces, gated, part, after=()):
        (total,) = staged_call(
            functools.partial(gather_kernel, gated=gated, cap=cap, part=part),
            [meta_of, *pieces],
            [small],
            after=after,
        )
        return total

    odd_came = swap(odd, "cuts", 1)
    (second,) = staged_call(
        functools.partial(sum_kernel, start=0),
        [(second, 6), (odd_came, 0)],
        [(pair_shape, 6)],
        scratch=[pltpu.VMEM((2 * width, hidden), LOW), pltpu.SemaphoreType.DMA((6,))],
        after=[ready],
    )
    second_came = swap(second, "cuts", 2)
    gathered = gather(far_meta, back_far, False, 0, after=[second])
    pieces = placed_call(
        functools.partial(out_kernel, extra=1, **sizes),
        [pair] * count,
        [*acts, *[w for w, _ in places], second],
        [all_wide, all_weights, all_slots],
        2 * cuts,
        count,
        cost=60,
    )
    came = cross(gathered)
    back_own = spread(back_own)
    other_scratch = [pltpu.VMEM((2, width, hidden), LOW), pltpu.SemaphoreType.DMA((2,))]
    input_grad, *rights = staged_call(
        functools.partial(back_kernel, head=head, parts=cuts),
        [meta, came, *back_own, residual, cotangent, norm_params]
        + [(a, 0) for a in (attn_copy, query, key, value, tokens)],
        [shape_of((rows, width), WIDE)] + [shape_of((rows + SPARE, width), LOW)] * cuts,
        scratch=[
            pltpu.VMEM((4, rows, width), LOW),
            pltpu.VMEM((4, width, width), LOW),
            pltpu.VMEM((4, rows, width), LOW),
            pltpu.SemaphoreType.DMA((8,)),
        ],
        smem=[flags],
        after=[pieces[0]],
    )
    rights_came = [rights[0]] + [swap(rights[r], "cuts", r) for r in range(1, cuts)]
    core_far_left = swap(far_lefts[rows:], "cuts", 1)
    own_shape = shape_of((2 * width, hidden), WIDE)
    (zeroth,) = staged_call(
        functools.partial(own_weight_kernel, start=2 * width),
        [slot_rows, hids[0], slot_grads, acts[0], (odd_came, 0), up_momentum[0], down_momentum[0]],
        [(own_shape, 2)],
        scratch=[pltpu.VMEM((2, width, hidden), LOW), pltpu.SemaphoreType.DMA((2,))],
        smem=[flags],
        after=[rights_came[1]],
    )

    strips = shape_of((BLOCK, packed_width(width)), WIDE)
    up_moment, down_moment, up_moment_low, down_moment_low, keep, send = staged_call(
        moments_kernel,
        [(zeroth, 2), (second_came, 2)],
        [square, square, square_low, square_low, strips, strips],
        smem=[flags],
    )
    masks = masks_of("expert")
    order = (masks[0:2], [masks[1], masks[0]])

    def part_shape(share, extra):
        return shape_of((width // share + extra * SPARE, width), LOW)

    def trade(sends, step):
        return [swap(v, "expert", order[i][step]) for i, v in enumerate(sends)]

    send_a, keep_a, send_b, keep_b = staged_call(
        functools.partial(
            products_kernel, starts=(0, 4 * width, 0, 0), masks=(order[0][0], order[1][0])
        ),
        [*rights_came, (left, 0), (both, 0), (far_lefts, 0), (core_far_left, 0)],
        [part_shape(4, 1)] * 2 + [part_shape(4, 0)] * 2,
        scratch=[pltpu.VMEM((cuts, rows, width), LOW), pltpu.SemaphoreType.DMA((cuts,))],
        smem=[flags],
        cost=60,
    )
    (keep,) = staged_call(gram_kernel, [keep, swap(send, "cuts", 1)], [strips], after=[send_a])
    other = swap(keep, "cuts", 2)
    came_a, came_b = trade([send_a, send_b], 0)
    send_a, keep_a, send_b, keep_b = staged_call(
        functools.partial(divide_kernel, masks=(order[0][1], order[1][1])),
        [keep_a, came_a, keep_b, came_b],
        [part_shape(8, 1)] * 2 + [part_shape(8, 0)] * 2,
        smem=[flags],
    )
    came_a, came_b = trade([send_a, send_b], 1)
    (total,) = staged_call(whole_kernel, [keep_a, came_a, keep_b, came_b], [part_shape(4, 1)])
    for mask in masks[2:-1]:
        (total,) = staged_call(add_kernel, [total, swap(total, "expert", mask)], [part_shape(4, 1)])
    came = swap(total, "expert", masks[-1])
    factor = staged_call(
        polar_kernel,
        [keep, other],
        [shape_of((width // 4, width), LOW)] * 4,
        scratch=[
            *[pltpu.VMEM((width, width), t) for t in (WIDE, LOW, WIDE, LOW, WIDE, LOW, LOW)],
            *square_scratch(width),
        ],
        after=[total],
    )
    pieces = spread(pieces)
    gathered_out = gather(far_meta, pieces, True, 1, after=[factor[0]])
    came_out = cross(gathered_out)
    part_a, part_b, norm_sums = staged_call(
        part_kernel,
        [total, came],
        [part_shape(8, 0)] * 2 + [shape_of((SPARE, width), LOW)],
        after=[factor[0]],
    )
    came_a, came_b = trade([part_a, part_b], 1)
    half_a, half_b = staged_call(
        functools.partial(join_kernel, masks=(order[0][1], order[1][1])),
        [part_a, came_a, part_b, came_b],
        [part_shape(4, 0)] * 2,
        smem=[flags],
    )
    came_a, came_b = trade([half_a, half_b], 0)
    norm_total = norm_sums[:4].astype(WIDE)
    (output,) = staged_call(
        functools.partial(mix_kernel, cap=cap),
        [meta, residual, came_out, *pieces],
        [small],
        after=[half_a],
    )
    attn_moment, attn_new, attn_low = staged_call(
        functools.partial(attn_step_kernel, masks=(order[0][0], order[1][0])),
        [half_a, came_a, half_b, came_b, attn_momentum[0], attn_master[0]],
        [square, square, square_low],
        scratch=[*[pltpu.VMEM((width, width), t) for t in (WIDE, LOW, LOW)], *square_scratch(width)],
        smem=[flags],
        after=[output],
    )
    thirds = width // BLOCK
    up_new, up_low, down_new, down_low = staged_call(
        functools.partial(apply_kernel, wide_scale=0.2 * max(width, FF) ** 0.5, strips=thirds),
        [*factor, *[swap(f, "cuts", 1) for f in factor], up_moment_low, down_moment_low, (up_master[0], thirds), (down_master[0], thirds)],
        [(square, thirds), (square_low, thirds)] * 2,
        smem=[flags],
    )
    first_new = FIRST_DECAY * norm_first + (1.0 - FIRST_DECAY) * norm_total
    second_new = SECOND_DECAY * norm_second + (1.0 - SECOND_DECAY) * norm_total * norm_total
    first_hat = first_new / (1.0 - FIRST_DECAY**STEP_COUNT)
    second_hat = second_new / (1.0 - SECOND_DECAY**STEP_COUNT)
    norm_new = norm_params - ADAM_RATE * (
        first_hat / (jnp.sqrt(second_hat) + ADAM_EPSILON) + ADAM_DECAY * norm_params
    )
    return (
        output,
        input_grad,
        attn_new[None],
        attn_moment[None],
        attn_low[None],
        up_new[None],
        up_moment[None],
        up_low[None],
        down_new[None],
        down_moment[None],
        down_low[None],
        norm_new,
        first_new,
        second_new,
    )


def solution(mesh):
    rows = P(("expert", "cuts"), None)
    attn = P("cuts", None, None)
    ups = P("expert", None, "cuts")
    downs = P("expert", "cuts", None)
    return jax.shard_map(
        body,
        mesh=mesh,
        in_specs=(rows, rows, rows, rows, P(), P("expert"), P(), attn, attn, P(), P(), P())
        + (ups, ups, ups, downs, downs, downs),
        out_specs=(rows, rows, attn, attn, attn, ups, ups, ups, downs, downs, downs, P(), P(), P()),
        check_vma=False,
    )
```

```python
import functools

import jax
import jax.numpy as jnp
from jax import lax
from jax.experimental import pallas as pl
from jax.experimental.pallas import tpu as pltpu
from jax.sharding import PartitionSpec as P

HEADS = 12
FF = 3072
ITERS = 5
STEP_COUNT = 10

NORM_EPSILON = 1e-05
SCHULZ_LINEAR = 3.4445
SCHULZ_SQUARE = -4.775
SCHULZ_QUARTIC = 2.0315
MUON_RATE = 0.2
MUON_DECAY = 0.01
MOMENT_KEEP = 0.5
ADAM_RATE = 0.5
FIRST_DECAY = 0.9
SECOND_DECAY = 0.999
ADAM_EPSILON = 1e-08
ADAM_DECAY = 0.01
GATE_UNIT = 4096.0

CENTRE = -SCHULZ_SQUARE / (2.0 * SCHULZ_QUARTIC)
REST = SCHULZ_LINEAR - SCHULZ_QUARTIC * CENTRE * CENTRE

GELU_SCALE = 0.7978845608028654
GELU_CUBIC = 0.044715

LOW = jnp.bfloat16
BLOCK = 256
WIDE = jnp.float32
MIB = 1024 * 1024


def nn(left, right):
    return jnp.dot(left, right, preferred_element_type=WIDE)


def nt(left, right):
    return lax.dot_general(left, right, (((1,), (1,)), ((), ())), preferred_element_type=WIDE)


def tn(left, right):
    return lax.dot_general(left, right, (((0,), (0,)), ((), ())), preferred_element_type=WIDE)


def iota(shape, axis):
    return lax.broadcasted_iota(jnp.int32, shape, axis)


def shape_of(shape, dtype):
    return jax.ShapeDtypeStruct(shape, dtype)


VMEM_BYTES = 64 * MIB - 262144


def cost_of(microseconds):
    return pl.CostEstimate(flops=int(1 + microseconds * 1e9), bytes_accessed=1, transcendentals=0)


class Fetch:
    def __init__(self, source, held, semaphore):
        self.held, self.pending = held, pltpu.make_async_copy(source, held, semaphore)
        self.pending.start()

    def ref(self):
        if self.pending is not None:
            self.pending.wait()
            self.pending = None
        return self.held

    def get(self):
        return self.ref()[...]


class Put:
    def __init__(self, target, held, semaphore):
        self.ref, self.copy, self.started = held, pltpu.make_async_copy(held, target, semaphore), False

    def send(self):
        self.copy.start()
        self.started = True

    def set(self, value):
        self.ref[...] = value.astype(self.ref.dtype)
        self.send()

    def finish(self):
        if not self.started:
            self.send()
        self.copy.wait()


def views(ref, parts):
    if parts == 1:
        return [ref]
    size = ref.shape[0] // parts
    return [ref.at[pl.ds(i * size, size)] for i in range(parts)]


def staged_call(kernel, ins, outs, cost=0, smem=(), scratch=(), after=()):
    ins = [i if isinstance(i, tuple) else (i, 1) for i in ins]
    outs = [o if isinstance(o, tuple) else (o, 1) for o in outs]
    first, given, wanted, extra = len(smem), len(ins), len(outs), len(scratch)
    reads, writes = sum(n for _, n in ins), sum(n for _, n in outs)
    staged = sum(n > 0 for _, n in ins)

    def run(*refs):
        scalars, sources, refs = refs[:first], refs[first : first + given], refs[first + given + len(after) :]
        targets, work, refs = refs[:wanted], refs[wanted : wanted + extra], refs[wanted + extra :]
        held_in, held_out, (in_sem, out_sem) = refs[:staged], refs[staged : staged + wanted], refs[staged + wanted :]
        fetches, puts = [], []
        held_in, reads = list(held_in), 0
        for source, (_, n) in zip(sources, ins):
            if n == 0:
                fetches.append(source)
                continue
            for a, b in zip(views(source, n), views(held_in.pop(0), n)):
                fetches.append(Fetch(a, b, in_sem.at[reads]))
                reads += 1
        for target, held, (_, n) in zip(targets, held_out, outs):
            for a, b in zip(views(target, n), views(held, n)):
                puts.append(Put(a, b, out_sem.at[len(puts)]))
        kernel(*scalars, fetches, puts, *work)
        for put in puts:
            put.finish()

    shapes = [i for i, n in ins if n > 0] + [o for o, _ in outs]
    hbm = pl.BlockSpec(memory_space=pltpu.HBM)
    return pl.pallas_call(
        run,
        out_shape=[o for o, _ in outs],
        in_specs=[pl.BlockSpec(memory_space=pltpu.SMEM)] * first
        + [hbm] * given
        + [hbm] * len(after),
        out_specs=[hbm] * wanted,
        scratch_shapes=[
            *scratch,
            *[pltpu.VMEM(s.shape, s.dtype) for s in shapes],
            pltpu.SemaphoreType.DMA((max(reads, 1),)),
            pltpu.SemaphoreType.DMA((writes,)),
        ],
        compiler_params=pltpu.CompilerParams(vmem_limit_bytes=VMEM_BYTES),
        cost_estimate=cost_of(cost),
    )(*smem, *[i for i, _ in ins], *after)


def swap(value, axis, mask):
    count = lax.axis_size(axis)
    return lax.ppermute(value, axis, [(i, i ^ mask) for i in range(count)])


def turned(meta):
    return meta.T


def chosen_slots(meta, slots):
    rows = iota((slots, meta.shape[1]), 0).astype(WIDE)
    return ((rows == meta[0:1, :]) | (rows == meta[1:2, :])).astype(WIDE).astype(LOW)


def split_gates(gates):
    high = gates.astype(LOW)
    return high, (gates - high.astype(WIDE)).astype(LOW)


def gated_rows(meta, values, slots):
    rows = iota((slots, meta.shape[1]), 0).astype(WIDE)
    gates = jnp.where(rows == meta[0:1, :], meta[2:3, :], 0.0) + jnp.where(rows == meta[1:2, :], meta[3:4, :], 0.0)
    high, rest = split_gates(gates)
    return (nn(high, values) + nn(rest, values)).astype(LOW)


def collect(meta, pieces, gated):
    meta = turned(meta)
    lanes = iota((meta.shape[0], pieces.shape[0]), 1).astype(WIDE)
    first, second = lanes == meta[:, 0:1], lanes == meta[:, 1:2]
    if not gated:
        return nn((first | second).astype(WIDE).astype(LOW), pieces)
    high, rest = split_gates(jnp.where(first, meta[:, 2:3], 0.0) + jnp.where(second, meta[:, 3:4], 0.0))
    return nn(high, pieces) + nn(rest, pieces)


SMALL = 64.0
SPARE = 16


def routed(ids, units, capacity_ref, me, cap):
    rows = ids.shape[1]
    experts = capacity_ref.shape[0]
    numbers = iota((experts, rows), 0)
    hots = [numbers == ids[i : i + 1, :] for i in range(2)]
    later = (iota((rows, rows), 0) < iota((rows, rows), 1)).astype(WIDE).astype(LOW)
    counts = nn((hots[0] | hots[1]).astype(WIDE).astype(LOW), later)
    slots = []
    for i in range(2):
        name = ids[i : i + 1, :]
        placed = jnp.sum(jnp.where(hots[i], counts, 0.0), axis=0, keepdims=True)
        limit = jnp.zeros_like(name)
        for e in range(experts):
            limit = jnp.where(name == e, capacity_ref[e], limit)
        near = (name ^ me).astype(WIDE)
        slots.append(jnp.where(placed < limit.astype(WIDE), near * cap + placed, -1.0))
    empty = jnp.zeros((1, rows), WIDE)
    meta = jnp.concatenate([*slots, units[0:1, :] / GATE_UNIT, units[1:2, :] / GATE_UNIT] + [empty] * 4, axis=0)
    return meta


def pack_kernel(flags_ref, capacity_ref, ins, outs, *, cap):
    ids_in, units_in, cotangent_in, up_in, down_in = ins
    meta_out, packed_out, up_out, down_out, *sends = outs
    rows, width = cotangent_in.held.shape
    ids, units = ids_in.get(), units_in.get().astype(WIDE)
    high = jnp.floor(units * (1.0 / SMALL))
    empty = jnp.zeros((SPARE - 6, rows), WIDE)
    lines = jnp.concatenate([ids.astype(WIDE), high, units - high * SMALL, empty], axis=0)
    packed_out.ref[rows:, :] = jnp.zeros((SPARE, width), LOW)
    packed_out.ref[rows:, 0:rows] = lines.astype(LOW)
    packed_out.ref[0:rows, :] = cotangent_in.get()
    packed_out.send()
    up_out.set(up_in.get())
    down_out.set(down_in.get())
    meta = routed(ids, units, capacity_ref, flags_ref[2], cap)
    meta_out.set(meta)
    put_slots(sends, [gated_rows(meta, cotangent_in.get(), len(sends) * cap)], cap)


def stack_kernel(ins, outs):
    blocks = iter(outs)
    for fetch in ins:
        value = fetch.ref()
        for at in range(0, value.shape[0], BLOCK):
            next(blocks).set(value[at : at + BLOCK, :])


def unpack(lines):
    lines = lines.astype(WIDE)
    return lines[0:2, :].astype(jnp.int32), lines[2:4, :] * SMALL + lines[4:6, :]


def copy_kernel(ins, outs, held, semaphores, *, start):
    outs[0].set(Fetch(ins[0].at[pl.ds(start, held.shape[0])], held, semaphores.at[0]).get())


def far_kernel(ins, outs, *, cap):
    meta_in, low_in = ins
    low = nn(chosen_slots(meta_in.get(), len(outs) * cap), low_in.get()).astype(LOW)
    put_slots(outs, [low], cap)


def put_slots(sends, parts, cap):
    for r, put in enumerate(sends):
        for at, part in enumerate(parts):
            put.ref[at * cap : (at + 1) * cap, :] = part[r * cap : (r + 1) * cap, :]
        put.send()


def normalize(values):
    centre = values - jnp.mean(values, axis=-1, keepdims=True)
    spread = jnp.mean(centre * centre, axis=-1, keepdims=True)
    inverse = lax.rsqrt(spread + NORM_EPSILON)
    return centre * inverse, inverse


def head_probs(query, key, scale):
    rows = query.shape[0]
    scores = nt(query, key) * scale
    scores = jnp.where(iota((rows, rows), 1) <= iota((rows, rows), 0), scores, -1e30)
    exps = jnp.exp(scores - jnp.max(scores, axis=-1, keepdims=True))
    return exps / jnp.sum(exps, axis=-1, keepdims=True)


def front_kernel(flags_ref, ins, outs, weight_ref, semaphores, *, head):
    tokens_in, norm_in, all_weights = ins
    weights = [Fetch(all_weights.at[i], weight_ref.at[i], semaphores.at[i]) for i in range(3)]
    query_out, key_out, value_out, left_out, *lefts = outs
    scale = head**-0.5
    inputs = tokens_in.get().astype(WIDE)
    norm_ref = norm_in.ref()
    rows, width = inputs.shape
    unit, _ = normalize(inputs)
    low = (unit * norm_ref[0:1, :] + norm_ref[1:2, :]).astype(LOW)
    left_out.ref[0:rows, :] = low
    for which, put in enumerate((query_out, key_out, value_out)):
        put.set(nn(low, weights[which].get()))
    group = 128 // head
    lane = iota((1, 128), 1) // head
    for at in range(0, width, 128):
        query, key, value = (p.ref[:, at : at + 128] for p in (query_out, key_out, value_out))
        total = jnp.zeros(query.shape, WIDE)
        for h in range(group):
            mine = lane == h
            probs = head_probs(jnp.where(mine, query, jnp.zeros_like(query)), key, scale)
            total = jnp.where(mine, nn(probs.astype(LOW), value), total)
        left_out.ref[rows:, at : at + 128] = total.astype(LOW)
    left_out.send()
    for r in range(4):
        last = ((flags_ref[3] ^ r) == 3).astype(jnp.int32) * rows
        here = max(r - 2, 0) * rows
        lefts[min(r, 2)].ref[here : here + rows, :] = left_out.ref[pl.ds(pl.multiple_of(last, rows), rows), :]


def residual_kernel(flags_ref, capacity_ref, ins, outs, weight_ref, semaphores, *, cap):
    left_in, tokens_in, norm_in, meta_in, far_packed_in, all_weights = ins
    weight_in = Fetch(all_weights.at[3], weight_ref, semaphores.at[0])
    second_out, residual_out, far_meta_out, *sends = outs
    rows, width = tokens_in.held.shape
    slots = len(sends) * cap
    norm_ref = norm_in.ref()
    residual = tokens_in.get().astype(WIDE) + nn(left_in.ref()[rows:, :], weight_in.get())
    residual_out.set(residual)
    unit, _ = normalize(residual)
    second = (unit * norm_ref[2:3, :] + norm_ref[3:4, :]).astype(LOW)
    second_out.set(second)
    packed = far_packed_in.ref()
    far_meta = routed(*unpack(packed[rows:, 0:rows]), capacity_ref, flags_ref[2], cap)
    far_meta_out.set(far_meta)
    own = nn(chosen_slots(meta_in.get(), slots), second).astype(LOW)
    put_slots(sends, [gated_rows(far_meta, packed[0:rows, :], slots), own], cap)


class Loads:
    def __init__(self, in_sem, out_sem):
        self.in_sem, self.out_sem, self.loads, self.puts = in_sem, out_sem, [], []

    def load(self, source, target):
        self.loads.append(Fetch(source, target, self.in_sem.at[len(self.loads)]))
        return self.loads[-1]

    def put(self, source, target):
        self.puts.append(pltpu.make_async_copy(source, target, self.out_sem.at[len(self.puts)]))
        self.puts[-1].start()

    def finish(self):
        for copy in self.puts:
            copy.wait()


def slot_loads(moves, own, far, target, cap):
    for r in range(len(own)):
        for at, (piece, start) in enumerate((own[r], far[r])):
            moves.load(piece.at[pl.ds(start, cap)], target.at[pl.ds((2 * r + at) * cap, cap)])


def expert_kernel(*refs, parts, count, cap, step, starts, extra):
    first, middle, last = (refs[i * count : (i + 1) * count] for i in range(3))
    weights, refs = refs[3 * count : 3 * count + parts], refs[3 * count + parts + extra :]
    rows_out, grads_out, act_outs, hid_outs = refs[0], refs[1], refs[2 : 2 + parts], refs[2 + parts : 2 + 2 * parts]
    third_out, second_out, refs = refs[2 + 2 * parts], refs[3 + 2 * parts], refs[4 + 2 * parts :]
    back_own, back_far = refs[:count], refs[count : 2 * count]
    refs = refs[2 * count :]
    rows_ref, grads_ref, act_ref, hid_ref, back_ref, weight_ref, total_ref, product_ref, in_sem, out_sem = refs
    width = rows_ref.shape[1]
    moves = Loads(in_sem, out_sem)
    slot_loads(moves, [(p, cap) for p in middle], [(p, 0) for p in last], rows_ref, cap)
    rows_loads = list(moves.loads)
    ups, downs, order = {}, {}, (3, 1, 2, 0)

    def load_weights(r):
        ups[r] = moves.load(weights[r].at[pl.ds(starts[r], width)], weight_ref.at[2 * r])
        downs[r] = moves.load(weights[r].at[pl.ds(starts[r] + width, width)], weight_ref.at[2 * r + 1])

    load_weights(order[0])
    slot_loads(moves, [(p, 0) for p in first], [(p, 0) for p in middle], grads_ref, cap)
    grads_loads = moves.loads[len(rows_loads) + 2 :]
    for r in order[1:]:
        load_weights(r)
    for fetch in rows_loads:
        fetch.ref()
    moves.put(rows_ref, rows_out)
    blocks = 2 * cap * count // step
    for r in order:
        for b in range(blocks):
            here = pl.ds(b * step, step)
            hidden = nn(rows_ref[here, :], ups[r].ref()[...])
            if r == order[0] and b == 0:
                for fetch in grads_loads:
                    fetch.ref()
                moves.put(grads_ref, grads_out)
            grad = nt(grads_ref[here, :], downs[r].ref()[...])
            inner = hidden * (GELU_SCALE + GELU_SCALE * GELU_CUBIC * (hidden * hidden))
            half = 0.5 + 0.5 * jnp.tanh(inner)
            act_ref[r, here, :] = (hidden * half).astype(LOW)
            bend = 6.0 * inner - (4.0 * GELU_SCALE) * hidden
            hid = (grad * (half + half * (1.0 - half) * bend)).astype(LOW)
            hid_ref[r, here, :] = hid
            more = nt(hid, ups[r].ref()[...])
            if r != order[0]:
                more = more + total_ref[here, :]
            if r != order[-1]:
                total_ref[here, :] = more
                continue
            back_ref[here, :] = more.astype(LOW)
            for at in range(b * step, (b + 1) * step, 2 * cap):
                own = at // (2 * cap)
                moves.put(back_ref.at[pl.ds(at, cap), :], back_own[own])
                moves.put(back_ref.at[pl.ds(at + cap, cap), :], back_far[own])
        moves.put(act_ref.at[r], act_outs[r])
        moves.put(hid_ref.at[r], hid_outs[r])
        if r > 0:
            target, start, at = {3: (third_out, 0, 0), 1: (third_out, 2 * width, 2), 2: (second_out, 0, 4)}[r]
            product_ref[at] = tn(rows_ref[...], hid_ref[r]).astype(LOW)
            moves.put(product_ref.at[at], target.at[pl.ds(start, width)])
            product_ref[at + 1] = tn(act_ref[r], grads_ref[...]).astype(LOW)
            moves.put(product_ref.at[at + 1], target.at[pl.ds(start + width, width)])
    moves.finish()


def other_halves(came, start, held, semaphores):
    size = held.shape[1]
    return [Fetch(came.at[pl.ds(start + i * size, size)], held.at[i], semaphores.at[i]) for i in range(2)]


def sum_kernel(ins, outs, held, semaphores, *, start):
    *blocks, came = ins
    size = held.shape[0] // len(outs)
    others = [
        Fetch(came.at[pl.ds(start + i * size, size)], held.at[pl.ds(i * size, size)], semaphores.at[i])
        for i in range(len(outs))
    ]
    for put, block, other in zip(outs, blocks, others):
        put.set(block.get().astype(WIDE) + other.get().astype(WIDE))


def own_weight_kernel(flags_ref, ins, outs, other_ref, semaphores, *, start):
    rows, hid, grads, act, came, *momenta = ins
    others = other_halves(came, start, other_ref, semaphores)
    frozen = flags_ref[0] > 0
    for left, right, put, at in ((rows, hid, outs[0], 0), (act, grads, outs[1], 1)):
        total = tn(left.get(), right.get()) + others[at].get().astype(WIDE)
        old = momenta[at].get()
        put.set(jnp.where(frozen, old, MOMENT_KEEP * old + total))


def out_kernel(*refs, parts, count, cap, step, starts, extra):
    acts, weights, outs = refs[:parts], refs[parts : 2 * parts], refs[2 * parts + extra : 2 * parts + extra + count]
    act_ref, weight_ref, total_ref, in_sem, out_sem = refs[2 * parts + extra + count :]
    width = weight_ref.shape[2]
    moves = Loads(in_sem, out_sem)
    loads = []
    for r in range(parts):
        act = moves.load(acts[r], act_ref.at[r])
        loads.append((act, moves.load(weights[r].at[pl.ds(starts[r] + width, width)], weight_ref.at[r])))
    for b in range(2 * cap * count // step):
        here = slice(b * step, (b + 1) * step)
        total = None
        for act, down in loads:
            more = nn(act.ref()[here, :], down.ref()[...])
            total = more if total is None else total + more
        total_ref[here, :] = total.astype(LOW)
        for at in range(b * step, (b + 1) * step, 2 * cap):
            moves.put(total_ref.at[pl.ds(at, 2 * cap)], outs[at // (2 * cap)])
    moves.finish()


def gather_kernel(ins, outs, *, gated, cap, part):
    meta_in, *pieces = ins
    pieces = jnp.concatenate([p.ref()[part * cap : (part + 1) * cap, :] for p in pieces], axis=0)
    outs[0].set(collect(meta_in.get(), pieces, gated))


def mix_kernel(ins, outs, *, cap):
    meta_in, residual_in, came_in, *pieces = ins
    pieces = jnp.concatenate([p.ref()[:cap, :] for p in pieces], axis=0)
    total = collect(meta_in.get(), pieces, True) + came_in.get().astype(WIDE)
    outs[0].set(residual_in.get() + total)


def norm_backward(grad, unit, inverse, gain):
    scaled = grad * gain
    mean = jnp.mean(scaled, axis=-1, keepdims=True)
    along = jnp.mean(scaled * unit, axis=-1, keepdims=True)
    return inverse * (scaled - mean - unit * along)


def back_kernel(flags_ref, ins, outs, right_ref, weight_ref, small_ref, semaphores, *, head, parts):
    meta_in, came_in, *rest = ins
    pieces, (residual_in, cotangent_in, norm_in, all_weights, *smalls) = rest[:-8], rest[-8:]
    weights = [None] * 4
    weights[3] = Fetch(all_weights.at[3], weight_ref.at[3], semaphores.at[3])
    smalls = [Fetch(s, small_ref.at[i], semaphores.at[4 + i]) for i, s in enumerate(smalls)]
    query_in, key_in, value_in, tokens_in = smalls
    for i in range(3):
        weights[i] = Fetch(all_weights.at[i], weight_ref.at[i], semaphores.at[i])
    input_out, *rights = outs
    scale = head**-0.5
    pieces = jnp.concatenate([p.get() for p in pieces], axis=0)
    grad = collect(meta_in.get(), pieces, False) + came_in.get().astype(WIDE)
    unit, inverse = normalize(residual_in.get())
    norm_ref = norm_in.ref()
    rows, width = unit.shape
    second = [jnp.sum(grad * unit, axis=0, keepdims=True), jnp.sum(grad, axis=0, keepdims=True)]
    through = cotangent_in.get().astype(WIDE) + norm_backward(grad, unit, inverse, norm_ref[2:3, :])
    branch = through.astype(LOW)
    right_ref[3] = branch
    grad_heads = nt(branch, weights[3].get()).astype(LOW)
    group = 128 // head
    lane = iota((1, 128), 1) // head
    held = [r.ref() for r in (query_in, key_in, value_in)]
    for at in range(0, width, 128):
        query, key, value = (r[:, at : at + 128] for r in held)
        grad_out = grad_heads[:, at : at + 128]
        none = jnp.zeros_like(query)
        totals = [jnp.zeros(query.shape, WIDE) for _ in range(3)]
        for h in range(group):
            mine = lane == h
            probs = head_probs(jnp.where(mine, query, none), key, scale)
            dprob = nt(jnp.where(mine, grad_out, none), value)
            centre = jnp.sum(probs * dprob, axis=-1, keepdims=True)
            dscore = (probs * (dprob - centre)).astype(LOW)
            news = (
                nn(dscore, key) * scale,
                tn(dscore, query) * scale,
                tn(probs.astype(LOW), grad_out),
            )
            totals = [jnp.where(mine, p, t) for p, t in zip(news, totals)]
        for which in range(3):
            right_ref[which, :, at : at + 128] = totals[which].astype(LOW)
    grad = nt(right_ref[0], weights[0].get())
    grad = grad + nt(right_ref[1], weights[1].get())
    grad = grad + nt(right_ref[2], weights[2].get())
    unit, inverse = normalize(tokens_in.get().astype(WIDE))
    first = [jnp.sum(grad * unit, axis=0, keepdims=True), jnp.sum(grad, axis=0, keepdims=True)]
    sums = jnp.concatenate([*first, *second, jnp.zeros((SPARE - 4, width), WIDE)], axis=0).astype(LOW)
    size = rows + SPARE
    for r in range(parts):
        put, start = rights[min(r, 2)], max(r - 2, 0) * size
        put.ref[start : start + rows, :] = right_ref[flags_ref[3] ^ r]
        put.ref[start + rows : start + size, :] = sums
    for put in rights:
        put.send()
    input_out.set(through + norm_backward(grad, unit, inverse, norm_ref[0:1, :]))


def products_kernel(flags_ref, ins, outs, left_ref, right_ref, semaphores, *, starts, masks):
    parts = len(starts)
    first, second, last, far, *lefts = ins
    rows = left_ref.shape[1]
    third = Fetch(far.at[pl.ds(0, rows + SPARE)], right_ref, semaphores.at[parts])
    rights = [first, second, third, last]
    lefts = [
        Fetch(left.at[pl.ds(start, rows)], left_ref.at[r], semaphores.at[r])
        for r, (left, start) in enumerate(zip(lefts, starts))
    ]
    total = None
    for left, right in zip(lefts, rights):
        more = tn(left.get(), right.ref()[0:rows, :])
        total = more if total is None else total + more
    sums = [right.ref()[rows:, :].astype(WIDE) for right in rights]
    while len(sums) > 1:
        sums = [a + b for a, b in zip(sums[::2], sums[1::2])]
    total, half = total.astype(LOW), total.shape[0] // 2
    divide(flags_ref[2], [total[:half], total[half:]], sums[0].astype(LOW), outs, masks)


def divide(me, totals, sums, outs, masks):
    for i, (total, mask) in enumerate(zip(totals, masks)):
        size = total.shape[0] // 2
        upper = (me & mask) > 0
        send = jnp.where(upper, total[:size], total[size:])
        keep = jnp.where(upper, total[size:], total[:size])
        for put, part in ((outs[2 * i], send), (outs[2 * i + 1], keep)):
            put.ref[0:size, :] = part
            if i == 0:
                put.ref[size:, :] = sums
            put.send()


def added(keep, came):
    return (keep.get().astype(WIDE) + came.get().astype(WIDE)).astype(LOW)


def divide_kernel(flags_ref, ins, outs, *, masks):
    totals = [added(*ins[0:2]), added(*ins[2:4])]
    size = totals[1].shape[0]
    divide(flags_ref[2], [totals[0][:size], totals[1]], totals[0][size:], outs, masks)


def whole_kernel(ins, outs):
    outs[0].set(jnp.concatenate([added(*ins[0:2]), added(*ins[2:4])], axis=0))


def add_kernel(ins, outs):
    outs[0].set(added(*ins))


def part_kernel(ins, outs):
    total = added(*ins[:2])
    first, second, params = (i.get() for i in ins[2:])
    size = outs[0].ref.shape[0]
    outs[0].set(total[:size])
    outs[1].set(total[size + SPARE :])
    sums = total[size : size + 4].astype(WIDE)
    first = FIRST_DECAY * first + (1.0 - FIRST_DECAY) * sums
    second = SECOND_DECAY * second + (1.0 - SECOND_DECAY) * sums * sums
    outs[3].set(first)
    outs[4].set(second)
    first = first / (1.0 - FIRST_DECAY**STEP_COUNT)
    second = second / (1.0 - SECOND_DECAY**STEP_COUNT)
    outs[2].set(params - ADAM_RATE * (first / (jnp.sqrt(second) + ADAM_EPSILON) + ADAM_DECAY * params))


def joined(me, mine, came, mask):
    upper = (me & mask) > 0
    mine, came = mine.get(), came.get()
    return jnp.concatenate([jnp.where(upper, came, mine), jnp.where(upper, mine, came)], axis=0)


def join_kernel(flags_ref, ins, outs, *, masks):
    for i, mask in enumerate(masks):
        outs[i].set(joined(flags_ref[2], *ins[2 * i : 2 * i + 2], mask))


def packed_width(width):
    return sum(width - at for at in range(0, width, BLOCK))


def moments_kernel(flags_ref, ins, outs):
    up_own, down_own, up_other, down_other = ins
    up_out, down_out, up_low_out, down_low_out, *sends = outs
    frozen = flags_ref[0] > 0
    even = flags_ref[1] == 0
    lows = []
    for own, other, out, low_out in ((up_own, up_other, up_out, up_low_out), (down_own, down_other, down_out, down_low_out)):
        own = own.get()
        moment = jnp.where(frozen, own, own + other.get().astype(WIDE))
        out.set(moment)
        lows.append(moment.astype(LOW))
        low_out.set(lows[-1])
    size = lows[0].shape[0] // len(sends)
    for i, put in enumerate(sends):
        here = slice(i * size, (i + 1) * size)
        put.set(jnp.where(even, lows[1][here, :], lows[0][here, :]))


def gram_kernel(flags_ref, ins, outs, mine_ref, came_ref, semaphores):
    up_low, down_low, *pieces = ins
    size = pieces[0].held.shape[0]
    width = mine_ref.shape[0]
    for i, piece in enumerate(pieces):
        came_ref[i * size : (i + 1) * size, :] = piece.get()

    def whole(source, product):
        copy = pltpu.make_async_copy(source, mine_ref, semaphores.at[0])
        copy.start()
        copy.wait()
        column = 0
        for at in range(0, width, BLOCK):
            here = slice(column, column + width - at)
            outs[0].ref[:, here] = product(mine_ref, at) + product(came_ref, at)
            column += width - at

    @pl.when(flags_ref[1] == 0)
    def _():
        whole(up_low, lambda ref, at: nt(ref[at : at + BLOCK, :], ref[at:, :]))

    @pl.when(flags_ref[1] != 0)
    def _():
        whole(down_low, lambda ref, at: tn(ref[:, at : at + BLOCK], ref[:, at:]))


class Square:
    SHAPES = (WIDE, LOW, LOW, LOW)

    def __init__(self, refs, lines):
        self.shifted, self.shifted_low, self.shifted_rest, self.factor_rest = refs
        self.shifted_line, self.factor_line = lines
        width = self.shifted.shape[0]
        self.strips = [slice(at, at + BLOCK) for at in range(0, width, BLOCK)]

    def diagonal(self, here, strip):
        same = iota(strip.shape, 0) + here.start == iota(strip.shape, 1)
        return same, jnp.sum(jnp.where(same, strip, 0.0), axis=1, keepdims=True)

    def take(self, here, gram):
        same, line = self.diagonal(here, gram)
        line = line - CENTRE
        strip = jnp.where(same, line, gram)
        self.shifted[here, :] = strip
        self.shifted_low[here, :] = strip.astype(LOW)
        self.shifted_rest[here, :] = jnp.where(same, 0.0, strip).astype(LOW)
        self.shifted_line[here, :] = jnp.broadcast_to(line, (BLOCK, 128))

    def square(self):
        for here in self.strips:
            product = nn(self.shifted_rest[here, :], self.shifted_low[...])
            strip = SCHULZ_QUARTIC * (self.shifted_line[here, 0:1] * self.shifted[here, :] + product)
            same, line = self.diagonal(here, strip)
            self.factor_rest[here, :] = jnp.where(same, 0.0, strip).astype(LOW)
            self.factor_line[here, :] = jnp.broadcast_to(line + REST, (BLOCK, 128))

    def times(self, here, strip, low):
        return self.factor_line[here, 0:1] * strip + nn(self.factor_rest[here, :], low)


def square_scratch(width):
    return [pltpu.VMEM((width, width), t) for t in Square.SHAPES] + [pltpu.VMEM((width, 128), WIDE)] * 2


def attn_step_kernel(flags_ref, ins, outs, now_ref, low_a, low_b, *refs, masks):
    momentum, master = ins[4:]
    moment_out, new_out, low_out = outs
    square = Square(refs[:4], refs[4:])
    width = now_ref.shape[1]
    half = width // 2
    old = momentum.ref()
    for i, mask in enumerate(masks):
        here = slice(i * half, (i + 1) * half)
        grad = joined(flags_ref[2], *ins[2 * i : 2 * i + 2], mask)
        moment_out.ref[here, :] = MOMENT_KEEP * old[here, :] + grad.astype(WIDE)
    moment_out.send()
    moment = moment_out.ref[...]
    now = moment * (1.0 / (jnp.sqrt(jnp.sum(moment * moment)) + 1e-07))
    now_ref[...] = now
    low_a[...] = now.astype(LOW)
    low, later = low_a, low_b
    for k in range(ITERS):
        for here in square.strips:
            square.take(here, nt(low[here, :], low[...]))
        square.square()
        for here in square.strips:
            strip = square.times(here, now_ref[here, :], low[...])
            if k < ITERS - 1:
                now_ref[here, :] = strip
                later[here, :] = strip.astype(LOW)
                continue
            new = master.ref()[here, :] * (1.0 - MUON_RATE * MUON_DECAY) - MUON_RATE * 0.2 * width**0.5 * strip
            new_out.ref[here, :] = new
            low_out.ref[here, :] = new.astype(LOW)
        low, later = later, low


def polar_kernel(ins, outs, gram_ref, gram_low, half_ref, half_low, product_ref, low_a, low_b, *refs):
    square = Square(refs[:4], refs[4:])
    mine_ref, other_ref = (i.ref() for i in ins)
    width = gram_ref.shape[0]
    column = 0
    for at in range(0, width, BLOCK):
        here = slice(column, column + width - at)
        strip = mine_ref[:, here] + other_ref[:, here]
        gram_ref[at : at + BLOCK, at:] = strip
        for far in range(BLOCK, width - at, BLOCK):
            gram_ref[at + far : at + far + BLOCK, at : at + BLOCK] = strip[:, far : far + BLOCK].T
        column += width - at
    total = 0.0
    for here in square.strips:
        total = total + jnp.sum(square.diagonal(here, gram_ref[here, :])[1])
    length = jnp.sqrt(total) + 1e-07

    def take(here, strip):
        gram_ref[here, :] = strip
        gram_low[here, :] = strip.astype(LOW)
        square.take(here, strip)

    for here in square.strips:
        take(here, gram_ref[here, :] * (1.0 / (length * length)))
    low, later = low_a, low_b
    for k in range(ITERS):
        square.square()
        for here in square.strips:
            if k == 0:
                same = iota((BLOCK, width), 0) + here.start == iota((BLOCK, width), 1)
                strip = jnp.where(same, square.factor_line[here, 0:1], square.factor_rest[here, :].astype(WIDE))
            else:
                strip = square.times(here, product_ref[here, :], low[...])
            if k < ITERS - 1:
                product_ref[here, :] = strip
                later[here, :] = strip.astype(LOW)
                half = square.times(here, gram_ref[here, :], gram_low[...])
                half_ref[here, :] = half
                half_low[here, :] = half.astype(LOW)
            else:
                product_ref[here, :] = strip * (1.0 / length)
        if k < ITERS - 1:
            for here in square.strips:
                take(here, square.times(here, half_ref[here, :], half_low[...]))
        low, later = later, low
    size = width // len(outs)
    for i, put in enumerate(outs):
        put.set(product_ref[i * size : (i + 1) * size, :])


def apply_kernel(flags_ref, ins, outs, *, wide_scale, strips):
    quarters, ins = ins[:8], ins[8:]
    up_moment, down_moment = ins[:2]
    up_masters, down_masters = ins[2 : 2 + strips], ins[2 + strips :]
    up_new, up_low, down_new, down_low = (outs[i * strips : (i + 1) * strips] for i in range(4))
    frozen = flags_ref[0] > 0
    even = flags_ref[1] == 0
    factors = [jnp.concatenate([q.get() for q in part], axis=0) for part in (quarters[:4], quarters[4:])]
    up_factor = jnp.where(even, factors[0], factors[1])
    down_factor = jnp.where(even, factors[1], factors[0])

    def update(master, new_put, low_put, ortho):
        old = master.get()
        new = old * (1.0 - MUON_RATE * MUON_DECAY) - MUON_RATE * wide_scale * ortho
        new = jnp.where(frozen, old, new)
        new_put.set(new)
        low_put.set(new)

    up_matrix, down_matrix = up_moment.get(), down_moment.get()
    size = up_factor.shape[0] // strips
    for i in range(strips):
        here = slice(i * size, (i + 1) * size)
        update(up_masters[i], up_new[i], up_low[i], nn(up_factor[here, :], up_matrix))
        update(down_masters[i], down_new[i], down_low[i], nn(down_matrix[here, :], down_factor))


def masks_of(axis):
    count = lax.axis_size(axis)
    return [1 << i for i in range(count.bit_length() - 1)]


def body(
    tokens,
    cotangent,
    expert_ids,
    gate_units,
    capacity,
    frozen,
    attn_copy,
    attn_master,
    attn_momentum,
    norm_params,
    norm_first,
    norm_second,
    up_copy,
    up_master,
    up_momentum,
    down_copy,
    down_master,
    down_momentum,
):
    rows, width = tokens.shape
    cuts = lax.axis_size("cuts")
    experts = capacity.shape[0]
    members = lax.axis_size("expert")
    cap = 4 * rows // members
    slots = experts * cap
    head = width // HEADS
    hidden = up_copy.shape[2]
    cut = lax.axis_index("cuts")
    me = lax.axis_index("expert")
    count = members // 2
    flags = jnp.stack([frozen[0], cut & 1, me, cut])
    small = shape_of((rows, width), LOW)
    square = shape_of((width, width), WIDE)
    square_low = shape_of((width, width), LOW)

    def cross(value):
        return swap(value, "expert", count)

    def spread(values):
        return [values[0]] + [swap(values[r], "expert", r) for r in range(1, count)]

    pair_shape = shape_of((2 * width, hidden), LOW)
    meta_shape = shape_of((8, rows), WIDE)
    piece = shape_of((cap, width), LOW)
    pair = shape_of((2 * cap, width), LOW)
    meta, packed, weights, *sends = staged_call(
        functools.partial(pack_kernel, cap=cap),
        [expert_ids.T, gate_units.T, cotangent, up_copy[0], down_copy[0]],
        [meta_shape, shape_of((rows + SPARE, width), LOW), (pair_shape, 2)] + [piece] * count,
        smem=[flags, capacity],
    )
    far_packed = cross(packed)
    weights = {0: weights, 2: swap(weights, "cuts", 2)}
    first = spread(sends)
    query, key, value, both_lefts, left, core_left, far_lefts = staged_call(
        functools.partial(front_kernel, head=head),
        [tokens, norm_params, (attn_copy, 0)],
        [small] * 3 + [shape_of((2 * rows, width), LOW), small, small, shape_of((2 * rows, width), LOW)],
        scratch=[pltpu.VMEM((3, width, width), LOW), pltpu.SemaphoreType.DMA((3,))],
        smem=[flags],
        after=[packed],
    )
    normed_two, residual, far_meta, *sends = staged_call(
        functools.partial(residual_kernel, cap=cap),
        [both_lefts, tokens, norm_params, meta, far_packed, (attn_copy, 0)],
        [small, shape_of((rows, width), WIDE), meta_shape] + [pair] * count,
        scratch=[pltpu.VMEM((width, width), LOW), pltpu.SemaphoreType.DMA((1,))],
        after=first[1:],
        smem=[flags, capacity],
    )
    far_normed = cross(normed_two)
    middle = spread(sends)
    sends = staged_call(functools.partial(far_kernel, cap=cap), [far_meta, far_normed], [piece] * count)
    last = spread(sends)
    (both,) = staged_call(
        stack_kernel,
        [weights[0], weights[2], core_left],
        [(shape_of((4 * width + rows, hidden), LOW), (4 * width + rows) // BLOCK)],
        after=[sends[0], *middle[1:]],
    )
    both = swap(both, "cuts", 1)
    places = ((weights[0], 0), (both, 0), (weights[2], 0), (both, 2 * width))

    step = 256
    wide = shape_of((slots, hidden), LOW)
    slot_shape = shape_of((slots, width), LOW)
    anywhere = pl.BlockSpec(memory_space=pltpu.HBM)
    scalars = pl.BlockSpec(memory_space=pltpu.SMEM)
    all_slots = pltpu.VMEM((slots, width), LOW)
    all_wide = pltpu.VMEM((cuts, slots, hidden), LOW)
    all_weights = pltpu.VMEM((cuts, width, hidden), LOW)

    def placed_call(kernel, outs, args, held, loads, puts, cost=0):
        return pl.pallas_call(
            kernel,
            out_shape=outs,
            in_specs=[anywhere] * len(args),
            out_specs=[anywhere] * len(outs),
            scratch_shapes=[*held, pltpu.SemaphoreType.DMA((loads,)), pltpu.SemaphoreType.DMA((puts,))],
            compiler_params=pltpu.CompilerParams(vmem_limit_bytes=VMEM_BYTES),
            cost_estimate=cost_of(cost),
        )(*args)

    sizes = dict(parts=cuts, count=count, cap=cap, step=step, starts=[at for _, at in places])
    slot_rows, slot_grads, *outs = placed_call(
        functools.partial(expert_kernel, extra=0, **sizes),
        [slot_shape] * 2 + [wide] * (2 * cuts)
        + [shape_of((4 * width, hidden), LOW), pair_shape]
        + [piece] * (2 * count),
        [*first, *middle, *last, *[w for w, _ in places]],
        [
            *[all_slots, all_slots, all_wide, all_wide, all_slots],
            pltpu.VMEM((2 * cuts, width, hidden), LOW),
            pltpu.VMEM((slots, width), WIDE),
            pltpu.VMEM((6, width, hidden), LOW),
        ],
        2 * cuts + 4 * count,
        8 + 2 * cuts + 2 * count,
    )
    acts, hids = outs[:cuts], outs[cuts : 2 * cuts]
    odd, second = outs[2 * cuts : 2 * cuts + 2]
    back_own, back_far = outs[2 * cuts + 2 : 2 * cuts + 2 + count], outs[2 * cuts + 2 + count :]
    back_far = spread(back_far)

    far_lefts = swap(far_lefts, "cuts", 2)

    def rows_from(array, start, after, cost=0):
        shape = (array.shape[0] - start, array.shape[1])
        (part,) = staged_call(
            functools.partial(copy_kernel, start=start),
            [(array, 0)],
            [shape_of(shape, array.dtype)],
            cost=cost,
            scratch=[pltpu.VMEM(shape, array.dtype), pltpu.SemaphoreType.DMA((1,))],
            after=after,
        )
        return part

    ready = rows_from(far_lefts, rows, [slot_rows], cost=60)
    def gather(meta_of, pieces, gated, part, after=()):
        (total,) = staged_call(
            functools.partial(gather_kernel, gated=gated, cap=cap, part=part),
            [meta_of, *pieces],
            [small],
            after=after,
        )
        return total

    odd_came = swap(odd, "cuts", 1)
    (second,) = staged_call(
        functools.partial(sum_kernel, start=0),
        [(second, 6), (odd_came, 0)],
        [(pair_shape, 6)],
        scratch=[pltpu.VMEM((2 * width, hidden), LOW), pltpu.SemaphoreType.DMA((6,))],
        after=[ready],
    )
    second_came = swap(second, "cuts", 2)
    gathered = gather(far_meta, back_far, False, 0, after=[second])
    pieces = placed_call(
        functools.partial(out_kernel, extra=1, **sizes),
        [pair] * count,
        [*acts, *[w for w, _ in places], second],
        [all_wide, all_weights, all_slots],
        2 * cuts,
        count,
        cost=60,
    )
    came = cross(gathered)
    back_own = spread(back_own)
    other_scratch = [pltpu.VMEM((2, width, hidden), LOW), pltpu.SemaphoreType.DMA((2,))]
    input_grad, right, core_right, far_rights = staged_call(
        functools.partial(back_kernel, head=head, parts=cuts),
        [meta, came, *back_own, residual, cotangent, norm_params]
        + [(a, 0) for a in (attn_copy, query, key, value, tokens)],
        [shape_of((rows, width), WIDE)]
        + [shape_of((n * (rows + SPARE), width), LOW) for n in (1, 1, 2)],
        scratch=[
            pltpu.VMEM((4, rows, width), LOW),
            pltpu.VMEM((4, width, width), LOW),
            pltpu.VMEM((4, rows, width), LOW),
            pltpu.SemaphoreType.DMA((8,)),
        ],
        smem=[flags],
        after=[pieces[0]],
    )
    core_right = swap(core_right, "cuts", 1)
    far_rights = swap(far_rights, "cuts", 2)
    core_far_left = swap(ready, "cuts", 1)
    own_shape = shape_of((2 * width, hidden), WIDE)
    (zeroth,) = staged_call(
        functools.partial(own_weight_kernel, start=2 * width),
        [slot_rows, hids[0], slot_grads, acts[0], (odd_came, 0), up_momentum[0], down_momentum[0]],
        [(own_shape, 2)],
        scratch=[pltpu.VMEM((2, width, hidden), LOW), pltpu.SemaphoreType.DMA((2,))],
        smem=[flags],
        after=[core_right],
    )

    strips = shape_of((BLOCK, packed_width(width)), WIDE)
    up_moment, down_moment, up_moment_low, down_moment_low, *sends = staged_call(
        moments_kernel,
        [(zeroth, 2), (second_came, 2)],
        [square, square, square_low, square_low] + [shape_of((width // 2, width), LOW)] * 2,
        smem=[flags],
    )
    (keep,) = staged_call(
        gram_kernel,
        [(up_moment_low, 0), (down_moment_low, 0), *[swap(v, "cuts", 1) for v in sends]],
        [strips],
        scratch=[pltpu.VMEM((width, width), LOW)] * 2 + [pltpu.SemaphoreType.DMA((1,))],
        smem=[flags],
    )
    other = swap(keep, "cuts", 2)
    last_right = swap(rows_from(far_rights, rows + SPARE, [keep]), "cuts", 1)
    masks = masks_of("expert")
    order = (masks[0:2], [masks[1], masks[0]])

    def part_shape(share, extra):
        return shape_of((width // share + extra * SPARE, width), LOW)

    def trade(sends, step):
        return [swap(v, "expert", order[i][step]) for i, v in enumerate(sends)]

    send_a, keep_a, send_b, keep_b = staged_call(
        functools.partial(
            products_kernel, starts=(0, 4 * width, 0, 0), masks=(order[0][0], order[1][0])
        ),
        [right, core_right, last_right, (far_rights, 0), (left, 0), (both, 0), (far_lefts, 0), (core_far_left, 0)],
        [part_shape(4, 1)] * 2 + [part_shape(4, 0)] * 2,
        scratch=[
            pltpu.VMEM((cuts, rows, width), LOW),
            pltpu.VMEM((rows + SPARE, width), LOW),
            pltpu.SemaphoreType.DMA((cuts + 1,)),
        ],
        smem=[flags],
        cost=60,
        after=[keep],
    )
    came_a, came_b = trade([send_a, send_b], 0)
    send_a, keep_a, send_b, keep_b = staged_call(
        functools.partial(divide_kernel, masks=(order[0][1], order[1][1])),
        [keep_a, came_a, keep_b, came_b],
        [part_shape(8, 1)] * 2 + [part_shape(8, 0)] * 2,
        smem=[flags],
    )
    came_a, came_b = trade([send_a, send_b], 1)
    (total,) = staged_call(whole_kernel, [keep_a, came_a, keep_b, came_b], [part_shape(4, 1)])
    for mask in masks[2:-1]:
        (total,) = staged_call(add_kernel, [total, swap(total, "expert", mask)], [part_shape(4, 1)])
    came = swap(total, "expert", masks[-1])
    factor = staged_call(
        polar_kernel,
        [keep, other],
        [shape_of((width // 4, width), LOW)] * 4,
        scratch=[
            *[pltpu.VMEM((width, width), t) for t in (WIDE, LOW, WIDE, LOW, WIDE, LOW, LOW)],
            *square_scratch(width),
        ],
        after=[total],
    )
    pieces = spread(pieces)
    gathered_out = gather(far_meta, pieces, True, 1, after=[factor[0]])
    came_out = cross(gathered_out)
    norm_shape = shape_of(norm_params.shape, WIDE)
    part_a, part_b, norm_new, first_new, second_new = staged_call(
        part_kernel,
        [total, came, norm_first, norm_second, norm_params],
        [part_shape(8, 0)] * 2 + [norm_shape] * 3,
        after=[factor[0]],
    )
    came_a, came_b = trade([part_a, part_b], 1)
    half_a, half_b = staged_call(
        functools.partial(join_kernel, masks=(order[0][1], order[1][1])),
        [part_a, came_a, part_b, came_b],
        [part_shape(4, 0)] * 2,
        smem=[flags],
    )
    came_a, came_b = trade([half_a, half_b], 0)
    (output,) = staged_call(
        functools.partial(mix_kernel, cap=cap),
        [meta, residual, came_out, *pieces],
        [small],
        after=[half_a],
    )
    attn_moment, attn_new, attn_low = staged_call(
        functools.partial(attn_step_kernel, masks=(order[0][0], order[1][0])),
        [half_a, came_a, half_b, came_b, attn_momentum[0], attn_master[0]],
        [square, square, square_low],
        scratch=[*[pltpu.VMEM((width, width), t) for t in (WIDE, LOW, LOW)], *square_scratch(width)],
        smem=[flags],
        after=[output],
    )
    thirds = width // BLOCK
    up_new, up_low, down_new, down_low = staged_call(
        functools.partial(apply_kernel, wide_scale=0.2 * max(width, FF) ** 0.5, strips=thirds),
        [*factor, *[swap(f, "cuts", 1) for f in factor], up_moment_low, down_moment_low, (up_master[0], thirds), (down_master[0], thirds)],
        [(square, thirds), (square_low, thirds)] * 2,
        smem=[flags],
    )
    return (
        output,
        input_grad,
        attn_new[None],
        attn_moment[None],
        attn_low[None],
        up_new[None],
        up_moment[None],
        up_low[None],
        down_new[None],
        down_moment[None],
        down_low[None],
        norm_new,
        first_new,
        second_new,
    )


def solution(mesh):
    rows = P(("expert", "cuts"), None)
    attn = P("cuts", None, None)
    ups = P("expert", None, "cuts")
    downs = P("expert", "cuts", None)
    return jax.shard_map(
        body,
        mesh=mesh,
        in_specs=(rows, rows, rows, rows, P(), P("expert"), P(), attn, attn, P(), P(), P())
        + (ups, ups, ups, downs, downs, downs),
        out_specs=(rows, rows, attn, attn, attn, ups, ups, ups, downs, downs, downs, P(), P(), P()),
        check_vma=False,
    )
```
